512 devices in a mesh: dp: 8 (over x_hi, y), seq: 64 (over z, x_lo, core).
Axes of the slice: x: 4 (x_hi: 2, x_lo: 2; x = x_hi * 2 + x_lo), y: 4, z: 16, core: 2. Of those that a mesh axis runs over, the one named last changes fastest.
Arguments:
- video: bfloat16 [8, 64, 256, 768], P('dp', 'seq'), may hold values from -6 to 6
- upstream: bfloat16 [8, 64, 256, 768], P('dp', 'seq'), may hold values from -6 to 6
- standardize_scale: float32 [768], replicated, may hold values from 0.25 to 1.75
- ln_bias: float32 [768], replicated, may hold values from -3 to 3
- w_qkv: bfloat16 [768, 2304], P('seq'), may hold values from -0.21875 to 0.21875
- w_out: bfloat16 [768, 768], P('seq'), may hold values from -0.21875 to 0.21875
- windows: float32 [64, 768], replicated, may hold values from -6 to 6
- positives: int32 [64], replicated, may hold values from 0 to 63, each once
Outputs:
- grad_video: bfloat16 [8, 64, 256, 768], P('dp', 'seq')
- grad_out_weight: float32 [512, 1152], P(('dp', 'seq'))
- pooled: float32 [64, 768], replicated
- contrast_loss: float32 [], replicated
The draws below stay inside these ranges and needn't reach their ends.
Inputs may be any that keep to these rules, and one draw needn't show every extreme that they name: `positives`: each window index is the positive of exactly one clip.
All inputs are finite; a program needn't handle non-finite values.
Results may differ from the reference program's by a relative error of at most 0.0075.
Values may be sent and summed in bfloat16 or wider, within the bound.
A program may use at most 64 MiB of HBM per device.

```python
import jax
import jax.numpy as jnp
from jax import lax

D = 768
HEADS = 12
HEAD_DIM = 64
PATCHES = 256
CLIP = 8
FRAMES = 64
SLABS = 8
CLIPS = 64
N_DP = 8
N_SEQ = 64


def draw_video(key, part):
    key = jax.random.fold_in(key, 11)
    token_key = jax.random.fold_in(key, 0)
    clip_key = jax.random.fold_in(key, 1)
    frame_key = jax.random.fold_in(key, 3)
    full_shape = (SLABS, FRAMES, PATCHES, D)
    clip_shape = (SLABS, FRAMES // CLIP, 1, 1, D)
    frame_shape = (SLABS, FRAMES, 1, D)
    token_part = jax.random.normal(token_key, full_shape, jnp.float32)
    clip_part = jax.random.normal(clip_key, clip_shape, jnp.float32)
    frame_part = jax.random.normal(frame_key, frame_shape, jnp.float32)
    clip_part = jnp.repeat(clip_part, CLIP, axis=1).reshape(SLABS, FRAMES, 1, D)
    return jnp.clip(token_part + clip_part + frame_part, -6.0, 6.0).astype(jnp.bfloat16)


def levels(rng, shape, cuts, low, top_value):
    loudness = 1.0
    for axis_at, parts in cuts:
        heights = jax.random.uniform(jax.random.fold_in(jax.random.fold_in(rng, 6), axis_at), (parts,), jnp.float32, low / len(cuts), top_value / len(cuts))
        loudness = loudness * jnp.repeat(jnp.exp(heights), shape[axis_at] // parts).reshape((-1,) + (1,) * (len(shape) - 1 - axis_at))
    return loudness


def gaussian(rng, shape, scale, bound, cuts=(), kind=jnp.bfloat16):
    array = jax.random.normal(rng, shape, jnp.float32) * scale
    if len(cuts) > 0:
        array = levels(rng, shape, cuts, -0.22, 0.18) * array
    return jnp.clip(array, min=-bound, max=bound).astype(kind)


def setup_inputs(seed: int = 0) -> dict:
    key_of = jax.random.split(jax.random.key(seed), 9)
    return {
        "video": draw_video(jax.random.fold_in(key_of[8], 71), 0),
        "upstream": gaussian(key_of[1], (SLABS, FRAMES, PATCHES, D), 1.0, 6.0, ((0, 8), (1, 64))),
        "standardize_scale": jnp.clip(1.0 + 0.15 * jax.random.normal(key_of[2], (D,), jnp.float32), 0.25, 1.75),
        "ln_bias": gaussian(key_of[3], (D,), 0.5, 3.0, (), jnp.float32),
        "w_qkv": gaussian(key_of[4], (D, 3 * D), D ** -0.5, 0.21875, ((0, 64),)),
        "w_out": gaussian(key_of[5], (D, D), D ** -0.5, 0.21875, ((0, 64),)),
        "windows": gaussian(key_of[6], (CLIPS, D), 1.0, 6.0, (), jnp.float32),
        "positives": jax.random.permutation(key_of[7], CLIPS).astype(jnp.int32),
    }


sharpness_factor = 1.0 / 0.07

def contrast(pooled_features, windows, positives):
    segment_direction_normalized = pooled_features * lax.rsqrt(lax.optimization_barrier(jnp.mean(pooled_features * pooled_features, -1, keepdims=True)) + 1e-06) * pooled_features.shape[-1] ** (-0.5)
    span_direction_normalized = windows * lax.rsqrt(lax.optimization_barrier(jnp.mean(windows * windows, -1, keepdims=True)) + 1e-06) * windows.shape[-1] ** (-0.5)
    cosine_score_matrix = jnp.dot(segment_direction_normalized, span_direction_normalized.T, precision=lax.Precision.HIGHEST) * sharpness_factor
    row_lse = jax.nn.logsumexp(cosine_score_matrix, axis=1)
    column_lse = jax.nn.logsumexp(cosine_score_matrix, axis=0)
    matched = positives[:, None] == lax.iota(jnp.int32, cosine_score_matrix.shape[1])[None, :]
    positive = lax.optimization_barrier(jnp.sum(jnp.where(matched, cosine_score_matrix, jnp.zeros_like(cosine_score_matrix)), 1))
    return 0.5 * (jnp.mean(row_lse) + jnp.mean(column_lse)) - jnp.mean(positive)

def forward_slab(tokens, standardize_scale, ln_bias, w_qkv, w_out):
    tokens_f = tokens.astype(jnp.float32)
    centered = tokens_f - lax.optimization_barrier(jnp.mean(tokens_f, -1, keepdims=True))
    inverse_deviation = lax.rsqrt(lax.optimization_barrier(jnp.mean(centered * centered, -1, keepdims=True)) + 1e-06)
    unit = centered * inverse_deviation
    normed = (unit * standardize_scale + ln_bias).astype(jnp.bfloat16)
    qkv = jnp.dot(normed.reshape(-1, D), w_qkv, preferred_element_type=jnp.float32).astype(jnp.bfloat16)
    qkv_parts = qkv.reshape(FRAMES, PATCHES, 3, HEADS, HEAD_DIM).astype(jnp.float32)
    query_part, key_part, value_part = (qkv_parts[:, :, 0], qkv_parts[:, :, 1], qkv_parts[:, :, 2])
    scores = jnp.einsum('tphd,uphd->phtu', query_part, key_part) * HEAD_DIM ** (-0.5)
    attention_probabilities = jax.nn.softmax(scores, -1)
    probability_half = attention_probabilities.astype(jnp.bfloat16)
    attended_context = jnp.einsum('phtu,uphd->tphd', probability_half.astype(jnp.float32), value_part).astype(jnp.bfloat16)
    context_rows = attended_context.reshape(-1, D)
    output = tokens_f + jnp.dot(context_rows, w_out, preferred_element_type=jnp.float32).reshape(FRAMES, PATCHES, D)
    return (unit, inverse_deviation, query_part, key_part, value_part, attention_probabilities, probability_half, context_rows, output)

def reference(video, upstream, standardize_scale, ln_bias, w_qkv, w_out, windows, positives):
    clip_slab = FRAMES // CLIP

    def pool_one(tokens):
        output = forward_slab(tokens, standardize_scale, ln_bias, w_qkv, w_out)[-1]
        return lax.optimization_barrier(jnp.sum(output.reshape(clip_slab, CLIP, PATCHES, D), (1, 2))) / (CLIP * PATCHES)
    pooled_features = lax.map(pool_one, video).reshape(CLIPS, D)
    contrast_loss, derivative_averaged_embedding = jax.value_and_grad(contrast)(pooled_features, windows, positives)
    grad_slabs = derivative_averaged_embedding.reshape(SLABS, clip_slab, D)

    def back_one(weight_sum, items):
        tokens, upper, grad_clip = items
        unit, inverse_deviation, query_part, key_part, value_part, attention_probabilities, probability_half, context_rows, output = forward_slab(tokens, standardize_scale, ln_bias, w_qkv, w_out)
        spread = jnp.repeat(grad_clip, CLIP, axis=0)[:, None, :]
        grad_output = upper.astype(jnp.float32) + CLIPS * spread
        grad_rows = grad_output.astype(jnp.bfloat16).reshape(-1, D)
        weight_term = jnp.dot(context_rows.T, grad_rows, preferred_element_type=jnp.float32)
        derivative_mixed_frames = jnp.dot(grad_rows, w_out.T, preferred_element_type=jnp.float32).astype(jnp.bfloat16)
        derivative_mixed_frames = derivative_mixed_frames.reshape(FRAMES, PATCHES, HEADS, HEAD_DIM).astype(jnp.float32)
        grad_prob = jnp.einsum('tphd,uphd->phtu', derivative_mixed_frames, value_part)
        grad_value = jnp.einsum('phtu,tphd->uphd', probability_half.astype(jnp.float32), derivative_mixed_frames).astype(jnp.bfloat16)
        row_dot = lax.optimization_barrier(jnp.sum(attention_probabilities * grad_prob, -1, keepdims=True))
        grad_score = (attention_probabilities * (grad_prob - row_dot) * HEAD_DIM ** (-0.5)).astype(jnp.bfloat16).astype(jnp.float32)
        grad_query = jnp.einsum('phtu,uphd->tphd', grad_score, key_part).astype(jnp.bfloat16)
        grad_key = jnp.einsum('phtu,tphd->uphd', grad_score, query_part).astype(jnp.bfloat16)
        grad_qkv = jnp.stack([grad_query, grad_key, grad_value], 2).reshape(-1, 3 * D)
        grad_normed = jnp.dot(grad_qkv, w_qkv.T, preferred_element_type=jnp.float32).astype(jnp.bfloat16)
        scaled = grad_normed.reshape(FRAMES, PATCHES, D).astype(jnp.float32) * standardize_scale
        grad_norm = inverse_deviation * (scaled - lax.optimization_barrier(jnp.mean(scaled, -1, keepdims=True)) - unit * lax.optimization_barrier(jnp.mean(scaled * unit, -1, keepdims=True)))
        return (weight_sum + weight_term, (grad_output + grad_norm).astype(jnp.bfloat16))
    weight_sum, grad_video = lax.scan(back_one, jnp.zeros((D, D), jnp.float32), (video, upstream, grad_slabs))
    return (grad_video, weight_sum.reshape(N_DP * N_SEQ, -1), pooled_features, contrast_loss)
```

```python
import jax
import jax.numpy as jnp
from jax import lax
from jax.experimental import pallas as pl
from jax.experimental.pallas import tpu as pltpu
from jax.sharding import PartitionSpec as P

MESH = pl.DeviceIdType.MESH
F32 = jnp.float32
BF16 = jnp.bfloat16
D = 768
EPS = 1e-6
NEG = -1e30
SHARP = 1.0 / 0.07
VMEM_LIMIT = 56 * 1024 * 1024


class Place:
    def __init__(self):
        self.dp = lax.axis_index("dp")
        self.seq = lax.axis_index("seq")
        self.x_hi = self.dp // 4
        self.y = self.dp % 4
        self.z = self.seq // 4
        self.role = self.seq % 4
        self.x_lo = self.role // 2
        self.core = self.seq % 2
        self.k = self.seq // 2
        self.x = self.x_hi * 2 + self.x_lo
        self.m = self.dp * 4 + self.role


def send(src, dst, send_sem, recv_sem, dp, seq):
    pltpu.make_async_remote_copy(
        src_ref=src,
        dst_ref=dst,
        send_sem=send_sem,
        recv_sem=recv_sem,
        device_id=(dp, seq),
        device_id_type=MESH,
    ).start()


def drain(ref, sem):
    pltpu.make_async_copy(ref, ref, sem).wait()


def barrier(me):
    sem = pltpu.get_barrier_semaphore()

    def slab(i, carry):
        to = lax.rem(me.k + i, 32) * 2 + me.core
        pl.semaphore_signal(sem, inc=1, device_id=(me.dp, to), device_id_type=MESH)
        return carry

    def plane(i, carry):
        to = lax.rem(me.m + i, 32)
        pl.semaphore_signal(
            sem, inc=1, device_id=(to // 4, me.z * 4 + to % 4), device_id_type=MESH
        )
        return carry

    lax.fori_loop(1, 32, slab, 0)
    lax.fori_loop(1, 32, plane, 0)
    pl.semaphore_wait(sem, 62)


def dot(a, b):
    return lax.dot_general(a, b, (((1,), (0,)), ((), ())), preferred_element_type=F32)


def dot_nt(a, b):
    return lax.dot_general(a, b, (((1,), (1,)), ((), ())), preferred_element_type=F32)


def dot_tn(a, b):
    return lax.dot_general(a, b, (((0,), (0,)), ((), ())), preferred_element_type=F32)


def iota(shape, dim):
    return lax.broadcasted_iota(jnp.int32, shape, dim)


def one_hot(condition):
    return jnp.where(condition, 1.0, 0.0).astype(BF16)


def gather_order():
    j = iota((1, D), 1)
    block, rest = j // 96, j % 96
    core, half, x_lo = block // 4, (block // 2) % 2, block % 2
    z8, r = rest // 12, rest % 12
    natural = ((half * 8 + z8) * 4 + x_lo * 2 + core) * 12 + r
    return one_hot(iota((D, D), 0) == natural)


def scatter_order():
    j = iota((1, D), 1)
    dp, rest = j // 96, j % 96
    x_lo, z, r = rest // 48, (rest % 48) // 3, rest % 3
    natural = dp * 96 + z * 6 + x_lo * 3 + r
    return one_hot(iota((D, D), 0) == natural)


def split3(a):
    high = a.astype(BF16)
    rest = a - high.astype(F32)
    mid = rest.astype(BF16)
    low = (rest - mid.astype(F32)).astype(BF16)
    return jnp.concatenate([high.astype(F32), mid.astype(F32), low.astype(F32)], 0).astype(BF16)


def start_tokens(me, src, buf, local_sem, send_sem, recv_sem):
    pltpu.make_async_copy(src.at[me.k], buf.at[me.k], local_sem).start()

    def step(i, carry):
        offset = jnp.where(i % 2 == 0, 32 - i // 2, (i + 1) // 2)
        to = lax.rem(me.k + offset, 32)
        send(src.at[to], buf.at[me.k], send_sem, recv_sem, me.dp, to * 2 + me.core)
        return carry

    lax.fori_loop(1, 32, step, 0)


def wait_tokens(me, src, buf, local_sem, recv_sem):
    pltpu.make_async_copy(src.at[me.k], buf.at[me.k], local_sem).wait()
    drain(buf.at[pl.ds(0, 31)], recv_sem)


def start_pair(me, buf, out, box, send_sem, recv_sem):
    rows = buf[...].astype(F32).reshape(256, D).astype(BF16)
    r, col = iota((128, 1), 0), iota((128, 256), 1)
    at = (r % 32) * 8 + r // 32
    theirs = dot(one_hot(col == at + 4 * (1 - me.core)), rows)
    box[...] = theirs.astype(BF16).reshape(4, 32, D)
    send(box, out.at[me.core], send_sem, recv_sem, me.dp, me.seq + 1 - 2 * me.core)
    mine = dot(one_hot(col == at + 4 * me.core), rows)
    out[me.core] = mine.astype(BF16).reshape(4, 32, D)


def start_weights_z(me, piece, buf, local_sem, send_sem, recv_sem):
    pltpu.make_async_copy(piece, buf.at[me.z], local_sem).start()

    def step(i, carry):
        to = lax.rem(me.z + i, 16)
        send(piece, buf.at[me.z], send_sem, recv_sem, me.dp, to * 4 + me.role)
        return carry

    lax.fori_loop(1, 16, step, 0)


def start_weights_first(me, piece, buf, full, local_sem, recv_z, send_sem, recv_a, recv_b):
    pltpu.make_async_copy(piece, buf.at[me.z], local_sem).wait()
    drain(buf.at[pl.ds(0, 15)], recv_z)
    rows = buf[...].reshape(256, 384)
    r = iota((192, 1), 0)
    pick = one_hot(iota((192, 256), 1) == (r // 12) * 16 + r % 12)
    block = dot(pick, rows).astype(BF16)
    full[me.x_hi, me.y, me.core, 0, me.x_lo] = block[:96]
    full[me.x_hi, me.y, me.core, 1, me.x_lo] = block[96:]
    mine = full.at[me.x_hi, me.y, me.core, 0, me.x_lo]
    for i in range(1, 4):
        x = lax.rem(me.x + i, 4)
        send(mine, mine, send_sem, recv_a, (x // 2) * 4 + me.y, me.z * 4 + (x % 2) * 2 + me.core)
    mine = full.at[me.x_hi, me.y, me.core, 1, me.x_lo]
    for i in range(1, 4):
        y = lax.rem(me.y + i, 4)
        send(mine, mine, send_sem, recv_b, me.x_hi * 4 + y, me.seq)


def start_weights_second(me, full, recv_a, recv_b, send_sem, recv_a2, recv_b2, send_pair, recv_pair):
    pair = me.seq + 1 - 2 * me.core
    drain(full.at[0, pl.ds(0, 3), 0, 0, 0], recv_a)
    mine = full.at[:, me.y, me.core, 0]
    for i in range(1, 4):
        y = lax.rem(me.y + i, 4)
        send(mine, mine, send_sem, recv_a2.at[i - 1], me.x_hi * 4 + y, me.seq)
    send(mine, mine, send_pair, recv_pair, me.dp, pair)
    drain(full.at[0, pl.ds(0, 3), 0, 0, 0], recv_b)
    mine = full.at[me.x_hi, :, me.core, 1, me.x_lo]
    for i in range(1, 4):
        x = lax.rem(me.x + i, 4)
        send(
            mine, mine, send_sem, recv_b2.at[i - 1],
            (x // 2) * 4 + me.y, me.z * 4 + (x % 2) * 2 + me.core,
        )
    send(mine, mine, send_pair, recv_pair, me.dp, pair)


def finish_weights(me, full, recv_a2, recv_b2, send_pair, recv_pair):
    pair = me.seq + 1 - 2 * me.core
    for i in range(1, 4):
        y = lax.rem(me.y + 4 - i, 4)
        block = full.at[:, y, me.core, 0]
        drain(block, recv_a2.at[i - 1])
        send(block, block, send_pair, recv_pair, me.dp, pair)
        x = lax.rem(me.x + 4 - i, 4)
        block = full.at[x // 2, :, me.core, 1, x % 2]
        drain(block, recv_b2.at[i - 1])
        send(block, block, send_pair, recv_pair, me.dp, pair)
    drain(full.at[:, :, 0], recv_pair)


def reduce_pooled(me, part, box1, in1, buf2, pool, send_sem, recv1, recv2, recv3):
    for q in range(4):
        box1[q] = part[2 * q : 2 * q + 2, :]
    in1[me.role] = box1[me.role]
    for i in range(1, 4):
        to = lax.rem(me.role + i, 4)
        send(box1.at[to], in1.at[me.role], send_sem.at[0], recv1, me.dp, me.z * 4 + to)
    drain(in1.at[pl.ds(0, 3)], recv1)
    buf2[me.z] = jnp.sum(in1[...], 0)

    def along_z(i, carry):
        to = lax.rem(me.z + i, 16)
        send(buf2.at[me.z], buf2.at[me.z], send_sem.at[1], recv2, me.dp, to * 4 + me.role)
        return carry

    lax.fori_loop(1, 16, along_z, 0)
    drain(buf2.at[pl.ds(0, 15)], recv2)
    pool[me.m] = jnp.sum(buf2[...], 0) * (1.0 / 2048.0)

    def in_plane(i, carry):
        to = lax.rem(me.m + i, 32)
        send(pool.at[me.m], pool.at[me.m], send_sem.at[2], recv3, to // 4, me.z * 4 + to % 4)
        return carry

    lax.fori_loop(1, 32, in_plane, 0)
    drain(pool.at[pl.ds(0, 31)], recv3)
    drain(in1.at[pl.ds(0, 3)], send_sem.at[0])
    drain(buf2.at[pl.ds(0, 15)], send_sem.at[1])
    drain(pool.at[pl.ds(0, 31)], send_sem.at[2])


def start_weight_sum(me, box, buf, send_sem, recv_sem):
    buf[me.m] = box[me.m]

    def step(i, carry):
        to = lax.rem(me.m + i, 32)
        send(box.at[to], buf.at[me.m], send_sem, recv_sem, to // 4, me.z * 4 + to % 4)
        return carry

    lax.fori_loop(1, 32, step, 0)


def second_weight_sum(me, buf, recv_sem, box_z, buf_z, send_sem, recv_z):
    drain(buf.at[pl.ds(0, 31)], recv_sem)
    total = lax.fori_loop(
        0, 32, lambda i, t: t + buf[i].astype(F32), jnp.zeros((48, 384), F32)
    )
    box_z[...] = jnp.zeros_like(box_z)
    for z in range(16):
        box_z[z, 0:3, :] = total[3 * z : 3 * z + 3, :]
    buf_z[me.z] = box_z[me.z]

    def step(i, carry):
        to = lax.rem(me.z + i, 16)
        send(box_z.at[to], buf_z.at[me.z], send_sem, recv_z, me.dp, to * 4 + me.role)
        return carry

    lax.fori_loop(1, 16, step, 0)


def third_weight_sum(me, buf_z, recv_z, rows, send_sem, recv_sem):
    drain(buf_z.at[pl.ds(0, 15)], recv_z)
    rows[me.core] = jnp.sum(buf_z[...], 0)
    send(
        rows.at[me.core], rows.at[me.core], send_sem, recv_sem,
        me.dp, me.seq + 1 - 2 * me.core,
    )


def finish_weight_sum(me, rows, recv_sem, out):
    drain(rows.at[0], recv_sem)
    left, right = rows[0], rows[1]
    first = me.core == 0
    out[0:1, 0:384] = jnp.where(first, left[0:1], right[1:2])
    out[0:1, 384:768] = jnp.where(first, right[0:1], left[2:3])
    out[0:1, 768:1152] = jnp.where(first, left[1:2], right[2:3])


def start_back_pair(me, grads, buf, send_sem, recv_sem):
    theirs = 1 - me.core
    send(grads.at[theirs], buf.at[me.core], send_sem, recv_sem, me.dp, me.seq + 1 - 2 * me.core)
    buf[me.core] = grads[me.core]


def start_back(me, buf, recv_pair, box, out, local_sem, send_sem, recv_sem):
    drain(buf.at[0], recv_pair)
    r = iota((256, 1), 0)
    at = ((r // 4) % 2) * 128 + (r % 4) * 32 + r // 8
    rows = dot(one_hot(iota((256, 256), 1) == at), buf[...].reshape(256, D))
    box[...] = rows.reshape(32, 8, D).astype(BF16)
    start_tokens(me, box, out, local_sem, send_sem, recv_sem)


def normalize(x):
    centered = x - jnp.mean(x, -1, keepdims=True)
    inverse = lax.rsqrt(jnp.mean(centered * centered, -1, keepdims=True) + EPS)
    return centered * inverse, inverse


def clip_pick():
    return one_hot((iota((8, 256), 1) % 32) // 4 == iota((8, 256), 0))


def unit_rows(ref, u, columns):
    return jnp.concatenate(
        [ref[u * 64 : u * 64 + 64, columns], ref[128 + u * 64 : 192 + u * 64, columns]], 0
    )


def put_rows(ref, u, columns, value):
    ref[u * 64 : u * 64 + 64, columns] = value[:64]
    ref[128 + u * 64 : 192 + u * 64, columns] = value[64:]


def heads(a):
    even = iota(a.shape, 1) < 64
    zero = jnp.zeros_like(a)
    return jnp.concatenate([jnp.where(even, a, zero), jnp.where(even, zero, a)], 0)


def same_patch():
    return (iota((256, 128), 0) // 32) % 2 == (iota((256, 128), 1) // 32) % 2


def forward(tokens, full, scale, bias, order, qkv, prob, context, part):
    x = tokens[...].reshape(256, D)
    unit, _ = normalize(x.astype(F32))
    normed = (unit * scale[...] + bias[...]).astype(BF16)
    normed = dot(normed, order[...]).astype(BF16)
    for n in range(6):
        weight = full[n // 4, n % 4].reshape(D, 384)
        qkv[:, n * 384 : n * 384 + 384] = dot(normed, weight).astype(BF16)
    keep = same_patch()
    for j in range(6):
        for u in range(2):
            columns = [slice(s * D + j * 128, s * D + j * 128 + 128) for s in range(3)]
            query, key, value = [unit_rows(qkv, u, c) for c in columns]
            score = dot_nt(heads(query), key) * 0.125
            score = jnp.where(keep, score, NEG)
            top = jnp.max(score, -1, keepdims=True)
            weight = jnp.exp(score - top)
            p = weight / jnp.sum(weight, -1, keepdims=True)
            prob[j * 2 + u] = p
            half = p.astype(BF16)
            both = jnp.concatenate([half[:128], half[128:]], 1)
            mixed = dot(both, heads(value)).astype(BF16)
            put_rows(context, u, slice(j * 128, j * 128 + 128), mixed)
    pick = clip_pick()
    ctx_sum = split3(dot(pick, context[...]))
    ctx_sum = dot(ctx_sum, order[...]).astype(BF16)
    sums = dot(pick, x)
    for n in range(2):
        weight = full[1, 2 + n].reshape(D, 384)
        s = dot(ctx_sum, weight)
        columns = slice(n * 384, n * 384 + 384)
        part[:, columns] = sums[:, columns] + s[0:8] + s[8:16] + s[16:24]


def spread(upstream, grad_clip):
    pick = one_hot((iota((256, 24), 0) % 32) // 4 == iota((256, 24), 1) % 8)
    return upstream[...].reshape(256, D).astype(F32) + dot(pick, split3(grad_clip))


def backward_weights(grad_half, full, order, scatter, context, grad_context, box):
    back = dot_nt(grad_half[:, :384], full[1, 2].reshape(D, 384))
    back = back + dot_nt(grad_half[:, 384:], full[1, 3].reshape(D, 384))
    grad_context[...] = dot_nt(back.astype(BF16), order[...]).astype(BF16)
    ordered = dot(context[...], scatter[...]).astype(BF16)
    term = dot_tn(ordered, grad_half).astype(BF16)
    for n in range(16):
        for c in range(2):
            box[n * 2 + c] = term[n * 48 : n * 48 + 48, c * 384 : c * 384 + 384]


def backward_attention(qkv, prob, grad_context, grad_qkv):
    for j in range(6):
        for u in range(2):
            columns = [slice(s * D + j * 128, s * D + j * 128 + 128) for s in range(3)]
            query, key, value = [unit_rows(qkv, u, c) for c in columns]
            grad = heads(unit_rows(grad_context, u, slice(j * 128, j * 128 + 128)))
            p = prob[j * 2 + u]
            half = p.astype(BF16)
            grad_prob = dot_nt(grad, value)
            grad_value = dot_tn(half, grad).astype(BF16)
            row = jnp.sum(p * grad_prob, -1, keepdims=True)
            grad_score = (p * (grad_prob - row) * 0.125).astype(BF16)
            both = jnp.concatenate([grad_score[:128], grad_score[128:]], 1)
            put_rows(grad_qkv, u, columns[0], dot(both, heads(key)).astype(BF16))
            put_rows(grad_qkv, u, columns[1], dot_tn(grad_score, heads(query)).astype(BF16))
            put_rows(grad_qkv, u, columns[2], grad_value)


def backward_tokens(tokens, grad_output, grad_qkv, full, order, scale, out):
    back = jnp.zeros((256, D), F32)
    for n in range(6):
        weight = full[n // 4, n % 4].reshape(D, 384)
        back = back + dot_nt(grad_qkv[:, n * 384 : n * 384 + 384], weight)
    grad_normed = dot_nt(back.astype(BF16), order[...])
    scaled = grad_normed * scale[...]
    unit, inverse = normalize(tokens[...].reshape(256, D).astype(F32))
    grad_norm = inverse * (
        scaled
        - jnp.mean(scaled, -1, keepdims=True)
        - unit * jnp.mean(scaled * unit, -1, keepdims=True)
    )
    out[...] = (grad_output + grad_norm).astype(BF16).reshape(2, 4, 32, D)


def kernel_in(
    video, upstream, piece, tokens, ups, full,
    vbuf, ubuf, vbox, ubox, zbuf, local, tok_send, tok_recv, pair_send, pair_recv,
    w_send, w_recv, w_recv_a2, w_recv_b2, wp_send, wp_recv,
):
    me = Place()
    barrier(me)
    start_weights_z(me, piece, zbuf, local.at[0], w_send.at[0], w_recv.at[0])
    start_tokens(me, video, vbuf, local.at[1], tok_send.at[0], tok_recv.at[0])
    start_weights_first(
        me, piece, zbuf, full, local.at[0], w_recv.at[0], w_send.at[1], w_recv.at[1], w_recv.at[2]
    )
    start_tokens(me, upstream, ubuf, local.at[2], tok_send.at[1], tok_recv.at[1])
    start_weights_second(
        me, full, w_recv.at[1], w_recv.at[2], w_send.at[2], w_recv_a2, w_recv_b2, wp_send, wp_recv
    )
    wait_tokens(me, video, vbuf, local.at[1], tok_recv.at[0])
    start_pair(me, vbuf, tokens, vbox, pair_send.at[0], pair_recv.at[0])
    finish_weights(me, full, w_recv_a2, w_recv_b2, wp_send, wp_recv)
    wait_tokens(me, upstream, ubuf, local.at[2], tok_recv.at[1])
    start_pair(me, ubuf, ups, ubox, pair_send.at[1], pair_recv.at[1])
    drain(tokens.at[0], pair_recv.at[0])
    drain(ups.at[0], pair_recv.at[1])
    drain(zbuf.at[pl.ds(0, 15)], w_send.at[0])
    drain(full.at[0, pl.ds(0, 3), 0, 0], w_send.at[1])
    drain(full.at[0, pl.ds(0, 3)], w_send.at[2])
    drain(full.at[:, :, 0], wp_send)
    for i in range(2):
        drain(vbuf.at[pl.ds(0, 31)], tok_send.at[i])
        drain(vbox, pair_send.at[i])


def kernel_forward(tokens, full, scale, bias, order, qkv, prob, context, part):
    forward(tokens, full, scale, bias, order, qkv, prob, context, part)


def kernel_pooled(part, pooled, box1, in1, buf2, pool, send_sem, recv_sem):
    me = Place()
    barrier(me)
    reduce_pooled(
        me, part, box1, in1, buf2, pool, send_sem, recv_sem.at[0], recv_sem.at[1], recv_sem.at[2]
    )
    for m in range(32):
        pooled[2 * m : 2 * m + 2, :] = pool[m]


def kernel_backward(
    tokens, ups, full, scale, order, scatter, qkv, prob, context, grad_clip, grads, box,
    grad_context, grad_qkv, grad_out,
):
    grad_out[...] = spread(ups, grad_clip[...])
    backward_weights(
        grad_out[...].astype(BF16), full, order, scatter, context, grad_context, box
    )
    backward_attention(qkv, prob, grad_context, grad_qkv)
    backward_tokens(tokens, grad_out[...], grad_qkv, full, order, scale, grads)


def kernel_out(
    grads, box, video_out, weight_out,
    pair_buf, out_box, gw_buf, box_z, buf_z, rows, local, send_sem, recv_sem,
):
    me = Place()
    barrier(me)
    start_back_pair(me, grads, pair_buf, send_sem.at[0], recv_sem.at[0])
    start_weight_sum(me, box, gw_buf, send_sem.at[1], recv_sem.at[1])
    start_back(
        me, pair_buf, recv_sem.at[0], out_box, video_out, local, send_sem.at[2], recv_sem.at[2]
    )
    second_weight_sum(me, gw_buf, recv_sem.at[1], box_z, buf_z, send_sem.at[3], recv_sem.at[3])
    third_weight_sum(me, buf_z, recv_sem.at[3], rows, send_sem.at[4], recv_sem.at[4])
    finish_weight_sum(me, rows, recv_sem.at[4], weight_out)
    wait_tokens(me, out_box, video_out, local, recv_sem.at[2])
    drain(pair_buf.at[0], send_sem.at[0])
    drain(gw_buf.at[pl.ds(0, 31)], send_sem.at[1])
    drain(out_box.at[pl.ds(0, 31)], send_sem.at[2])
    drain(box_z.at[pl.ds(0, 15)], send_sem.at[3])
    drain(rows.at[0], send_sem.at[4])


def shape(*dims, dtype=BF16):
    return jax.ShapeDtypeStruct(dims, dtype)


def call(kernel, outs, ins, out_spaces, in_spaces, scratch, collective=None):
    params = dict(vmem_limit_bytes=VMEM_LIMIT)
    if collective is not None:
        params.update(collective_id=collective, has_side_effects=True)
    return pl.pallas_call(
        kernel,
        out_shape=outs,
        in_specs=[pl.BlockSpec(memory_space=s) for s in in_spaces],
        out_specs=[pl.BlockSpec(memory_space=s) for s in out_spaces],
        scratch_shapes=scratch,
        compiler_params=pltpu.CompilerParams(**params),
    )(*ins)


def contrast(pooled, windows, positives):
    root = D ** (-0.5)
    clip_unit = pooled * lax.rsqrt(jnp.mean(pooled * pooled, -1, keepdims=True) + EPS) * root
    window_unit = windows * lax.rsqrt(jnp.mean(windows * windows, -1, keepdims=True) + EPS) * root
    logits = jnp.dot(clip_unit, window_unit.T, precision=lax.Precision.HIGHEST) * SHARP
    matched = positives[:, None] == lax.iota(jnp.int32, logits.shape[1])[None, :]
    positive = jnp.sum(jnp.where(matched, logits, jnp.zeros_like(logits)), 1)
    row_lse = jax.nn.logsumexp(logits, axis=1)
    column_lse = jax.nn.logsumexp(logits, axis=0)
    return 0.5 * (jnp.mean(row_lse) + jnp.mean(column_lse)) - jnp.mean(positive)


def per_device(video, upstream, standardize_scale, ln_bias, w_qkv, w_out, windows, positives):
    V, A = pltpu.VMEM, pl.ANY
    dma = pltpu.SemaphoreType.DMA
    dp = lax.axis_index("dp")
    scale, bias = standardize_scale.reshape(1, D), ln_bias.reshape(1, D)
    both = jnp.concatenate([w_qkv, w_out], 1)
    piece = jnp.pad(lax.dynamic_slice(both, (0, dp * 384), (12, 384)), ((0, 4), (0, 0)))
    order, scatter = gather_order(), scatter_order()
    tokens, ups, full = call(
        kernel_in,
        [shape(2, 4, 32, D), shape(2, 4, 32, D), shape(2, 4, 2, 2, 2, 96, 384)],
        [video.reshape(32, 8, D), upstream.reshape(32, 8, D), piece],
        [V, V, V],
        [A, A, V],
        [
            V((32, 8, D), BF16), V((32, 8, D), BF16), V((4, 32, D), BF16), V((4, 32, D), BF16),
            V((16, 16, 384), BF16), dma((3,)), dma((2,)), dma((2,)), dma((2,)), dma((2,)),
            dma((3,)), dma((3,)), dma((3,)), dma((3,)), dma, dma,
        ],
        collective=1,
    )
    qkv, prob, context, part = call(
        kernel_forward,
        [shape(256, 3 * D), shape(12, 256, 128, dtype=F32), shape(256, D), shape(8, D, dtype=F32)],
        [tokens, full, scale, bias, order],
        [V] * 4,
        [V] * 5,
        [],
    )
    (pooled,) = call(
        kernel_pooled,
        [shape(64, D, dtype=F32)],
        [part],
        [V],
        [V],
        [
            V((4, 2, D), F32), V((4, 2, D), F32), V((16, 2, D), F32), V((32, 2, D), F32),
            dma((3,)), dma((3,)),
        ],
        collective=2,
    )
    contrast_loss, grad_pooled = jax.value_and_grad(contrast)(pooled, windows, positives)
    grad_clip = 64.0 * lax.dynamic_slice(grad_pooled, (dp * 8, 0), (8, D))
    grads, box = call(
        kernel_backward,
        [shape(2, 4, 32, D), shape(32, 48, 384)],
        [tokens, ups, full, scale, order, scatter, qkv, prob, context, grad_clip],
        [V, V],
        [V] * 10,
        [V((256, D), BF16), V((256, 3 * D), BF16), V((256, D), F32)],
    )
    grad_video, grad_out_weight = call(
        kernel_out,
        [shape(32, 8, D), shape(1, 1152, dtype=F32)],
        [grads, box],
        [A, V],
        [V, V],
        [
            V((2, 4, 32, D), BF16), V((32, 8, D), BF16), V((32, 48, 384), BF16),
            V((16, 4, 384), F32), V((16, 4, 384), F32), V((2, 4, 384), F32),
            dma, dma((5,)), dma((5,)),
        ],
        collective=3,
    )
    return grad_video.reshape(1, 1, 256, D), grad_out_weight, pooled, contrast_loss


def solution(mesh):
    in_specs = (
        P("dp", "seq", None, None),
        P("dp", "seq", None, None),
        P(),
        P(),
        P("seq", None),
        P("seq", None),
        P(),
        P(),
    )
    out_specs = (P("dp", "seq", None, None), P(("dp", "seq"), None), P(), P())
    return jax.shard_map(
        per_device, mesh=mesh, in_specs=in_specs, out_specs=out_specs, check_vma=False
    )
```

```python
import jax
import jax.numpy as jnp
from jax import lax
from jax.experimental import pallas as pl
from jax.experimental.pallas import tpu as pltpu
from jax.sharding import PartitionSpec as P

MESH = pl.DeviceIdType.MESH
F32 = jnp.float32
BF16 = jnp.bfloat16
D = 768
EPS = 1e-6
NEG = -1e30
SHARP = 1.0 / 0.07
VMEM_LIMIT = 56 * 1024 * 1024


class Place:
    def __init__(self):
        self.dp = lax.axis_index("dp")
        self.seq = lax.axis_index("seq")
        self.x_hi = self.dp // 4
        self.y = self.dp % 4
        self.z = self.seq // 4
        self.role = self.seq % 4
        self.x_lo = self.role // 2
        self.core = self.seq % 2
        self.k = self.seq // 2
        self.x = self.x_hi * 2 + self.x_lo
        self.m = self.dp * 4 + self.role


def send(src, dst, send_sem, recv_sem, dp, seq):
    pltpu.make_async_remote_copy(
        src_ref=src,
        dst_ref=dst,
        send_sem=send_sem,
        recv_sem=recv_sem,
        device_id=(dp, seq),
        device_id_type=MESH,
    ).start()


def drain(ref, sem):
    pltpu.make_async_copy(ref, ref, sem).wait()


def announce(me):
    sem = pltpu.get_barrier_semaphore()

    def slab(i, carry):
        to = lax.rem(me.k + i, 32) * 2 + me.core
        pl.semaphore_signal(sem, inc=1, device_id=(me.dp, to), device_id_type=MESH)
        return carry

    def plane(i, carry):
        to = lax.rem(me.m + i, 32)
        pl.semaphore_signal(
            sem, inc=1, device_id=(to // 4, me.z * 4 + to % 4), device_id_type=MESH
        )
        return carry

    lax.fori_loop(1, 32, slab, 0)
    lax.fori_loop(1, 32, plane, 0)


def arrive():
    pl.semaphore_wait(pltpu.get_barrier_semaphore(), 62)


def dot(a, b):
    return lax.dot_general(a, b, (((1,), (0,)), ((), ())), preferred_element_type=F32)


def dot_nt(a, b):
    return lax.dot_general(a, b, (((1,), (1,)), ((), ())), preferred_element_type=F32)


def dot_tn(a, b):
    return lax.dot_general(a, b, (((0,), (0,)), ((), ())), preferred_element_type=F32)


def iota(shape, dim):
    return lax.broadcasted_iota(jnp.int32, shape, dim)


def one_hot(condition):
    return jnp.where(condition, 1.0, 0.0).astype(BF16)


def gather_order(me):
    j = iota((1, D), 1)
    block, rest = j // 96, j % 96
    core, chunk, x_lo = block // 4, (block // 2) % 2, block % 2
    z8, r = rest // 12, rest % 12
    far = jnp.where(z8 == 0, 0, z8 + 4)
    near = jnp.where(z8 < 4, z8 + 1, z8 + 8)
    from_z = (me.z + jnp.where(chunk == 0, far, near)) % 16
    natural = (from_z * 4 + x_lo * 2 + core) * 12 + r
    return one_hot(iota((D, D), 0) == natural)


def scatter_order():
    j = iota((1, D), 1)
    dp, rest = j // 96, j % 96
    x_lo, z, r = rest // 48, (rest % 48) // 3, rest % 3
    natural = dp * 96 + z * 6 + x_lo * 3 + r
    return one_hot(iota((D, D), 0) == natural)


def split3(a):
    high = a.astype(BF16)
    rest = a - high.astype(F32)
    mid = rest.astype(BF16)
    low = (rest - mid.astype(F32)).astype(BF16)
    return jnp.concatenate([high.astype(F32), mid.astype(F32), low.astype(F32)], 0).astype(BF16)


def start_tokens(me, src, buf, local_sem, send_sem, recv_sem):
    pltpu.make_async_copy(src.at[me.k], buf.at[me.k], local_sem).start()

    def step(i, carry):
        j = 32 - i
        to = lax.rem(me.k + jnp.where(j % 2 == 0, 32 - j // 2, (j + 1) // 2), 32)
        send(src.at[to], buf.at[me.k], send_sem, recv_sem, me.dp, to * 2 + me.core)
        return carry

    lax.fori_loop(1, 32, step, 0)


def wait_tokens(me, src, buf, local_sem, recv_sem):
    pltpu.make_async_copy(src.at[me.k], buf.at[me.k], local_sem).wait()
    drain(buf.at[pl.ds(0, 31)], recv_sem)


def start_pair(me, buf, out, box, send_sem, recv_sem):
    rows = buf[...].astype(F32).reshape(256, D).astype(BF16)
    r, col = iota((128, 1), 0), iota((128, 256), 1)
    at = (r % 32) * 8 + r // 32
    theirs = dot(one_hot(col == at + 4 * (1 - me.core)), rows)
    box[...] = theirs.astype(BF16).reshape(4, 32, D)
    send(box, out.at[me.core], send_sem, recv_sem, me.dp, me.seq + 1 - 2 * me.core)
    mine = dot(one_hot(col == at + 4 * me.core), rows)
    out[me.core] = mine.astype(BF16).reshape(4, 32, D)


OFFSETS = (0, 5, 6, 7, 8, 9, 10, 11, 1, 2, 3, 4, 12, 13, 14, 15)


def start_weights(me, zbuf, send_sem, recv_z):
    for d in (8, 7, 9, 6, 10, 5, 11, 4, 12, 3, 13, 2, 14, 1, 15):
        j = OFFSETS.index(16 - d)
        to = lax.rem(me.z + d, 16) * 4 + me.role
        send(zbuf.at[0], zbuf.at[j], send_sem, recv_z.at[j // 8], me.dp, to)


def x_device(me, x):
    return (x // 2) * 4 + me.y, me.z * 4 + (x % 2) * 2 + me.core


def spread_first(me, zbuf, full, chunk, recv_z, send_sem, recv):
    drain(zbuf.at[pl.ds(0, 7 + chunk)], recv_z.at[chunk])
    r = iota((96, 1), 0)
    pick = one_hot(iota((96, 128), 1) == (r // 12) * 16 + r % 12)
    rows = zbuf[chunk * 8 : chunk * 8 + 8].reshape(128, 384)
    block = dot(pick, rows).astype(BF16)
    full[me.x_hi, me.y, me.core, chunk, me.x_lo] = block.reshape(2, 48, 384)
    a = full.at[me.x_hi, me.y, me.core, chunk, me.x_lo, 0]
    b = full.at[me.x_hi, me.y, me.core, chunk, me.x_lo, 1]
    for i in (2, 1, 3):
        send(a, a, send_sem, recv.at[chunk, 0], *x_device(me, lax.rem(me.x + i, 4)))
        send(b, b, send_sem, recv.at[chunk, 1], me.x_hi * 4 + lax.rem(me.y + i, 4), me.seq)


def spread_second(me, full, chunk, recv_first, send_sem, recv, send_pair, recv_pair):
    pair = me.seq + 1 - 2 * me.core
    drain(full.at[0, pl.ds(0, 3), 0, 0, 0, 0], recv_first.at[chunk, 0])
    a = full.at[:, me.y, me.core, chunk, :, 0]
    for n, i in enumerate((1, 3)):
        send(a, a, send_sem, recv.at[chunk, 0, n], me.x_hi * 4 + lax.rem(me.y + i, 4), me.seq)
    drain(full.at[0, pl.ds(0, 3), 0, 0, 0, 0], recv_first.at[chunk, 1])
    b = full.at[me.x_hi, :, me.core, chunk, me.x_lo, 1]
    for n, i in enumerate((1, 3)):
        send(b, b, send_sem, recv.at[chunk, 1, n], *x_device(me, lax.rem(me.x + i, 4)))
    send(a, a, send_pair, recv_pair, me.dp, pair)
    send(b, b, send_pair, recv_pair, me.dp, pair)


def spread_third(me, full, chunk, recv_second, send_sem, recv, send_pair, recv_pair):
    pair = me.seq + 1 - 2 * me.core
    for n, (i, o) in enumerate(((3, 1), (1, 3))):
        y, x = lax.rem(me.y + i, 4), lax.rem(me.x + i, 4)
        a = full.at[:, y, me.core, chunk, :, 0]
        drain(a, recv_second.at[chunk, 0, n])
        half = full.at[n, y, me.core, chunk, :, 0]
        send(half, half, send_sem, recv.at[chunk, 0, n], me.x_hi * 4 + lax.rem(me.y + o, 4), me.seq)
        b = full.at[x // 2, :, me.core, chunk, x % 2, 1]
        drain(b, recv_second.at[chunk, 1, n])
        half = full.at[x // 2, pl.ds(2 * n, 2), me.core, chunk, x % 2, 1]
        send(half, half, send_sem, recv.at[chunk, 1, n], *x_device(me, lax.rem(me.x + o, 4)))
        send(a, a, send_pair, recv_pair, me.dp, pair)
        send(b, b, send_pair, recv_pair, me.dp, pair)


def spread_last(me, full, chunk, recv_third, send_pair, recv_pair):
    pair = me.seq + 1 - 2 * me.core
    y, x = lax.rem(me.y + 2, 4), lax.rem(me.x + 2, 4)
    for n in range(2):
        a = full.at[n, y, me.core, chunk, :, 0]
        drain(a, recv_third.at[chunk, 0, n])
        send(a, a, send_pair, recv_pair, me.dp, pair)
        b = full.at[x // 2, pl.ds(2 * n, 2), me.core, chunk, x % 2, 1]
        drain(b, recv_third.at[chunk, 1, n])
        send(b, b, send_pair, recv_pair, me.dp, pair)


def start_pooled(me, part, box1, in1, send_sem, recv_sem):
    for q in range(4):
        box1[q] = part[2 * q : 2 * q + 2, :]
    in1[me.role] = box1[me.role]
    for i in range(1, 4):
        to = lax.rem(me.role + i, 4)
        send(box1.at[to], in1.at[me.role], send_sem, recv_sem, me.dp, me.z * 4 + to)


def pooled_along_z(me, in1, recv_first, buf2, send_sem, recv_sem):
    drain(in1.at[pl.ds(0, 3)], recv_first)
    buf2[me.z] = jnp.sum(in1[...], 0)

    def step(i, carry):
        j = 16 - i
        to = lax.rem(me.z + jnp.where(j % 2 == 0, 16 - j // 2, (j + 1) // 2), 16)
        send(buf2.at[me.z], buf2.at[me.z], send_sem, recv_sem, me.dp, to * 4 + me.role)
        return carry

    lax.fori_loop(1, 16, step, 0)


def pooled_in_plane(me, buf2, recv_second, pool, send_sem, recv_sem):
    drain(buf2.at[pl.ds(0, 15)], recv_second)
    pool[me.m] = jnp.sum(buf2[...], 0) * (1.0 / 2048.0)

    def step(i, carry):
        to = lax.rem(me.m + i, 32)
        send(pool.at[me.m], pool.at[me.m], send_sem, recv_sem, to // 4, me.z * 4 + to % 4)
        return carry

    lax.fori_loop(1, 32, step, 0)


def finish_pooled(pool, recv_sem, pooled):
    drain(pool.at[pl.ds(0, 31)], recv_sem)
    for m in range(32):
        pooled[2 * m : 2 * m + 2, :] = pool[m]


def start_weight_sum(me, box, pair_buf, send_sem, recv_sem):
    send(
        box.at[1 - me.core], pair_buf, send_sem, recv_sem, me.dp, me.seq + 1 - 2 * me.core
    )


def plane_weight_sum(me, box, pair_buf, recv_pair, own, buf, send_sem, recv_sem):
    drain(pair_buf, recv_pair)
    own[...] = (box[me.core].astype(F32) + pair_buf[...].astype(F32)).astype(BF16)
    n = me.dp * 2 + me.x_lo
    buf[n] = own[n]

    def step(i, carry):
        to = lax.rem(n + i, 16)
        send(
            own.at[to], buf.at[n], send_sem, recv_sem,
            to // 2, me.z * 4 + (to % 2) * 2 + me.core,
        )
        return carry

    lax.fori_loop(1, 16, step, 0)


def second_weight_sum(me, buf, recv_sem, box_z, buf_z, send_sem, recv_z):
    drain(buf.at[pl.ds(0, 15)], recv_sem)
    total = lax.fori_loop(
        0, 16, lambda i, t: t + buf[i].astype(F32), jnp.zeros((48, 384), F32)
    )
    box_z[...] = jnp.zeros_like(box_z)
    for z in range(16):
        box_z[z, 0:3, :] = total[3 * z : 3 * z + 3, :]
    buf_z[me.z] = box_z[me.z]

    def step(i, carry):
        to = lax.rem(me.z + i, 16)
        send(box_z.at[to], buf_z.at[me.z], send_sem, recv_z, me.dp, to * 4 + me.role)
        return carry

    lax.fori_loop(1, 16, step, 0)


def third_weight_sum(me, buf_z, recv_z, rows, send_sem, recv_sem):
    drain(buf_z.at[pl.ds(0, 15)], recv_z)
    rows[me.core] = jnp.sum(buf_z[...], 0)
    send(
        rows.at[me.core], rows.at[me.core], send_sem, recv_sem,
        me.dp, me.seq + 1 - 2 * me.core,
    )


def finish_weight_sum(me, rows, recv_sem, out):
    drain(rows.at[0], recv_sem)
    left, right = rows[0], rows[1]
    first = me.core == 0
    out[0:1, 0:384] = jnp.where(first, left[0:1], right[1:2])
    out[0:1, 384:768] = jnp.where(first, right[0:1], left[2:3])
    out[0:1, 768:1152] = jnp.where(first, left[1:2], right[2:3])


def start_back_pair(me, grads, buf, send_sem, recv_sem):
    theirs = 1 - me.core
    send(grads.at[theirs], buf.at[me.core], send_sem, recv_sem, me.dp, me.seq + 1 - 2 * me.core)
    buf[me.core] = grads[me.core]


def start_back(me, buf, recv_pair, box, out, local_sem, send_sem, recv_sem):
    drain(buf.at[0], recv_pair)
    r = iota((256, 1), 0)
    at = ((r // 4) % 2) * 128 + (r % 4) * 32 + r // 8
    rows = dot(one_hot(iota((256, 256), 1) == at), buf[...].reshape(256, D))
    box[...] = rows.reshape(32, 8, D).astype(BF16)
    start_tokens(me, box, out, local_sem, send_sem, recv_sem)


def normalize(x):
    centered = x - jnp.mean(x, -1, keepdims=True)
    inverse = lax.rsqrt(jnp.mean(centered * centered, -1, keepdims=True) + EPS)
    return centered * inverse, inverse


def exact(a, b, contract):
    return lax.dot_general(
        a, b, (contract, ((), ())), precision=lax.Precision.HIGHEST, preferred_element_type=F32
    )


def window_units(windows, out):
    w = windows[...]
    out[...] = w * lax.rsqrt(jnp.mean(w * w, -1, keepdims=True) + EPS) * D ** (-0.5)


def contrast(pooled, units, positives, loss, grad):
    p, root = pooled[...], D ** (-0.5)
    inverse = lax.rsqrt(jnp.mean(p * p, -1, keepdims=True) + EPS)
    logits = exact(units[...], p * inverse * root, ((1,), (1,))) * SHARP
    matched = iota((64, 64), 0) == positives[...].reshape(1, 64)
    total = -jnp.sum(jnp.where(matched, logits, 0.0))
    slope = jnp.where(matched, -1.0, 0.0)
    for axis in range(2):
        top = jnp.max(logits, axis, keepdims=True)
        weight = jnp.exp(logits - top)
        size = jnp.sum(weight, axis, keepdims=True)
        total = total + 0.5 * jnp.sum(top + jnp.log(size))
        slope = slope + 0.5 * (weight / size)
    loss[...] = jnp.full((1, 1), total * (1.0 / 64.0), F32)
    grad_unit = exact(slope * (SHARP / 64.0), units[...], ((0,), (0,)))
    inner = jnp.mean(grad_unit * p, -1, keepdims=True)
    grad[...] = inverse * root * (grad_unit - p * (inverse * inverse) * inner)


def clip_pick():
    return one_hot((iota((8, 256), 1) % 32) // 4 == iota((8, 256), 0))


def unit_rows(ref, u, columns):
    return jnp.concatenate(
        [ref[u * 64 : u * 64 + 64, columns], ref[128 + u * 64 : 192 + u * 64, columns]], 0
    )


def put_rows(ref, u, columns, value):
    ref[u * 64 : u * 64 + 64, columns] = value[:64]
    ref[128 + u * 64 : 192 + u * 64, columns] = value[64:]


def heads(a):
    even = iota(a.shape, 1) < 64
    zero = jnp.zeros_like(a)
    return jnp.concatenate([jnp.where(even, a, zero), jnp.where(even, zero, a)], 0)


def same_patch():
    return (iota((256, 128), 0) // 32) % 2 == (iota((256, 128), 1) // 32) % 2


def norm_tokens(tokens, scale, bias, order, normed):
    unit, _ = normalize(tokens[...].reshape(256, D).astype(F32))
    rows = (unit * scale[...].reshape(1, D) + bias[...].reshape(1, D)).astype(BF16)
    normed[...] = dot(rows, order[...]).astype(BF16)


def project(normed, full, qkv):
    for n in range(6):
        weight = full[n // 4, n % 4].reshape(D, 384)
        qkv[:, n * 384 : n * 384 + 384] = dot(normed[...], weight).astype(BF16)


def attend(qkv, prob, context):
    keep = same_patch()
    for j in range(6):
        for u in range(2):
            columns = [slice(s * D + j * 128, s * D + j * 128 + 128) for s in range(3)]
            query, key, value = [unit_rows(qkv, u, c) for c in columns]
            score = dot_nt(heads(query), key) * 0.125
            score = jnp.where(keep, score, NEG)
            top = jnp.max(score, -1, keepdims=True)
            weight = jnp.exp(score - top)
            p = weight / jnp.sum(weight, -1, keepdims=True)
            prob[j * 2 + u] = p
            half = p.astype(BF16)
            both = jnp.concatenate([half[:128], half[128:]], 1)
            mixed = dot(both, heads(value)).astype(BF16)
            put_rows(context, u, slice(j * 128, j * 128 + 128), mixed)


def pool_clips(tokens, context, order, full, part):
    pick = clip_pick()
    ctx_sum = split3(dot(pick, context[...]))
    ctx_sum = dot(ctx_sum, order[...]).astype(BF16)
    sums = dot(pick, tokens[...].reshape(256, D))
    for n in range(2):
        weight = full[1, 2 + n].reshape(D, 384)
        s = dot(ctx_sum, weight)
        columns = slice(n * 384, n * 384 + 384)
        part[:, columns] = sums[:, columns] + s[0:8] + s[8:16] + s[16:24]


def spread(upstream, grad_clip):
    pick = one_hot((iota((256, 24), 0) % 32) // 4 == iota((256, 24), 1) % 8)
    return upstream[...].reshape(256, D).astype(F32) + dot(pick, split3(grad_clip))


def project_back(grad_half, full, order, grad_context):
    back = dot_nt(grad_half[:, :384], full[1, 2].reshape(D, 384))
    back = back + dot_nt(grad_half[:, 384:], full[1, 3].reshape(D, 384))
    grad_context[...] = dot_nt(back.astype(BF16), order[...]).astype(BF16)


def weight_term(grad_half, scatter, context, box):
    ordered = dot(context[...], scatter[...]).astype(BF16)
    term = dot_tn(ordered, grad_half).astype(BF16)
    for n in range(16):
        for c in range(2):
            box[c, n] = term[n * 48 : n * 48 + 48, c * 384 : c * 384 + 384]


def backward_attention(pairs, qkv, prob, grad_context, grad_qkv):
    for j in pairs:
        for u in range(2):
            columns = [slice(s * D + j * 128, s * D + j * 128 + 128) for s in range(3)]
            query, key, value = [unit_rows(qkv, u, c) for c in columns]
            grad = heads(unit_rows(grad_context, u, slice(j * 128, j * 128 + 128)))
            p = prob[j * 2 + u]
            half = p.astype(BF16)
            grad_prob = dot_nt(grad, value)
            grad_value = dot_tn(half, grad).astype(BF16)
            row = jnp.sum(p * grad_prob, -1, keepdims=True)
            grad_score = (p * (grad_prob - row) * 0.125).astype(BF16)
            both = jnp.concatenate([grad_score[:128], grad_score[128:]], 1)
            put_rows(grad_qkv, u, columns[0], dot(both, heads(key)).astype(BF16))
            put_rows(grad_qkv, u, columns[1], dot_tn(grad_score, heads(query)).astype(BF16))
            put_rows(grad_qkv, u, columns[2], grad_value)


def backward_tokens(tokens, grad_output, grad_qkv, full, order, scale, out):
    back = jnp.zeros((256, D), F32)
    for n in range(6):
        weight = full[n // 4, n % 4].reshape(D, 384)
        back = back + dot_nt(grad_qkv[:, n * 384 : n * 384 + 384], weight)
    grad_normed = dot_nt(back.astype(BF16), order[...])
    scaled = grad_normed * scale[...].reshape(1, D)
    unit, inverse = normalize(tokens[...].reshape(256, D).astype(F32))
    grad_norm = inverse * (
        scaled
        - jnp.mean(scaled, -1, keepdims=True)
        - unit * jnp.mean(scaled * unit, -1, keepdims=True)
    )
    out[...] = (grad_output + grad_norm).astype(BF16).reshape(2, 4, 32, D)


def kernel(
    video, upstream, w_qkv, w_out, scale_in, bias_in, windows_in, positives_in,
    video_out, weight_out, pooled_out, loss_out,
    wq, wo, scale, bias, windows, positives, order, scatter,
    vbuf, ubuf, vbox, ubox, tokens, ups, zbuf, full, normed, qkv, prob, context, part,
    box1, in1, buf2, pool, pooled, units, grad_pooled, grad_output, grad_context, grad_qkv, grads,
    box, gw_pair, gw_own, gw_buf, box_z, buf_z, rows, pair_buf, out_box,
    load, local, tok_send, tok_recv, pair_send, pair_recv,
    w_send, recv_z, recv_first, recv_second, recv_third, wp_sem,
    pool_send, pool_recv, gw_send, gw_recv, out_send, out_recv, store,
):
    me = Place()
    loads = [(w_qkv, wq), (w_out, wo), (scale_in, scale), (bias_in, bias)]
    loads += [(windows_in, windows), (positives_in, positives)]
    loads = [pltpu.make_async_copy(a, b, load.at[i]) for i, (a, b) in enumerate(loads)]
    for copy in loads:
        copy.start()
    announce(me)
    loads[0].wait()
    loads[1].wait()
    column = pl.multiple_of(lax.rem(me.dp, 6) * 384, 384)
    column_out = pl.multiple_of(lax.rem(me.dp, 2) * 384, 384)
    piece = jnp.where(me.dp < 6, wq[:, pl.ds(column, 384)], wo[:, pl.ds(column_out, 384)])
    zbuf[0] = jnp.concatenate([piece.astype(F32), jnp.zeros((4, 384), F32)], 0).astype(BF16)
    arrive()
    start_weights(me, zbuf, w_send.at[0], recv_z)
    start_tokens(me, video, vbuf, local.at[0], tok_send.at[0], tok_recv.at[0])
    order[...] = gather_order(me)
    scatter[...] = scatter_order()
    for copy in loads[2:]:
        copy.wait()
    window_units(windows, units)
    for chunk in range(2):
        spread_first(me, zbuf, full, chunk, recv_z, w_send.at[1], recv_first)
    pair_sems = (wp_sem.at[0], wp_sem.at[1])
    for chunk in range(2):
        spread_second(me, full, chunk, recv_first, w_send.at[2], recv_second, *pair_sems)
    for chunk in range(2):
        spread_third(me, full, chunk, recv_second, w_send.at[3], recv_third, *pair_sems)
    wait_tokens(me, video, vbuf, local.at[0], tok_recv.at[0])
    start_pair(me, vbuf, tokens, vbox, pair_send.at[0], pair_recv.at[0])
    start_tokens(me, upstream, ubuf, local.at[1], tok_send.at[1], tok_recv.at[1])
    for chunk in range(2):
        spread_last(me, full, chunk, recv_third, *pair_sems)
    drain(tokens.at[0], pair_recv.at[0])
    norm_tokens(tokens, scale, bias, order, normed)
    drain(full.at[:, :, 0], wp_sem.at[1])
    project(normed, full, qkv)
    attend(qkv, prob, context)
    pool_clips(tokens, context, order, full, part)
    start_pooled(me, part, box1, in1, pool_send.at[0], pool_recv.at[0])
    pooled_along_z(me, in1, pool_recv.at[0], buf2, pool_send.at[1], pool_recv.at[1])
    wait_tokens(me, upstream, ubuf, local.at[1], tok_recv.at[1])
    start_pair(me, ubuf, ups, ubox, pair_send.at[1], pair_recv.at[1])
    pooled_in_plane(me, buf2, pool_recv.at[1], pool, pool_send.at[2], pool_recv.at[2])
    drain(ups.at[0], pair_recv.at[1])
    finish_pooled(pool, pool_recv.at[2], pooled)
    contrast(pooled, units, positives, loss_out, grad_pooled)
    save = pltpu.make_async_copy(pooled, pooled_out, store)
    save.start()
    grad_clip = grad_pooled[pl.ds(pl.multiple_of(me.dp * 8, 8), 8), :] * 64.0
    grad_output[...] = spread(ups, grad_clip)
    grad_half = grad_output[...].astype(BF16)
    weight_term(grad_half, scatter, context, box)
    start_weight_sum(me, box, gw_pair, gw_send.at[0], gw_recv.at[0])
    project_back(grad_half, full, order, grad_context)
    backward_attention((0, 1), qkv, prob, grad_context, grad_qkv)
    plane_weight_sum(
        me, box, gw_pair, gw_recv.at[0], gw_own, gw_buf, gw_send.at[1], gw_recv.at[1]
    )
    backward_attention((2, 3, 4, 5), qkv, prob, grad_context, grad_qkv)
    backward_tokens(tokens, grad_output[...], grad_qkv, full, order, scale, grads)
    start_back_pair(me, grads, pair_buf, out_send.at[0], out_recv.at[0])
    start_back(
        me, pair_buf, out_recv.at[0], out_box, video_out, local.at[2], out_send.at[1], out_recv.at[1]
    )
    second_weight_sum(me, gw_buf, gw_recv.at[1], box_z, buf_z, gw_send.at[2], gw_recv.at[2])
    third_weight_sum(me, buf_z, gw_recv.at[2], rows, gw_send.at[3], gw_recv.at[3])
    finish_weight_sum(me, rows, gw_recv.at[3], weight_out)
    wait_tokens(me, out_box, video_out, local.at[2], out_recv.at[1])
    save.wait()
    drain(zbuf.at[pl.ds(0, 15)], w_send.at[0])
    drain(full.at[0, pl.ds(0, 3), 0, 0], w_send.at[1])
    drain(full.at[0, pl.ds(0, 2)], w_send.at[2])
    drain(full.at[0, 0], w_send.at[3])
    drain(full.at[:, :, 0], wp_sem.at[0])
    for i in range(2):
        drain(vbuf.at[pl.ds(0, 31)], tok_send.at[i])
        drain(vbox, pair_send.at[i])
    drain(in1.at[pl.ds(0, 3)], pool_send.at[0])
    drain(buf2.at[pl.ds(0, 15)], pool_send.at[1])
    drain(pool.at[pl.ds(0, 31)], pool_send.at[2])
    drain(gw_pair, gw_send.at[0])
    drain(gw_buf.at[pl.ds(0, 15)], gw_send.at[1])
    drain(buf_z.at[pl.ds(0, 15)], gw_send.at[2])
    drain(rows.at[0], gw_send.at[3])
    drain(pair_buf.at[0], out_send.at[0])
    drain(out_box.at[pl.ds(0, 31)], out_send.at[1])


def shape(*dims, dtype=BF16):
    return jax.ShapeDtypeStruct(dims, dtype)


def scratch_shapes():
    dma = pltpu.SemaphoreType.DMA

    def half(*dims):
        return pltpu.VMEM(dims, BF16)

    def single(*dims):
        return pltpu.VMEM(dims, F32)

    return [
        half(12, 3 * D), half(12, D), single(D), single(D), single(64, D),
        pltpu.VMEM((64,), jnp.int32), half(D, D), half(D, D),
        half(32, 8, D), half(32, 8, D), half(4, 32, D), half(4, 32, D),
        half(2, 4, 32, D), half(2, 4, 32, D), half(16, 16, 384), half(2, 4, 2, 2, 2, 2, 48, 384),
        half(256, D), half(256, 3 * D), single(12, 256, 128), half(256, D), single(8, D),
        single(4, 2, D), single(4, 2, D), single(16, 2, D), single(32, 2, D),
        single(64, D), single(64, D), single(64, D), single(256, D),
        half(256, D), half(256, 3 * D), half(2, 4, 32, D),
        half(2, 16, 48, 384), half(16, 48, 384), half(16, 48, 384), half(16, 48, 384),
        single(16, 4, 384), single(16, 4, 384), single(2, 4, 384),
        half(2, 4, 32, D), half(32, 8, D),
        dma((6,)), dma((3,)), dma((2,)), dma((2,)), dma((2,)), dma((2,)),
        dma((4,)), dma((2,)), dma((2, 2)), dma((2, 2, 2)), dma((2, 2, 2)), dma((2,)),
        dma((3,)), dma((3,)), dma((4,)), dma((4,)), dma((2,)), dma((2,)), dma,
    ]


def per_device(video, upstream, standardize_scale, ln_bias, w_qkv, w_out, windows, positives):
    anywhere, vmem = pl.BlockSpec(memory_space=pl.ANY), pl.BlockSpec(memory_space=pltpu.VMEM)
    grad_video, grad_out_weight, pooled, loss = pl.pallas_call(
        kernel,
        out_shape=[
            shape(32, 8, D), shape(1, 1152, dtype=F32), shape(64, D, dtype=F32),
            shape(1, 1, dtype=F32),
        ],
        in_specs=[anywhere] * 8,
        out_specs=[anywhere, vmem, anywhere, vmem],
        scratch_shapes=scratch_shapes(),
        compiler_params=pltpu.CompilerParams(
            vmem_limit_bytes=VMEM_LIMIT, collective_id=1, has_side_effects=True
        ),
    )(
        video.reshape(32, 8, D), upstream.reshape(32, 8, D), w_qkv, w_out,
        standardize_scale, ln_bias, windows, positives,
    )
    return grad_video.reshape(1, 1, 256, D), grad_out_weight, pooled, loss.reshape(())


def solution(mesh):
    in_specs = (
        P("dp", "seq", None, None),
        P("dp", "seq", None, None),
        P(),
        P(),
        P("seq", None),
        P("seq", None),
        P(),
        P(),
    )
    out_specs = (P("dp", "seq", None, None), P(("dp", "seq"), None), P(), P())
    return jax.shard_map(
        per_device, mesh=mesh, in_specs=in_specs, out_specs=out_specs, check_vma=False
    )
```

```python
import jax
import jax.numpy as jnp
from jax import lax
from jax.experimental import pallas as pl
from jax.experimental.pallas import tpu as pltpu
from jax.sharding import PartitionSpec as P

MESH = pl.DeviceIdType.MESH
F32 = jnp.float32
BF16 = jnp.bfloat16
D = 768
EPS = 1e-6
NEG = -1e30
SHARP = 1.0 / 0.07
VMEM_LIMIT = 56 * 1024 * 1024


class Place:
    def __init__(self):
        self.dp = lax.axis_index("dp")
        self.seq = lax.axis_index("seq")
        self.x_hi = self.dp // 4
        self.y = self.dp % 4
        self.z = self.seq // 4
        self.role = self.seq % 4
        self.x_lo = self.role // 2
        self.core = self.seq % 2
        self.k = self.seq // 2
        self.x = self.x_hi * 2 + self.x_lo
        self.m = self.dp * 4 + self.role


def send(src, dst, send_sem, recv_sem, dp, seq):
    pltpu.make_async_remote_copy(
        src_ref=src,
        dst_ref=dst,
        send_sem=send_sem,
        recv_sem=recv_sem,
        device_id=(dp, seq),
        device_id_type=MESH,
    ).start()


def wrap(a, n):
    return jnp.where(a >= n, a - n, a)


def drain(ref, sem):
    pltpu.make_async_copy(ref, ref, sem).wait()


def announce(me):
    sem = pltpu.get_barrier_semaphore()

    def slab(i, carry):
        to = wrap(me.k + i, 32) * 2 + me.core
        pl.semaphore_signal(sem, inc=1, device_id=(me.dp, to), device_id_type=MESH)
        return carry

    def plane(i, carry):
        dp = wrap(me.dp + i, 8)
        for role in range(4):
            pl.semaphore_signal(sem, inc=1, device_id=(dp, me.z * 4 + role), device_id_type=MESH)
        return carry

    lax.fori_loop(1, 32, slab, 0)
    lax.fori_loop(1, 8, plane, 0)
    for i in range(1, 4):
        to = me.z * 4 + wrap(me.role + i, 4)
        pl.semaphore_signal(sem, inc=1, device_id=(me.dp, to), device_id_type=MESH)


def arrive():
    pl.semaphore_wait(pltpu.get_barrier_semaphore(), 62)


def dot(a, b):
    return lax.dot_general(a, b, (((1,), (0,)), ((), ())), preferred_element_type=F32)


def dot_nt(a, b):
    return lax.dot_general(a, b, (((1,), (1,)), ((), ())), preferred_element_type=F32)


def dot_tn(a, b):
    return lax.dot_general(a, b, (((0,), (0,)), ((), ())), preferred_element_type=F32)


def iota(shape, dim):
    return lax.broadcasted_iota(jnp.int32, shape, dim)


def one_hot(condition):
    return jnp.where(condition, 1.0, 0.0).astype(BF16)


def gather_order(me):
    j = iota((1, D), 1)
    block, rest = j // 96, j % 96
    core, chunk, x_lo = block // 4, (block // 2) % 2, block % 2
    z8, r = rest // 12, rest % 12
    near = jnp.where(z8 < 5, z8, z8 + 8)
    from_z = (me.z + jnp.where(chunk == 0, near, z8 + 5)) % 16
    natural = (from_z * 4 + x_lo * 2 + core) * 12 + r
    return one_hot(iota((D, D), 0) == natural)


def scatter_order():
    j = iota((1, D), 1)
    dp, rest = j // 96, j % 96
    x_lo, z, r = rest // 48, (rest % 48) // 3, rest % 3
    natural = dp * 96 + z * 6 + x_lo * 3 + r
    return one_hot(iota((D, D), 0) == natural)


def split3(a):
    high = a.astype(BF16)
    rest = a - high.astype(F32)
    mid = rest.astype(BF16)
    low = (rest - mid.astype(F32)).astype(BF16)
    return jnp.concatenate([high.astype(F32), mid.astype(F32), low.astype(F32)], 0).astype(BF16)


def start_tokens(me, src, buf, local_sem, send_sem, recv_sem, far=16, near=1):
    def one(to):
        send(src.at[to], buf.at[me.k], send_sem, recv_sem, me.dp, to * 2 + me.core)

    def step(i, carry):
        one(wrap(me.k + 16 - i, 32))
        one(wrap(me.k + 16 + i, 32))
        return carry

    if far == 16:
        pltpu.make_async_copy(src.at[me.k], buf.at[me.k], local_sem).start()
        one(wrap(me.k + 16, 32))
    lax.fori_loop(max(16 - far, 1), 17 - near, step, 0)


def wait_tokens(me, src, buf, local_sem, recv_sem):
    pltpu.make_async_copy(src.at[me.k], buf.at[me.k], local_sem).wait()
    drain(buf.at[pl.ds(0, 31)], recv_sem)


def start_pair(me, buf, out, box, send_sem, recv_sem):
    rows = buf[...].astype(F32).reshape(256, D).astype(BF16)
    r, col = iota((128, 1), 0), iota((128, 256), 1)
    at = (r % 32) * 8 + r // 32
    theirs = dot(one_hot(col == at + 4 * (1 - me.core)), rows)
    box[...] = theirs.astype(BF16).reshape(4, 32, D)
    send(box, out.at[me.core], send_sem, recv_sem, me.dp, me.seq + 1 - 2 * me.core)
    mine = dot(one_hot(col == at + 4 * me.core), rows)
    out[me.core] = mine.astype(BF16).reshape(4, 32, D)


OFFSETS = (0, 1, 2, 3, 4, 13, 14, 15, 5, 6, 7, 8, 9, 10, 11, 12)


def start_weights(me, zbuf, send_sem, recv_z):
    for d in (12, 13, 3, 14, 2, 15, 1, 8, 7, 9, 6, 10, 5, 11, 4):
        j = OFFSETS.index(16 - d)
        to = wrap(me.z + d, 16) * 4 + me.role
        send(zbuf.at[0], zbuf.at[j], send_sem, recv_z.at[j // 8], me.dp, to)


def x_device(me, x):
    return (x // 2) * 4 + me.y, me.z * 4 + (x % 2) * 2 + me.core


def spread_first(me, zbuf, full, chunk, recv_z, send_sem, recv):
    drain(zbuf.at[pl.ds(0, 7 + chunk)], recv_z.at[chunk])
    r = iota((96, 1), 0)
    pick = one_hot(iota((96, 128), 1) == (r // 12) * 16 + r % 12)
    rows = zbuf[chunk * 8 : chunk * 8 + 8].reshape(128, 384)
    block = dot(pick, rows).astype(BF16)
    full[me.x_hi, me.y, me.core, chunk, me.x_lo] = block.reshape(2, 48, 384)
    a = full.at[me.x_hi, me.y, me.core, chunk, me.x_lo, 0]
    b = full.at[me.x_hi, me.y, me.core, chunk, me.x_lo, 1]
    for i in (2, 1, 3):
        send(a, a, send_sem, recv.at[chunk, 0], *x_device(me, wrap(me.x + i, 4)))
        send(b, b, send_sem, recv.at[chunk, 1], me.x_hi * 4 + wrap(me.y + i, 4), me.seq)


def spread_second(me, full, chunk, recv_first, send_sem, recv, send_pair, recv_pair, to=(1, 3)):
    pair = me.seq + 1 - 2 * me.core
    drain(full.at[0, pl.ds(0, 3), 0, 0, 0, 0], recv_first.at[chunk, 0])
    a = full.at[:, me.y, me.core, chunk, :, 0]
    for i in to:
        send(a, a, send_sem, recv.at[chunk, 0, i - 1], me.x_hi * 4 + wrap(me.y + i, 4), me.seq)
    drain(full.at[0, pl.ds(0, 3), 0, 0, 0, 0], recv_first.at[chunk, 1])
    b = full.at[me.x_hi, :, me.core, chunk, me.x_lo, 1]
    for i in to:
        send(b, b, send_sem, recv.at[chunk, 1, i - 1], *x_device(me, wrap(me.x + i, 4)))
    send(a, a, send_pair, recv_pair, me.dp, pair)
    send(b, b, send_pair, recv_pair, me.dp, pair)


def spread_third(me, full, chunk, recv_second, send_sem, recv, send_pair, recv_pair):
    pair = me.seq + 1 - 2 * me.core
    for n, (i, o) in enumerate(((3, 1), (1, 3))):
        y, x = wrap(me.y + i, 4), wrap(me.x + i, 4)
        a = full.at[:, y, me.core, chunk, :, 0]
        drain(a, recv_second.at[chunk, 0, 2 * n])
        half = full.at[n, y, me.core, chunk, :, 0]
        send(half, half, send_sem, recv.at[chunk, 0, n], me.x_hi * 4 + wrap(me.y + o, 4), me.seq)
        b = full.at[x // 2, :, me.core, chunk, x % 2, 1]
        drain(b, recv_second.at[chunk, 1, 2 * n])
        half = full.at[x // 2, pl.ds(2 * n, 2), me.core, chunk, x % 2, 1]
        send(half, half, send_sem, recv.at[chunk, 1, n], *x_device(me, wrap(me.x + o, 4)))
        send(a, a, send_pair, recv_pair, me.dp, pair)
        send(b, b, send_pair, recv_pair, me.dp, pair)


def spread_last(me, full, chunk, recv_third, send_pair, recv_pair):
    pair = me.seq + 1 - 2 * me.core
    y, x = wrap(me.y + 2, 4), wrap(me.x + 2, 4)
    for n in range(2):
        a = full.at[n, y, me.core, chunk, :, 0]
        drain(a, recv_third.at[chunk, 0, n])
        send(a, a, send_pair, recv_pair, me.dp, pair)
        b = full.at[x // 2, pl.ds(2 * n, 2), me.core, chunk, x % 2, 1]
        drain(b, recv_third.at[chunk, 1, n])
        send(b, b, send_pair, recv_pair, me.dp, pair)


def spread_direct(me, full, chunk, recv_second, send_pair, recv_pair):
    pair = me.seq + 1 - 2 * me.core
    for i in (1, 3, 2):
        a = full.at[:, wrap(me.y + 4 - i, 4), me.core, chunk, :, 0]
        drain(a, recv_second.at[chunk, 0, i - 1])
        send(a, a, send_pair, recv_pair, me.dp, pair)
        x = wrap(me.x + 4 - i, 4)
        b = full.at[x // 2, :, me.core, chunk, x % 2, 1]
        drain(b, recv_second.at[chunk, 1, i - 1])
        send(b, b, send_pair, recv_pair, me.dp, pair)


def start_pooled(me, part, box1, in1, send_sem, recv_sem):
    for q in range(4):
        box1[q] = part[2 * q : 2 * q + 2, :]
    in1[me.role] = box1[me.role]
    for i in range(1, 4):
        to = wrap(me.role + i, 4)
        send(box1.at[to], in1.at[me.role], send_sem, recv_sem, me.dp, me.z * 4 + to)


def pooled_along_z(me, in1, recv_first, buf2, send_sem, recv_sem):
    drain(in1.at[pl.ds(0, 3)], recv_first)
    buf2[me.z] = jnp.sum(in1[...], 0)

    for i in (8, 9, 7, 10, 6, 11, 5, 12, 4, 13, 3, 14, 2, 15, 1):
        to = wrap(me.z + i, 16) * 4 + me.role
        send(buf2.at[me.z], buf2.at[me.z], send_sem, recv_sem, me.dp, to)


def pooled_in_plane(me, buf2, recv_second, pool, send_sem, recv_sem):
    drain(buf2.at[pl.ds(0, 15)], recv_second)
    pool[me.m] = jnp.sum(buf2[...], 0) * (1.0 / 2048.0)

    mine = pool.at[me.m]

    def step(i, carry):
        dp = wrap(me.dp + i, 8)
        for role in range(4):
            send(mine, mine, send_sem, recv_sem, dp, me.z * 4 + role)
        return carry

    lax.fori_loop(1, 8, step, 0)
    for i in range(1, 4):
        send(mine, mine, send_sem, recv_sem, me.dp, me.z * 4 + wrap(me.role + i, 4))


def finish_pooled(pool, recv_sem, pooled):
    drain(pool.at[pl.ds(0, 31)], recv_sem)
    for m in range(32):
        pooled[2 * m : 2 * m + 2, :] = pool[m]


def start_weight_sum(me, box, pair_buf, send_sem, recv_sem):
    send(
        box.at[1 - me.core], pair_buf, send_sem, recv_sem, me.dp, me.seq + 1 - 2 * me.core
    )


def plane_weight_sum(me, box, pair_buf, recv_pair, own, buf, send_sem, recv_sem):
    drain(pair_buf, recv_pair)
    own[...] = (box[me.core].astype(F32) + pair_buf[...].astype(F32)).astype(BF16)
    n = me.dp * 2 + me.x_lo
    buf[n] = own[n]

    def step(i, carry):
        dp = wrap(me.dp + i, 8)
        for x_lo in range(2):
            to = me.z * 4 + x_lo * 2 + me.core
            send(own.at[dp * 2 + x_lo], buf.at[n], send_sem, recv_sem, dp, to)
        return carry

    lax.fori_loop(1, 8, step, 0)
    other = 1 - me.x_lo
    to = me.z * 4 + other * 2 + me.core
    send(own.at[me.dp * 2 + other], buf.at[n], send_sem, recv_sem, me.dp, to)


def second_weight_sum(me, buf, recv_sem, box_z, buf_z, send_sem, recv_z):
    drain(buf.at[pl.ds(0, 15)], recv_sem)
    total = lax.fori_loop(
        0, 16, lambda i, t: t + buf[i].astype(F32), jnp.zeros((48, 384), F32)
    )
    for z in range(16):
        for r in range(3):
            box_z[z, :, r * 384 : r * 384 + 384] = total[3 * z + r : 3 * z + r + 1, :]
    buf_z[me.z] = box_z[me.z]
    for i in (8, 9, 7, 10, 6, 11, 5, 12, 4, 13, 3, 14, 2, 15, 1):
        to = wrap(me.z + i, 16)
        send(box_z.at[to], buf_z.at[me.z], send_sem, recv_z, me.dp, to * 4 + me.role)


def third_weight_sum(me, buf_z, recv_z, rows, send_sem, recv_sem):
    drain(buf_z.at[pl.ds(0, 15)], recv_z)
    rows[me.core] = jnp.sum(buf_z[...], 0)
    send(
        rows.at[me.core], rows.at[me.core], send_sem, recv_sem,
        me.dp, me.seq + 1 - 2 * me.core,
    )


def finish_weight_sum(me, rows, recv_sem, out):
    drain(rows.at[0], recv_sem)
    left, right = rows[0], rows[1]
    first = me.core == 0
    out[0:1, 0:384] = jnp.where(first, left[:, 0:384], right[:, 384:768])
    out[0:1, 384:768] = jnp.where(first, right[:, 0:384], left[:, 768:1152])
    out[0:1, 768:1152] = jnp.where(first, left[:, 384:768], right[:, 768:1152])


def start_back_pair(me, grads, buf, send_sem, recv_sem):
    theirs = 1 - me.core
    send(grads.at[theirs], buf.at[me.core], send_sem, recv_sem, me.dp, me.seq + 1 - 2 * me.core)
    buf[me.core] = grads[me.core]


def fill_back(buf, recv_pair, box):
    drain(buf.at[0], recv_pair)
    r = iota((256, 1), 0)
    at = ((r // 4) % 2) * 128 + (r % 4) * 32 + r // 8
    rows = dot(one_hot(iota((256, 256), 1) == at), buf[...].reshape(256, D))
    box[...] = rows.reshape(32, 8, D).astype(BF16)


def normalize(x):
    centered = x - jnp.mean(x, -1, keepdims=True)
    inverse = lax.rsqrt(jnp.mean(centered * centered, -1, keepdims=True) + EPS)
    return centered * inverse, inverse


def exact(a, b, contract):
    return lax.dot_general(
        a, b, (contract, ((), ())), precision=lax.Precision.HIGHEST, preferred_element_type=F32
    )


def window_units(windows, out):
    w = windows[...]
    out[...] = w * lax.rsqrt(jnp.mean(w * w, -1, keepdims=True) + EPS) * D ** (-0.5)


def contrast(pooled, units, positives, loss, grad):
    p, root = pooled[...], D ** (-0.5)
    inverse = lax.rsqrt(jnp.mean(p * p, -1, keepdims=True) + EPS)
    logits = exact(units[...], p * inverse * root, ((1,), (1,))) * SHARP
    matched = iota((64, 64), 0) == positives[...].reshape(1, 64)
    total = -jnp.sum(jnp.where(matched, logits, 0.0))
    slope = jnp.where(matched, -1.0, 0.0)
    for axis in range(2):
        top = jnp.max(logits, axis, keepdims=True)
        weight = jnp.exp(logits - top)
        size = jnp.sum(weight, axis, keepdims=True)
        total = total + 0.5 * jnp.sum(top + jnp.log(size))
        slope = slope + 0.5 * (weight / size)
    loss[...] = jnp.full((1, 1), total * (1.0 / 64.0), F32)
    grad_unit = exact(slope * (SHARP / 64.0), units[...], ((0,), (0,)))
    inner = jnp.mean(grad_unit * p, -1, keepdims=True)
    grad[...] = inverse * root * (grad_unit - p * (inverse * inverse) * inner)


def clip_pick():
    return one_hot((iota((8, 256), 1) % 32) // 4 == iota((8, 256), 0))


def unit_rows(ref, u, columns):
    return jnp.concatenate(
        [ref[u * 64 : u * 64 + 64, columns], ref[128 + u * 64 : 192 + u * 64, columns]], 0
    )


def put_rows(ref, u, columns, value):
    ref[u * 64 : u * 64 + 64, columns] = value[:64]
    ref[128 + u * 64 : 192 + u * 64, columns] = value[64:]


def heads(a):
    even = iota(a.shape, 1) < 64
    zero = jnp.zeros_like(a)
    return jnp.concatenate([jnp.where(even, a, zero), jnp.where(even, zero, a)], 0)


def same_patch():
    return (iota((256, 128), 0) // 32) % 2 == (iota((256, 128), 1) // 32) % 2


def norm_tokens(tokens, scale, bias, order, normed):
    unit, _ = normalize(tokens[...].reshape(256, D).astype(F32))
    rows = (unit * scale[...].reshape(1, D) + bias[...].reshape(1, D)).astype(BF16)
    normed[...] = dot(rows, order[...]).astype(BF16)


def project(normed, full, qkv):
    for n in range(6):
        weight = full[n // 4, n % 4].reshape(D, 384)
        qkv[:, n * 384 : n * 384 + 384] = dot(normed[...], weight).astype(BF16)


def attend(qkv, prob, context):
    keep = same_patch()
    for j in range(6):
        for u in range(2):
            columns = [slice(s * D + j * 128, s * D + j * 128 + 128) for s in range(3)]
            query, key, value = [unit_rows(qkv, u, c) for c in columns]
            score = dot_nt(heads(query), key) * 0.125
            score = jnp.where(keep, score, NEG)
            top = jnp.max(score, -1, keepdims=True)
            weight = jnp.exp(score - top)
            p = weight / jnp.sum(weight, -1, keepdims=True)
            prob[j * 2 + u] = p
            half = p.astype(BF16)
            both = jnp.concatenate([half[:128], half[128:]], 1)
            mixed = dot(both, heads(value)).astype(BF16)
            put_rows(context, u, slice(j * 128, j * 128 + 128), mixed)


def pool_clips(tokens, context, order, full, part):
    pick = clip_pick()
    ctx_sum = split3(dot(pick, context[...]))
    ctx_sum = dot(ctx_sum, order[...]).astype(BF16)
    sums = dot(pick, tokens[...].reshape(256, D))
    for n in range(2):
        weight = full[1, 2 + n].reshape(D, 384)
        s = dot(ctx_sum, weight)
        columns = slice(n * 384, n * 384 + 384)
        part[:, columns] = sums[:, columns] + s[0:8] + s[8:16] + s[16:24]


def spread(upstream, grad_clip):
    pick = one_hot((iota((256, 24), 0) % 32) // 4 == iota((256, 24), 1) % 8)
    return upstream[...].reshape(256, D).astype(F32) + dot(pick, split3(grad_clip))


def project_back(grad_half, full, order, grad_context):
    back = dot_nt(grad_half[:, :384], full[1, 2].reshape(D, 384))
    back = back + dot_nt(grad_half[:, 384:], full[1, 3].reshape(D, 384))
    grad_context[...] = dot_nt(back.astype(BF16), order[...]).astype(BF16)


def weight_term(grad_half, scatter, context, box):
    ordered = dot(context[...], scatter[...]).astype(BF16)
    term = dot_tn(ordered, grad_half).astype(BF16)
    for n in range(16):
        for c in range(2):
            box[c, n] = term[n * 48 : n * 48 + 48, c * 384 : c * 384 + 384]


def backward_attention(pairs, qkv, prob, grad_context, grad_qkv):
    for j in pairs:
        for u in range(2):
            columns = [slice(s * D + j * 128, s * D + j * 128 + 128) for s in range(3)]
            query, key, value = [unit_rows(qkv, u, c) for c in columns]
            grad = heads(unit_rows(grad_context, u, slice(j * 128, j * 128 + 128)))
            p = prob[j * 2 + u]
            half = p.astype(BF16)
            grad_prob = dot_nt(grad, value)
            grad_value = dot_tn(half, grad).astype(BF16)
            row = jnp.sum(p * grad_prob, -1, keepdims=True)
            grad_score = (p * (grad_prob - row) * 0.125).astype(BF16)
            both = jnp.concatenate([grad_score[:128], grad_score[128:]], 1)
            put_rows(grad_qkv, u, columns[0], dot(both, heads(key)).astype(BF16))
            put_rows(grad_qkv, u, columns[1], dot_tn(grad_score, heads(query)).astype(BF16))
            put_rows(grad_qkv, u, columns[2], grad_value)


def backward_tokens(tokens, grad_output, grad_qkv, full, order, scale, out):
    back = jnp.zeros((256, D), F32)
    for n in range(6):
        weight = full[n // 4, n % 4].reshape(D, 384)
        back = back + dot_nt(grad_qkv[:, n * 384 : n * 384 + 384], weight)
    grad_normed = dot_nt(back.astype(BF16), order[...])
    scaled = grad_normed * scale[...].reshape(1, D)
    unit, inverse = normalize(tokens[...].reshape(256, D).astype(F32))
    grad_norm = inverse * (
        scaled
        - jnp.mean(scaled, -1, keepdims=True)
        - unit * jnp.mean(scaled * unit, -1, keepdims=True)
    )
    out[...] = (grad_output + grad_norm).astype(BF16).reshape(2, 4, 32, D)


def kernel(
    video, upstream, w_qkv, w_out, scale_in, bias_in, windows_in, positives_in,
    video_out, weight_out, pooled_out, loss_out,
    wq, wo, scale, bias, windows, positives, order, scatter,
    vbuf, ubuf, vbox, ubox, tokens, ups, zbuf, full, normed, qkv, prob, context, part,
    box1, in1, buf2, pool, pooled, units, grad_pooled, grad_output, grad_context, grad_qkv, grads,
    box, gw_pair, gw_own, gw_buf, box_z, buf_z, rows, pair_buf, out_box,
    load, local, tok_send, tok_recv, pair_send, pair_recv,
    w_send, recv_z, recv_first, recv_second, recv_third, wp_sem,
    pool_send, pool_recv, gw_send, gw_recv, out_send, out_recv, store,
):
    me = Place()
    loads = [(w_qkv, wq), (w_out, wo), (scale_in, scale), (bias_in, bias)]
    loads += [(windows_in, windows), (positives_in, positives)]
    loads = [pltpu.make_async_copy(a, b, load.at[i]) for i, (a, b) in enumerate(loads)]
    for copy in loads:
        copy.start()
    announce(me)
    loads[0].wait()
    loads[1].wait()
    column = pl.multiple_of(lax.rem(me.dp, 6) * 384, 384)
    column_out = pl.multiple_of(lax.rem(me.dp, 2) * 384, 384)
    piece = jnp.where(me.dp < 6, wq[:, pl.ds(column, 384)], wo[:, pl.ds(column_out, 384)])
    zbuf[0] = jnp.concatenate([piece.astype(F32), jnp.zeros((4, 384), F32)], 0).astype(BF16)
    arrive()
    start_weights(me, zbuf, w_send.at[0], recv_z)
    start_tokens(me, video, vbuf, local.at[0], tok_send.at[0], tok_recv.at[0])
    order[...] = gather_order(me)
    scatter[...] = scatter_order()
    for copy in loads[2:]:
        copy.wait()
    window_units(windows, units)
    pair_sems = (wp_sem.at[0], wp_sem.at[1])
    second = (recv_second, *pair_sems)
    third = (w_send.at[3], recv_third, *pair_sems)
    spread_first(me, zbuf, full, 0, recv_z, w_send.at[1], recv_first)
    spread_second(me, full, 0, recv_first, w_send.at[2], *second)
    spread_first(me, zbuf, full, 1, recv_z, w_send.at[1], recv_first)
    spread_third(me, full, 0, recv_second, *third)
    spread_second(me, full, 1, recv_first, w_send.at[4], *second, to=(2, 1, 3))
    start_tokens(me, upstream, ubuf, local.at[1], tok_send.at[1], tok_recv.at[1], 16, 8)
    wait_tokens(me, video, vbuf, local.at[0], tok_recv.at[0])
    start_pair(me, vbuf, tokens, vbox, pair_send.at[0], pair_recv.at[0])
    spread_last(me, full, 0, recv_third, *pair_sems)
    spread_direct(me, full, 1, recv_second, *pair_sems)
    drain(tokens.at[0], pair_recv.at[0])
    norm_tokens(tokens, scale, bias, order, normed)
    drain(full.at[:, :, 0], wp_sem.at[1])
    project(normed, full, qkv)
    attend(qkv, prob, context)
    pool_clips(tokens, context, order, full, part)
    start_pooled(me, part, box1, in1, pool_send.at[0], pool_recv.at[0])
    pooled_along_z(me, in1, pool_recv.at[0], buf2, pool_send.at[1], pool_recv.at[1])
    start_tokens(me, upstream, ubuf, local.at[1], tok_send.at[1], tok_recv.at[1], 7, 1)
    pooled_in_plane(me, buf2, pool_recv.at[1], pool, pool_send.at[2], pool_recv.at[2])
    wait_tokens(me, upstream, ubuf, local.at[1], tok_recv.at[1])
    start_pair(me, ubuf, ups, ubox, pair_send.at[1], pair_recv.at[1])
    finish_pooled(pool, pool_recv.at[2], pooled)
    contrast(pooled, units, positives, loss_out, grad_pooled)
    save = pltpu.make_async_copy(pooled, pooled_out, store)
    save.start()
    drain(ups.at[0], pair_recv.at[1])
    grad_clip = grad_pooled[pl.ds(pl.multiple_of(me.dp * 8, 8), 8), :] * 64.0
    grad_output[...] = spread(ups, grad_clip)
    grad_half = grad_output[...].astype(BF16)
    weight_term(grad_half, scatter, context, box)
    start_weight_sum(me, box, gw_pair, gw_send.at[0], gw_recv.at[0])
    project_back(grad_half, full, order, grad_context)
    backward_attention((0, 1), qkv, prob, grad_context, grad_qkv)
    plane_weight_sum(
        me, box, gw_pair, gw_recv.at[0], gw_own, gw_buf, gw_send.at[1], gw_recv.at[1]
    )
    backward_attention((2, 3, 4, 5), qkv, prob, grad_context, grad_qkv)
    backward_tokens(tokens, grad_output[...], grad_qkv, full, order, scale, grads)
    start_back_pair(me, grads, pair_buf, out_send.at[0], out_recv.at[0])
    fill_back(pair_buf, out_recv.at[0], out_box)
    out_sems = (local.at[2], out_send.at[1], out_recv.at[1])
    start_tokens(me, out_box, video_out, *out_sems, 16, 12)
    second_weight_sum(me, gw_buf, gw_recv.at[1], box_z, buf_z, gw_send.at[2], gw_recv.at[2])
    start_tokens(me, out_box, video_out, *out_sems, 11, 1)
    third_weight_sum(me, buf_z, gw_recv.at[2], rows, gw_send.at[3], gw_recv.at[3])
    finish_weight_sum(me, rows, gw_recv.at[3], weight_out)
    wait_tokens(me, out_box, video_out, local.at[2], out_recv.at[1])
    save.wait()
    drain(zbuf.at[pl.ds(0, 15)], w_send.at[0])
    drain(full.at[0, pl.ds(0, 3), 0, 0], w_send.at[1])
    drain(full.at[0, pl.ds(0, 2), 0], w_send.at[2])
    drain(full.at[0, 0, 0], w_send.at[3])
    drain(full.at[0, pl.ds(0, 3), 0], w_send.at[4])
    drain(full.at[:, :, 0], wp_sem.at[0])
    for i in range(2):
        drain(vbuf.at[pl.ds(0, 31)], tok_send.at[i])
        drain(vbox, pair_send.at[i])
    drain(in1.at[pl.ds(0, 3)], pool_send.at[0])
    drain(buf2.at[pl.ds(0, 15)], pool_send.at[1])
    drain(pool.at[pl.ds(0, 31)], pool_send.at[2])
    drain(gw_pair, gw_send.at[0])
    drain(gw_buf.at[pl.ds(0, 15)], gw_send.at[1])
    drain(buf_z.at[pl.ds(0, 15)], gw_send.at[2])
    drain(rows.at[0], gw_send.at[3])
    drain(pair_buf.at[0], out_send.at[0])
    drain(out_box.at[pl.ds(0, 31)], out_send.at[1])


def shape(*dims, dtype=BF16):
    return jax.ShapeDtypeStruct(dims, dtype)


def scratch_shapes():
    dma = pltpu.SemaphoreType.DMA

    def half(*dims):
        return pltpu.VMEM(dims, BF16)

    def single(*dims):
        return pltpu.VMEM(dims, F32)

    return [
        half(12, 3 * D), half(12, D), single(D), single(D), single(64, D),
        pltpu.VMEM((64,), jnp.int32), half(D, D), half(D, D),
        half(32, 8, D), half(32, 8, D), half(4, 32, D), half(4, 32, D),
        half(2, 4, 32, D), half(2, 4, 32, D), half(16, 16, 384), half(2, 4, 2, 2, 2, 2, 48, 384),
        half(256, D), half(256, 3 * D), single(12, 256, 128), half(256, D), single(8, D),
        single(4, 2, D), single(4, 2, D), single(16, 2, D), single(32, 2, D),
        single(64, D), single(64, D), single(64, D), single(256, D),
        half(256, D), half(256, 3 * D), half(2, 4, 32, D),
        half(2, 16, 48, 384), half(16, 48, 384), half(16, 48, 384), half(16, 48, 384),
        single(16, 1, 1152), single(16, 1, 1152), single(2, 1, 1152),
        half(2, 4, 32, D), half(32, 8, D),
        dma((6,)), dma((3,)), dma((2,)), dma((2,)), dma((2,)), dma((2,)),
        dma((5,)), dma((2,)), dma((2, 2)), dma((2, 2, 3)), dma((2, 2, 2)), dma((2,)),
        dma((3,)), dma((3,)), dma((4,)), dma((4,)), dma((2,)), dma((2,)), dma,
    ]


def per_device(video, upstream, standardize_scale, ln_bias, w_qkv, w_out, windows, positives):
    anywhere, vmem = pl.BlockSpec(memory_space=pl.ANY), pl.BlockSpec(memory_space=pltpu.VMEM)
    grad_video, grad_out_weight, pooled, loss = pl.pallas_call(
        kernel,
        out_shape=[
            shape(32, 8, D), shape(1, 1152, dtype=F32), shape(64, D, dtype=F32),
            shape(1, 1, dtype=F32),
        ],
        in_specs=[anywhere] * 8,
        out_specs=[anywhere, vmem, anywhere, vmem],
        scratch_shapes=scratch_shapes(),
        compiler_params=pltpu.CompilerParams(
            vmem_limit_bytes=VMEM_LIMIT, collective_id=1, has_side_effects=True
        ),
    )(
        video.reshape(32, 8, D), upstream.reshape(32, 8, D), w_qkv, w_out,
        standardize_scale, ln_bias, windows, positives,
    )
    return grad_video.reshape(1, 1, 256, D), grad_out_weight, pooled, loss.reshape(())


def solution(mesh):
    in_specs = (
        P("dp", "seq", None, None),
        P("dp", "seq", None, None),
        P(),
        P(),
        P("seq", None),
        P("seq", None),
        P(),
        P(),
    )
    out_specs = (P("dp", "seq", None, None), P(("dp", "seq"), None), P(), P())
    return jax.shard_map(
        per_device, mesh=mesh, in_specs=in_specs, out_specs=out_specs, check_vma=False
    )
```

```python
import jax
import jax.numpy as jnp
from jax import lax
from jax.experimental import pallas as pl
from jax.experimental.pallas import tpu as pltpu
from jax.sharding import PartitionSpec as P

MESH = pl.DeviceIdType.MESH
F32 = jnp.float32
BF16 = jnp.bfloat16
D = 768
EPS = 1e-6
NEG = -1e30
SHARP = 1.0 / 0.07
VMEM_LIMIT = 56 * 1024 * 1024


class Place:
    def __init__(self):
        self.dp = lax.axis_index("dp")
        self.seq = lax.axis_index("seq")
        self.x_hi = self.dp // 4
        self.y = self.dp % 4
        self.z = self.seq // 4
        self.role = self.seq % 4
        self.x_lo = self.role // 2
        self.core = self.seq % 2
        self.k = self.seq // 2
        self.x = self.x_hi * 2 + self.x_lo
        self.m = self.dp * 4 + self.role


def send(src, dst, send_sem, recv_sem, dp, seq):
    pltpu.make_async_remote_copy(
        src_ref=src,
        dst_ref=dst,
        send_sem=send_sem,
        recv_sem=recv_sem,
        device_id=(dp, seq),
        device_id_type=MESH,
    ).start()


def wrap(a, n):
    return jnp.where(a >= n, a - n, a)


def drain(ref, sem):
    pltpu.make_async_copy(ref, ref, sem).wait()


def announce(me):
    sem = pltpu.get_barrier_semaphore()

    def slab(i, carry):
        to = wrap(me.k + i, 32) * 2 + me.core
        pl.semaphore_signal(sem, inc=1, device_id=(me.dp, to), device_id_type=MESH)
        return carry

    def plane(i, carry):
        dp = wrap(me.dp + i, 8)
        for role in range(4):
            pl.semaphore_signal(sem, inc=1, device_id=(dp, me.z * 4 + role), device_id_type=MESH)
        return carry

    lax.fori_loop(1, 32, slab, 0)
    lax.fori_loop(1, 8, plane, 0)
    for i in range(1, 4):
        to = me.z * 4 + wrap(me.role + i, 4)
        pl.semaphore_signal(sem, inc=1, device_id=(me.dp, to), device_id_type=MESH)


def arrive():
    pl.semaphore_wait(pltpu.get_barrier_semaphore(), 62)


def dot(a, b):
    return lax.dot_general(a, b, (((1,), (0,)), ((), ())), preferred_element_type=F32)


def dot_nt(a, b):
    return lax.dot_general(a, b, (((1,), (1,)), ((), ())), preferred_element_type=F32)


def dot_tn(a, b):
    return lax.dot_general(a, b, (((0,), (0,)), ((), ())), preferred_element_type=F32)


def iota(shape, dim):
    return lax.broadcasted_iota(jnp.int32, shape, dim)


def one_hot(condition):
    return jnp.where(condition, 1.0, 0.0).astype(BF16)


def gather_order(me):
    j = iota((1, D), 1)
    block, rest = j // 96, j % 96
    core, chunk, x_lo = block // 4, (block // 2) % 2, block % 2
    z8, r = rest // 12, rest % 12
    near = jnp.where(z8 < 5, z8, z8 + 8)
    from_z = (me.z + jnp.where(chunk == 0, near, z8 + 5)) % 16
    natural = (from_z * 4 + x_lo * 2 + core) * 12 + r
    return one_hot(iota((D, D), 0) == natural)


def scatter_order():
    j = iota((1, D), 1)
    dp, rest = j // 96, j % 96
    x_lo, z, r = rest // 48, (rest % 48) // 3, rest % 3
    natural = dp * 96 + z * 6 + x_lo * 3 + r
    return one_hot(iota((D, D), 0) == natural)


def split3(a):
    high = a.astype(BF16)
    rest = a - high.astype(F32)
    mid = rest.astype(BF16)
    low = (rest - mid.astype(F32)).astype(BF16)
    return jnp.concatenate([high.astype(F32), mid.astype(F32), low.astype(F32)], 0).astype(BF16)


def start_tokens(me, src, buf, local_sem, send_sem, recv_sem, far=16, near=1):
    def one(to):
        send(src.at[to], buf.at[me.k], send_sem, recv_sem, me.dp, to * 2 + me.core)

    def step(i, carry):
        one(wrap(me.k + 16 - i, 32))
        one(wrap(me.k + 16 + i, 32))
        return carry

    if far == 16:
        pltpu.make_async_copy(src.at[me.k], buf.at[me.k], local_sem).start()
        one(wrap(me.k + 16, 32))
    lax.fori_loop(max(16 - far, 1), 17 - near, step, 0)


def wait_tokens(me, src, buf, local_sem, recv_sem):
    pltpu.make_async_copy(src.at[me.k], buf.at[me.k], local_sem).wait()
    drain(buf.at[pl.ds(0, 31)], recv_sem)


def start_pair(me, buf, out, box, send_sem, recv_sem):
    rows = buf[...].astype(F32).reshape(256, D).astype(BF16)
    r, col = iota((128, 1), 0), iota((128, 256), 1)
    at = (r % 32) * 8 + r // 32
    theirs = dot(one_hot(col == at + 4 * (1 - me.core)), rows)
    box[...] = theirs.astype(BF16).reshape(4, 32, D)
    send(box, out.at[me.core], send_sem, recv_sem, me.dp, me.seq + 1 - 2 * me.core)
    mine = dot(one_hot(col == at + 4 * me.core), rows)
    out[me.core] = mine.astype(BF16).reshape(4, 32, D)


OFFSETS = (0, 1, 2, 3, 4, 13, 14, 15, 5, 6, 7, 8, 9, 10, 11, 12)


def start_weights(me, zbuf, send_sem, recv_z):
    for d in (12, 13, 3, 14, 2, 15, 1, 8, 7, 9, 6, 10, 5, 11, 4):
        j = OFFSETS.index(16 - d)
        to = wrap(me.z + d, 16) * 4 + me.role
        send(zbuf.at[0], zbuf.at[j], send_sem, recv_z.at[j // 8], me.dp, to)


def x_device(me, x):
    return (x // 2) * 4 + me.y, me.z * 4 + (x % 2) * 2 + me.core


def spread_first(me, zbuf, full, chunk, recv_z, send_sem, recv):
    drain(zbuf.at[pl.ds(0, 7 + chunk)], recv_z.at[chunk])
    r = iota((96, 1), 0)
    pick = one_hot(iota((96, 128), 1) == (r // 12) * 16 + r % 12)
    rows = zbuf[chunk * 8 : chunk * 8 + 8].reshape(128, 384)
    block = dot(pick, rows).astype(BF16)
    full[me.x_hi, me.y, me.core, chunk, me.x_lo] = block.reshape(2, 48, 384)
    a = full.at[me.x_hi, me.y, me.core, chunk, me.x_lo, 0]
    b = full.at[me.x_hi, me.y, me.core, chunk, me.x_lo, 1]
    for i in (2, 1, 3):
        send(a, a, send_sem, recv.at[chunk, 0], *x_device(me, wrap(me.x + i, 4)))
        send(b, b, send_sem, recv.at[chunk, 1], me.x_hi * 4 + wrap(me.y + i, 4), me.seq)


def spread_second(me, full, chunk, recv_first, send_sem, recv, send_pair, recv_pair, to=(1, 3)):
    pair = me.seq + 1 - 2 * me.core
    drain(full.at[0, pl.ds(0, 3), 0, 0, 0, 0], recv_first.at[chunk, 0])
    a = full.at[:, me.y, me.core, chunk, :, 0]
    for i in to:
        send(a, a, send_sem, recv.at[chunk, 0, i - 1], me.x_hi * 4 + wrap(me.y + i, 4), me.seq)
    drain(full.at[0, pl.ds(0, 3), 0, 0, 0, 0], recv_first.at[chunk, 1])
    b = full.at[me.x_hi, :, me.core, chunk, me.x_lo, 1]
    for i in to:
        send(b, b, send_sem, recv.at[chunk, 1, i - 1], *x_device(me, wrap(me.x + i, 4)))
    send(a, a, send_pair, recv_pair, me.dp, pair)
    send(b, b, send_pair, recv_pair, me.dp, pair)


def spread_third(me, full, chunk, recv_second, send_sem, recv, send_pair, recv_pair):
    pair = me.seq + 1 - 2 * me.core
    for n, (i, o) in enumerate(((3, 1), (1, 3))):
        y, x = wrap(me.y + i, 4), wrap(me.x + i, 4)
        a = full.at[:, y, me.core, chunk, :, 0]
        drain(a, recv_second.at[chunk, 0, 2 * n])
        half = full.at[n, y, me.core, chunk, :, 0]
        send(half, half, send_sem, recv.at[chunk, 0, n], me.x_hi * 4 + wrap(me.y + o, 4), me.seq)
        b = full.at[x // 2, :, me.core, chunk, x % 2, 1]
        drain(b, recv_second.at[chunk, 1, 2 * n])
        half = full.at[x // 2, pl.ds(2 * n, 2), me.core, chunk, x % 2, 1]
        send(half, half, send_sem, recv.at[chunk, 1, n], *x_device(me, wrap(me.x + o, 4)))
        send(a, a, send_pair, recv_pair, me.dp, pair)
        send(b, b, send_pair, recv_pair, me.dp, pair)


def spread_last(me, full, chunk, recv_third, send_pair, recv_pair):
    pair = me.seq + 1 - 2 * me.core
    y, x = wrap(me.y + 2, 4), wrap(me.x + 2, 4)
    for n in range(2):
        a = full.at[n, y, me.core, chunk, :, 0]
        drain(a, recv_third.at[chunk, 0, n])
        send(a, a, send_pair, recv_pair, me.dp, pair)
        b = full.at[x // 2, pl.ds(2 * n, 2), me.core, chunk, x % 2, 1]
        drain(b, recv_third.at[chunk, 1, n])
        send(b, b, send_pair, recv_pair, me.dp, pair)


def spread_direct(me, full, chunk, recv_second, send_pair, recv_pair):
    pair = me.seq + 1 - 2 * me.core
    for i in (1, 3, 2):
        a = full.at[:, wrap(me.y + 4 - i, 4), me.core, chunk, :, 0]
        drain(a, recv_second.at[chunk, 0, i - 1])
        send(a, a, send_pair, recv_pair, me.dp, pair)
        x = wrap(me.x + 4 - i, 4)
        b = full.at[x // 2, :, me.core, chunk, x % 2, 1]
        drain(b, recv_second.at[chunk, 1, i - 1])
        send(b, b, send_pair, recv_pair, me.dp, pair)


def start_pooled(me, part, box1, in1, send_sem, recv_sem):
    for q in range(4):
        box1[q] = part[2 * q : 2 * q + 2, :]
    in1[me.role] = box1[me.role]
    for i in range(1, 4):
        to = wrap(me.role + i, 4)
        send(box1.at[to], in1.at[me.role], send_sem, recv_sem, me.dp, me.z * 4 + to)


def pooled_along_z(me, in1, recv_first, buf2, send_sem, recv_sem):
    drain(in1.at[pl.ds(0, 3)], recv_first)
    buf2[me.z] = jnp.sum(in1[...], 0)

    for i in (8, 9, 7, 10, 6, 11, 5, 12, 4, 13, 3, 14, 2, 15, 1):
        to = wrap(me.z + i, 16) * 4 + me.role
        send(buf2.at[me.z], buf2.at[me.z], send_sem, recv_sem, me.dp, to)


def pooled_in_plane(me, buf2, recv_second, pool, send_sem, recv_sem):
    drain(buf2.at[pl.ds(0, 15)], recv_second)
    pool[me.m] = jnp.sum(buf2[...], 0) * (1.0 / 2048.0)

    mine = pool.at[me.m]

    def step(i, carry):
        dp = wrap(me.dp + i, 8)
        for role in range(4):
            send(mine, mine, send_sem, recv_sem, dp, me.z * 4 + role)
        return carry

    lax.fori_loop(1, 8, step, 0)
    for i in range(1, 4):
        send(mine, mine, send_sem, recv_sem, me.dp, me.z * 4 + wrap(me.role + i, 4))


def finish_pooled(pool, recv_sem, pooled):
    drain(pool.at[pl.ds(0, 31)], recv_sem)
    for m in range(32):
        pooled[2 * m : 2 * m + 2, :] = pool[m]


def start_weight_sum(me, box, pair_buf, send_sem, recv_sem):
    send(
        box.at[1 - me.core], pair_buf, send_sem, recv_sem, me.dp, me.seq + 1 - 2 * me.core
    )


def plane_weight_sum(me, box, pair_buf, recv_pair, own, buf, send_sem, recv_sem):
    drain(pair_buf, recv_pair)
    own[...] = (box[me.core].astype(F32) + pair_buf[...].astype(F32)).astype(BF16)
    n = me.dp * 2 + me.x_lo
    buf[n] = own[n]

    def step(i, carry):
        dp = wrap(me.dp + i, 8)
        for x_lo in range(2):
            to = me.z * 4 + x_lo * 2 + me.core
            send(own.at[dp * 2 + x_lo], buf.at[n], send_sem, recv_sem, dp, to)
        return carry

    lax.fori_loop(1, 8, step, 0)
    other = 1 - me.x_lo
    to = me.z * 4 + other * 2 + me.core
    send(own.at[me.dp * 2 + other], buf.at[n], send_sem, recv_sem, me.dp, to)


def second_weight_sum(me, buf, recv_sem, wide, box_z, buf_z, send_sem, recv_z):
    drain(buf.at[pl.ds(0, 15)], recv_sem)
    total = lax.fori_loop(
        0, 16, lambda i, t: t + buf[i].astype(F32), jnp.zeros((48, 384), F32)
    )
    wide[...] = jnp.zeros_like(wide)
    for z in range(16):
        for r in range(3):
            row = total[3 * z + r : 3 * z + r + 1, :]
            for n in range(3):
                wide[z, r * 3 + n : r * 3 + n + 1, :] = row[:, n * 128 : n * 128 + 128]
    box_z[...] = wide[...].astype(BF16)
    buf_z[me.z] = box_z[me.z]
    for i in (8, 9, 7, 10, 6, 11, 5, 12, 4, 13, 3, 14, 2, 15, 1):
        to = wrap(me.z + i, 16)
        send(box_z.at[to], buf_z.at[me.z], send_sem, recv_z, me.dp, to * 4 + me.role)


def third_weight_sum(me, buf_z, recv_z, rows, send_sem, recv_sem):
    drain(buf_z.at[pl.ds(0, 15)], recv_z)
    rows[me.core] = jnp.sum(buf_z[...].astype(F32), 0)
    send(
        rows.at[me.core], rows.at[me.core], send_sem, recv_sem,
        me.dp, me.seq + 1 - 2 * me.core,
    )


def finish_weight_sum(me, rows, recv_sem, out):
    drain(rows.at[0], recv_sem)
    halves = (rows[0], rows[1])
    first = me.core == 0

    def part(source, row, n):
        at = row * 3 + n
        return halves[source][at : at + 1]

    for n in range(3):
        at = n * 128
        out[0:1, at : at + 128] = jnp.where(first, part(0, 0, n), part(1, 1, n))
        out[0:1, 384 + at : 512 + at] = jnp.where(first, part(1, 0, n), part(0, 2, n))
        out[0:1, 768 + at : 896 + at] = jnp.where(first, part(0, 1, n), part(1, 2, n))


def start_back_pair(me, grads, buf, send_sem, recv_sem):
    theirs = 1 - me.core
    send(grads.at[theirs], buf.at[me.core], send_sem, recv_sem, me.dp, me.seq + 1 - 2 * me.core)
    buf[me.core] = grads[me.core]


def fill_back(buf, recv_pair, box):
    drain(buf.at[0], recv_pair)
    r = iota((256, 1), 0)
    at = ((r // 4) % 2) * 128 + (r % 4) * 32 + r // 8
    rows = dot(one_hot(iota((256, 256), 1) == at), buf[...].reshape(256, D))
    box[...] = rows.reshape(32, 8, D).astype(BF16)


def normalize(x):
    centered = x - jnp.mean(x, -1, keepdims=True)
    inverse = lax.rsqrt(jnp.mean(centered * centered, -1, keepdims=True) + EPS)
    return centered * inverse, inverse


def exact(a, b, contract):
    return lax.dot_general(
        a, b, (contract, ((), ())), precision=lax.Precision.HIGHEST, preferred_element_type=F32
    )


def window_units(windows, out):
    w = windows[...]
    out[...] = w * lax.rsqrt(jnp.mean(w * w, -1, keepdims=True) + EPS) * D ** (-0.5)


def contrast(pooled, units, positives, loss, grad):
    p, root = pooled[...], D ** (-0.5)
    inverse = lax.rsqrt(jnp.mean(p * p, -1, keepdims=True) + EPS)
    logits = exact(units[...], p * inverse * root, ((1,), (1,))) * SHARP
    matched = iota((64, 64), 0) == positives[...].reshape(1, 64)
    total = -jnp.sum(jnp.where(matched, logits, 0.0))
    slope = jnp.where(matched, -1.0, 0.0)
    for axis in range(2):
        top = jnp.max(logits, axis, keepdims=True)
        weight = jnp.exp(logits - top)
        size = jnp.sum(weight, axis, keepdims=True)
        total = total + 0.5 * jnp.sum(top + jnp.log(size))
        slope = slope + 0.5 * (weight / size)
    loss[...] = jnp.full((1, 1), total * (1.0 / 64.0), F32)
    grad_unit = exact(slope * (SHARP / 64.0), units[...], ((0,), (0,)))
    inner = jnp.mean(grad_unit * p, -1, keepdims=True)
    grad[...] = inverse * root * (grad_unit - p * (inverse * inverse) * inner)


def clip_pick():
    return one_hot((iota((8, 256), 1) % 32) // 4 == iota((8, 256), 0))


def unit_rows(ref, u, columns):
    return jnp.concatenate(
        [ref[u * 64 : u * 64 + 64, columns], ref[128 + u * 64 : 192 + u * 64, columns]], 0
    )


def put_rows(ref, u, columns, value):
    ref[u * 64 : u * 64 + 64, columns] = value[:64]
    ref[128 + u * 64 : 192 + u * 64, columns] = value[64:]


def heads(a):
    even = iota(a.shape, 1) < 64
    zero = jnp.zeros_like(a)
    return jnp.concatenate([jnp.where(even, a, zero), jnp.where(even, zero, a)], 0)


def same_patch():
    return (iota((256, 128), 0) // 32) % 2 == (iota((256, 128), 1) // 32) % 2


def norm_tokens(tokens, scale, bias, order, units, inverses, normed):
    unit, inverse = normalize(tokens[...].reshape(256, D).astype(F32))
    units[...] = unit
    inverses[...] = inverse
    rows = (unit * scale[...].reshape(1, D) + bias[...].reshape(1, D)).astype(BF16)
    normed[...] = dot(rows, order[...]).astype(BF16)


def project(normed, full, qkv):
    for n in range(6):
        weight = full[n // 4, n % 4].reshape(D, 384)
        qkv[:, n * 384 : n * 384 + 384] = dot(normed[...], weight).astype(BF16)


def attend(qkv, prob, context):
    keep = same_patch()
    for j in range(6):
        for u in range(2):
            columns = [slice(s * D + j * 128, s * D + j * 128 + 128) for s in range(3)]
            query, key, value = [unit_rows(qkv, u, c) for c in columns]
            score = dot_nt(heads(query), key) * 0.125
            score = jnp.where(keep, score, NEG)
            top = jnp.max(score, -1, keepdims=True)
            weight = jnp.exp(score - top)
            p = weight / jnp.sum(weight, -1, keepdims=True)
            prob[j * 2 + u] = p
            half = p.astype(BF16)
            both = jnp.concatenate([half[:128], half[128:]], 1)
            mixed = dot(both, heads(value)).astype(BF16)
            put_rows(context, u, slice(j * 128, j * 128 + 128), mixed)


def pool_clips(tokens, context, order, full, part):
    pick = clip_pick()
    ctx_sum = split3(dot(pick, context[...]))
    ctx_sum = dot(ctx_sum, order[...]).astype(BF16)
    sums = dot(pick, tokens[...].reshape(256, D))
    for n in range(2):
        weight = full[1, 2 + n].reshape(D, 384)
        s = dot(ctx_sum, weight)
        columns = slice(n * 384, n * 384 + 384)
        part[:, columns] = sums[:, columns] + s[0:8] + s[8:16] + s[16:24]


def spread(upstream, grad_clip):
    pick = one_hot((iota((256, 24), 0) % 32) // 4 == iota((256, 24), 1) % 8)
    return upstream[...].reshape(256, D).astype(F32) + dot(pick, split3(grad_clip))


def project_back(grad_half, full, order, grad_context):
    back = dot_nt(grad_half[:, :384], full[1, 2].reshape(D, 384))
    back = back + dot_nt(grad_half[:, 384:], full[1, 3].reshape(D, 384))
    grad_context[...] = dot_nt(back.astype(BF16), order[...]).astype(BF16)


def weight_term(grad_half, scatter, context, box):
    ordered = dot(context[...], scatter[...]).astype(BF16)
    term = dot_tn(ordered, grad_half).astype(BF16)
    for n in range(16):
        for c in range(2):
            box[c, n] = term[n * 48 : n * 48 + 48, c * 384 : c * 384 + 384]


def backward_attention(pairs, qkv, prob, grad_context, grad_qkv):
    for j in pairs:
        for u in range(2):
            columns = [slice(s * D + j * 128, s * D + j * 128 + 128) for s in range(3)]
            query, key, value = [unit_rows(qkv, u, c) for c in columns]
            grad = heads(unit_rows(grad_context, u, slice(j * 128, j * 128 + 128)))
            p = prob[j * 2 + u]
            half = p.astype(BF16)
            grad_prob = dot_nt(grad, value)
            grad_value = dot_tn(half, grad).astype(BF16)
            row = jnp.sum(p * grad_prob, -1, keepdims=True)
            grad_score = (p * (grad_prob - row) * 0.125).astype(BF16)
            both = jnp.concatenate([grad_score[:128], grad_score[128:]], 1)
            put_rows(grad_qkv, u, columns[0], dot(both, heads(key)).astype(BF16))
            put_rows(grad_qkv, u, columns[1], dot_tn(grad_score, heads(query)).astype(BF16))
            put_rows(grad_qkv, u, columns[2], grad_value)


def backward_tokens(units, inverses, grad_output, grad_qkv, full, order, scale, out):
    back = jnp.zeros((256, D), F32)
    for n in range(6):
        weight = full[n // 4, n % 4].reshape(D, 384)
        back = back + dot_nt(grad_qkv[:, n * 384 : n * 384 + 384], weight)
    grad_normed = dot_nt(back.astype(BF16), order[...])
    scaled = grad_normed * scale[...].reshape(1, D)
    unit, inverse = units[...], inverses[...]
    grad_norm = inverse * (
        scaled
        - jnp.mean(scaled, -1, keepdims=True)
        - unit * jnp.mean(scaled * unit, -1, keepdims=True)
    )
    out[...] = (grad_output + grad_norm).astype(BF16).reshape(2, 4, 32, D)


def kernel(
    video, upstream, w_qkv, w_out, scale_in, bias_in, windows_in, positives_in,
    video_out, weight_out, pooled_out, loss_out,
    wq, wo, scale, bias, windows, positives, order, scatter,
    vbuf, ubuf, vbox, ubox, tokens, ups, zbuf, full, normed, qkv, prob, context, part,
    box1, in1, buf2, pool, pooled, units, grad_pooled, grad_output, grad_context, grad_qkv, grads,
    box, gw_pair, gw_own, gw_buf, wide, box_z, buf_z, rows, pair_buf, out_box,
    token_unit, token_inverse,
    load, local, tok_send, tok_recv, pair_send, pair_recv,
    w_send, recv_z, recv_first, recv_second, recv_third, wp_sem,
    pool_send, pool_recv, gw_send, gw_recv, out_send, out_recv, store,
):
    me = Place()
    loads = [(w_qkv, wq), (w_out, wo), (scale_in, scale), (bias_in, bias)]
    loads += [(windows_in, windows), (positives_in, positives)]
    loads = [pltpu.make_async_copy(a, b, load.at[i]) for i, (a, b) in enumerate(loads)]
    for copy in loads:
        copy.start()
    announce(me)
    loads[0].wait()
    loads[1].wait()
    column = pl.multiple_of(lax.rem(me.dp, 6) * 384, 384)
    column_out = pl.multiple_of(lax.rem(me.dp, 2) * 384, 384)
    piece = jnp.where(me.dp < 6, wq[:, pl.ds(column, 384)], wo[:, pl.ds(column_out, 384)])
    zbuf[0] = jnp.concatenate([piece.astype(F32), jnp.zeros((4, 384), F32)], 0).astype(BF16)
    arrive()
    start_weights(me, zbuf, w_send.at[0], recv_z)
    start_tokens(me, video, vbuf, local.at[0], tok_send.at[0], tok_recv.at[0])
    order[...] = gather_order(me)
    scatter[...] = scatter_order()
    for copy in loads[2:]:
        copy.wait()
    window_units(windows, units)
    pair_sems = (wp_sem.at[0], wp_sem.at[1])
    second = (recv_second, *pair_sems)
    third = (w_send.at[3], recv_third, *pair_sems)
    spread_first(me, zbuf, full, 0, recv_z, w_send.at[1], recv_first)
    spread_second(me, full, 0, recv_first, w_send.at[2], *second)
    spread_first(me, zbuf, full, 1, recv_z, w_send.at[1], recv_first)
    spread_third(me, full, 0, recv_second, *third)
    spread_second(me, full, 1, recv_first, w_send.at[4], *second, to=(2, 1, 3))
    start_tokens(me, upstream, ubuf, local.at[1], tok_send.at[1], tok_recv.at[1], 16, 8)
    wait_tokens(me, video, vbuf, local.at[0], tok_recv.at[0])
    start_pair(me, vbuf, tokens, vbox, pair_send.at[0], pair_recv.at[0])
    spread_last(me, full, 0, recv_third, *pair_sems)
    spread_direct(me, full, 1, recv_second, *pair_sems)
    drain(tokens.at[0], pair_recv.at[0])
    norm_tokens(tokens, scale, bias, order, token_unit, token_inverse, normed)
    drain(full.at[:, :, 0], wp_sem.at[1])
    project(normed, full, qkv)
    attend(qkv, prob, context)
    pool_clips(tokens, context, order, full, part)
    start_pooled(me, part, box1, in1, pool_send.at[0], pool_recv.at[0])
    pooled_along_z(me, in1, pool_recv.at[0], buf2, pool_send.at[1], pool_recv.at[1])
    start_tokens(me, upstream, ubuf, local.at[1], tok_send.at[1], tok_recv.at[1], 7, 1)
    pooled_in_plane(me, buf2, pool_recv.at[1], pool, pool_send.at[2], pool_recv.at[2])
    wait_tokens(me, upstream, ubuf, local.at[1], tok_recv.at[1])
    start_pair(me, ubuf, ups, ubox, pair_send.at[1], pair_recv.at[1])
    finish_pooled(pool, pool_recv.at[2], pooled)
    contrast(pooled, units, positives, loss_out, grad_pooled)
    save = pltpu.make_async_copy(pooled, pooled_out, store)
    save.start()
    drain(ups.at[0], pair_recv.at[1])
    grad_clip = grad_pooled[pl.ds(pl.multiple_of(me.dp * 8, 8), 8), :] * 64.0
    grad_output[...] = spread(ups, grad_clip)
    grad_half = grad_output[...].astype(BF16)
    weight_term(grad_half, scatter, context, box)
    start_weight_sum(me, box, gw_pair, gw_send.at[0], gw_recv.at[0])
    project_back(grad_half, full, order, grad_context)
    backward_attention((0, 1), qkv, prob, grad_context, grad_qkv)
    plane_weight_sum(
        me, box, gw_pair, gw_recv.at[0], gw_own, gw_buf, gw_send.at[1], gw_recv.at[1]
    )
    backward_attention((2, 3, 4, 5), qkv, prob, grad_context, grad_qkv)
    backward_tokens(token_unit, token_inverse, grad_output[...], grad_qkv, full, order, scale, grads)
    start_back_pair(me, grads, pair_buf, out_send.at[0], out_recv.at[0])
    fill_back(pair_buf, out_recv.at[0], out_box)
    out_sems = (local.at[2], out_send.at[1], out_recv.at[1])
    start_tokens(me, out_box, video_out, *out_sems, 16, 12)
    second_weight_sum(me, gw_buf, gw_recv.at[1], wide, box_z, buf_z, gw_send.at[2], gw_recv.at[2])
    start_tokens(me, out_box, video_out, *out_sems, 11, 1)
    third_weight_sum(me, buf_z, gw_recv.at[2], rows, gw_send.at[3], gw_recv.at[3])
    finish_weight_sum(me, rows, gw_recv.at[3], weight_out)
    wait_tokens(me, out_box, video_out, local.at[2], out_recv.at[1])
    save.wait()
    drain(zbuf.at[pl.ds(0, 15)], w_send.at[0])
    drain(full.at[0, pl.ds(0, 3), 0, 0], w_send.at[1])
    drain(full.at[0, pl.ds(0, 2), 0], w_send.at[2])
    drain(full.at[0, 0, 0], w_send.at[3])
    drain(full.at[0, pl.ds(0, 3), 0], w_send.at[4])
    drain(full.at[:, :, 0], wp_sem.at[0])
    for i in range(2):
        drain(vbuf.at[pl.ds(0, 31)], tok_send.at[i])
        drain(vbox, pair_send.at[i])
    drain(in1.at[pl.ds(0, 3)], pool_send.at[0])
    drain(buf2.at[pl.ds(0, 15)], pool_send.at[1])
    drain(pool.at[pl.ds(0, 31)], pool_send.at[2])
    drain(gw_pair, gw_send.at[0])
    drain(gw_buf.at[pl.ds(0, 15)], gw_send.at[1])
    drain(buf_z.at[pl.ds(0, 15)], gw_send.at[2])
    drain(rows.at[0], gw_send.at[3])
    drain(pair_buf.at[0], out_send.at[0])
    drain(out_box.at[pl.ds(0, 31)], out_send.at[1])


def shape(*dims, dtype=BF16):
    return jax.ShapeDtypeStruct(dims, dtype)


def keep(*refs):
    n = 4
    ins, outs, held, sems = refs[:n], refs[n : 2 * n], refs[2 * n : 3 * n], refs[3 * n]
    reads = [pltpu.make_async_copy(ins[i], held[i], sems.at[0, i]) for i in range(n)]
    writes = [pltpu.make_async_copy(held[i], outs[i], sems.at[1, i]) for i in range(n)]
    for copy in reads:
        copy.start()
    for read, write in zip(reads, writes):
        read.wait()
        write.start()
    for copy in writes:
        copy.wait()


def scratch_shapes():
    dma = pltpu.SemaphoreType.DMA

    def half(*dims):
        return pltpu.VMEM(dims, BF16)

    def single(*dims):
        return pltpu.VMEM(dims, F32)

    return [
        half(12, 3 * D), half(12, D), single(D), single(D), single(64, D),
        pltpu.VMEM((64,), jnp.int32), half(D, D), half(D, D),
        half(32, 8, D), half(32, 8, D), half(4, 32, D), half(4, 32, D),
        half(2, 4, 32, D), half(2, 4, 32, D), half(16, 16, 384), half(2, 4, 2, 2, 2, 2, 48, 384),
        half(256, D), half(256, 3 * D), single(12, 256, 128), half(256, D), single(8, D),
        single(4, 2, D), single(4, 2, D), single(16, 2, D), single(32, 2, D),
        single(64, D), single(64, D), single(64, D), single(256, D),
        half(256, D), half(256, 3 * D), half(2, 4, 32, D),
        half(2, 16, 48, 384), half(16, 48, 384), half(16, 48, 384), half(16, 48, 384),
        single(16, 16, 128), half(16, 16, 128), half(16, 16, 128), single(2, 16, 128),
        half(2, 4, 32, D), half(32, 8, D), single(256, D), single(256, 1),
        dma((6,)), dma((3,)), dma((2,)), dma((2,)), dma((2,)), dma((2,)),
        dma((5,)), dma((2,)), dma((2, 2)), dma((2, 2, 3)), dma((2, 2, 2)), dma((2,)),
        dma((3,)), dma((3,)), dma((4,)), dma((4,)), dma((2,)), dma((2,)), dma,
    ]


def per_device(video, upstream, standardize_scale, ln_bias, w_qkv, w_out, windows, positives):
    anywhere, vmem = pl.BlockSpec(memory_space=pl.ANY), pl.BlockSpec(memory_space=pltpu.VMEM)
    grad_video, grad_out_weight, pooled, loss = pl.pallas_call(
        kernel,
        out_shape=[
            shape(32, 8, D), shape(1, 1152, dtype=F32), shape(64, D, dtype=F32),
            shape(1, 1, dtype=F32),
        ],
        in_specs=[anywhere] * 8,
        out_specs=[anywhere, vmem, anywhere, vmem],
        scratch_shapes=scratch_shapes(),
        compiler_params=pltpu.CompilerParams(
            vmem_limit_bytes=VMEM_LIMIT, collective_id=1, has_side_effects=True
        ),
    )(
        video.reshape(32, 8, D), upstream.reshape(32, 8, D), w_qkv, w_out,
        standardize_scale, ln_bias, windows, positives,
    )
    results = (grad_video, grad_out_weight, pooled, loss)
    grad_video, grad_out_weight, pooled, loss = pl.pallas_call(
        keep,
        out_shape=[jax.ShapeDtypeStruct(a.shape, a.dtype) for a in results],
        in_specs=[anywhere] * 4,
        out_specs=[anywhere] * 4,
        scratch_shapes=[pltpu.VMEM(a.shape, a.dtype) for a in results]
        + [pltpu.SemaphoreType.DMA((2, 4))],
    )(*results)
    return grad_video.reshape(1, 1, 256, D), grad_out_weight, pooled, loss.reshape(())


def solution(mesh):
    in_specs = (
        P("dp", "seq", None, None),
        P("dp", "seq", None, None),
        P(),
        P(),
        P("seq", None),
        P("seq", None),
        P(),
        P(),
    )
    out_specs = (P("dp", "seq", None, None), P(("dp", "seq"), None), P(), P())
    return jax.shard_map(
        per_device, mesh=mesh, in_specs=in_specs, out_specs=out_specs, check_vma=False
    )
```

```python
import jax
import jax.numpy as jnp
from jax import lax
from jax.experimental import pallas as pl
from jax.experimental.pallas import tpu as pltpu
from jax.sharding import PartitionSpec as P

MESH = pl.DeviceIdType.MESH
F32 = jnp.float32
BF16 = jnp.bfloat16
D = 768
EPS = 1e-6
NEG = -1e30
SHARP = 1.0 / 0.07
VMEM_LIMIT = 56 * 1024 * 1024


class Place:
    def __init__(self):
        self.dp = lax.axis_index("dp")
        self.seq = lax.axis_index("seq")
        self.x_hi = self.dp // 4
        self.y = self.dp % 4
        self.z = self.seq // 4
        self.role = self.seq % 4
        self.x_lo = self.role // 2
        self.core = self.seq % 2
        self.k = self.seq // 2
        self.x = self.x_hi * 2 + self.x_lo
        self.m = self.dp * 4 + self.role


def send(src, dst, send_sem, recv_sem, dp, seq):
    pltpu.make_async_remote_copy(
        src_ref=src,
        dst_ref=dst,
        send_sem=send_sem,
        recv_sem=recv_sem,
        device_id=(dp, seq),
        device_id_type=MESH,
    ).start()


def wrap(a, n):
    return jnp.where(a >= n, a - n, a)


def drain(ref, sem):
    pltpu.make_async_copy(ref, ref, sem).wait()


def announce(me):
    sem = pltpu.get_barrier_semaphore()

    def slab(i, carry):
        to = wrap(me.k + i, 32) * 2 + me.core
        pl.semaphore_signal(sem, inc=1, device_id=(me.dp, to), device_id_type=MESH)
        return carry

    def plane(i, carry):
        dp = wrap(me.dp + i, 8)
        for role in range(4):
            pl.semaphore_signal(sem, inc=1, device_id=(dp, me.z * 4 + role), device_id_type=MESH)
        return carry

    lax.fori_loop(1, 32, slab, 0)
    lax.fori_loop(1, 8, plane, 0)
    for i in range(1, 4):
        to = me.z * 4 + wrap(me.role + i, 4)
        pl.semaphore_signal(sem, inc=1, device_id=(me.dp, to), device_id_type=MESH)


def arrive():
    pl.semaphore_wait(pltpu.get_barrier_semaphore(), 62)


def dot(a, b):
    return lax.dot_general(a, b, (((1,), (0,)), ((), ())), preferred_element_type=F32)


def dot_nt(a, b):
    return lax.dot_general(a, b, (((1,), (1,)), ((), ())), preferred_element_type=F32)


def dot_tn(a, b):
    return lax.dot_general(a, b, (((0,), (0,)), ((), ())), preferred_element_type=F32)


def iota(shape, dim):
    return lax.broadcasted_iota(jnp.int32, shape, dim)


def one_hot(condition):
    return jnp.where(condition, 1.0, 0.0).astype(BF16)


def gather_order(me):
    j = iota((1, D), 1)
    block, rest = j // 96, j % 96
    core, chunk, x_lo = block // 4, (block // 2) % 2, block % 2
    z8, r = rest // 12, rest % 12
    near = jnp.where(z8 < 5, z8, z8 + 8)
    from_z = (me.z + jnp.where(chunk == 0, near, z8 + 5)) % 16
    natural = (from_z * 4 + x_lo * 2 + core) * 12 + r
    return one_hot(iota((D, D), 0) == natural)


def scatter_order():
    j = iota((1, D), 1)
    dp, rest = j // 96, j % 96
    x_lo, z, r = rest // 48, (rest % 48) // 3, rest % 3
    natural = dp * 96 + z * 6 + x_lo * 3 + r
    return one_hot(iota((D, D), 0) == natural)


def split3(a):
    high = a.astype(BF16)
    rest = a - high.astype(F32)
    mid = rest.astype(BF16)
    low = (rest - mid.astype(F32)).astype(BF16)
    return jnp.concatenate([high.astype(F32), mid.astype(F32), low.astype(F32)], 0).astype(BF16)


def start_tokens(me, src, buf, local_sem, send_sem, recv_sem, far=16, near=1):
    def one(to):
        send(src.at[to], buf.at[me.k], send_sem, recv_sem, me.dp, to * 2 + me.core)

    def step(i, carry):
        one(wrap(me.k + 16 - i, 32))
        one(wrap(me.k + 16 + i, 32))
        return carry

    if far == 16:
        pltpu.make_async_copy(src.at[me.k], buf.at[me.k], local_sem).start()
        one(wrap(me.k + 16, 32))
    lax.fori_loop(max(16 - far, 1), 17 - near, step, 0)


def wait_tokens(me, src, buf, local_sem, recv_sem):
    pltpu.make_async_copy(src.at[me.k], buf.at[me.k], local_sem).wait()
    drain(buf.at[pl.ds(0, 31)], recv_sem)


def start_pair(me, buf, out, box, send_sem, recv_sem):
    rows = buf[...].astype(F32).reshape(256, D).astype(BF16)
    r, col = iota((128, 1), 0), iota((128, 256), 1)
    at = (r % 32) * 8 + r // 32
    theirs = dot(one_hot(col == at + 4 * (1 - me.core)), rows)
    box[...] = theirs.astype(BF16).reshape(4, 32, D)
    send(box, out.at[me.core], send_sem, recv_sem, me.dp, me.seq + 1 - 2 * me.core)
    mine = dot(one_hot(col == at + 4 * me.core), rows)
    out[me.core] = mine.astype(BF16).reshape(4, 32, D)


OFFSETS = (0, 1, 2, 3, 4, 13, 14, 15, 5, 6, 7, 8, 9, 10, 11, 12)


def start_weights(me, zbuf, send_sem, recv_z):
    for d in (12, 13, 3, 14, 2, 15, 1, 8, 7, 9, 6, 10, 5, 11, 4):
        j = OFFSETS.index(16 - d)
        to = wrap(me.z + d, 16) * 4 + me.role
        send(zbuf.at[0], zbuf.at[j], send_sem, recv_z.at[j // 8], me.dp, to)


def x_device(me, x):
    return (x // 2) * 4 + me.y, me.z * 4 + (x % 2) * 2 + me.core


def spread_first(me, zbuf, full, chunk, recv_z, send_sem, recv):
    drain(zbuf.at[pl.ds(0, 7 + chunk)], recv_z.at[chunk])
    r = iota((96, 1), 0)
    pick = one_hot(iota((96, 128), 1) == (r // 12) * 16 + r % 12)
    rows = zbuf[chunk * 8 : chunk * 8 + 8].reshape(128, 384)
    block = dot(pick, rows).astype(BF16)
    full[me.x_hi, me.y, me.core, chunk, me.x_lo] = block.reshape(2, 48, 384)
    a = full.at[me.x_hi, me.y, me.core, chunk, me.x_lo, 0]
    b = full.at[me.x_hi, me.y, me.core, chunk, me.x_lo, 1]
    for i in (2, 1, 3):
        send(a, a, send_sem, recv.at[chunk, 0], *x_device(me, wrap(me.x + i, 4)))
        send(b, b, send_sem, recv.at[chunk, 1], me.x_hi * 4 + wrap(me.y + i, 4), me.seq)


def spread_second(me, full, chunk, recv_first, send_sem, recv, send_pair, recv_pair, to=(1, 3)):
    pair = me.seq + 1 - 2 * me.core
    drain(full.at[0, pl.ds(0, 3), 0, 0, 0, 0], recv_first.at[chunk, 0])
    a = full.at[:, me.y, me.core, chunk, :, 0]
    for i in to:
        send(a, a, send_sem, recv.at[chunk, 0, i - 1], me.x_hi * 4 + wrap(me.y + i, 4), me.seq)
    drain(full.at[0, pl.ds(0, 3), 0, 0, 0, 0], recv_first.at[chunk, 1])
    b = full.at[me.x_hi, :, me.core, chunk, me.x_lo, 1]
    for i in to:
        send(b, b, send_sem, recv.at[chunk, 1, i - 1], *x_device(me, wrap(me.x + i, 4)))
    send(a, a, send_pair, recv_pair, me.dp, pair)
    send(b, b, send_pair, recv_pair, me.dp, pair)


def spread_third(me, full, chunk, recv_second, send_sem, recv, send_pair, recv_pair):
    pair = me.seq + 1 - 2 * me.core
    for n, (i, o) in enumerate(((3, 1), (1, 3))):
        y, x = wrap(me.y + i, 4), wrap(me.x + i, 4)
        a = full.at[:, y, me.core, chunk, :, 0]
        drain(a, recv_second.at[chunk, 0, 2 * n])
        half = full.at[n, y, me.core, chunk, :, 0]
        send(half, half, send_sem, recv.at[chunk, 0, n], me.x_hi * 4 + wrap(me.y + o, 4), me.seq)
        b = full.at[x // 2, :, me.core, chunk, x % 2, 1]
        drain(b, recv_second.at[chunk, 1, 2 * n])
        half = full.at[x // 2, pl.ds(2 * n, 2), me.core, chunk, x % 2, 1]
        send(half, half, send_sem, recv.at[chunk, 1, n], *x_device(me, wrap(me.x + o, 4)))
        send(a, a, send_pair, recv_pair, me.dp, pair)
        send(b, b, send_pair, recv_pair, me.dp, pair)


def spread_last(me, full, chunk, recv_third, send_pair, recv_pair):
    pair = me.seq + 1 - 2 * me.core
    y, x = wrap(me.y + 2, 4), wrap(me.x + 2, 4)
    for n in range(2):
        a = full.at[n, y, me.core, chunk, :, 0]
        drain(a, recv_third.at[chunk, 0, n])
        send(a, a, send_pair, recv_pair, me.dp, pair)
        b = full.at[x // 2, pl.ds(2 * n, 2), me.core, chunk, x % 2, 1]
        drain(b, recv_third.at[chunk, 1, n])
        send(b, b, send_pair, recv_pair, me.dp, pair)


def spread_direct(me, full, chunk, recv_second, send_pair, recv_pair):
    pair = me.seq + 1 - 2 * me.core
    for i in (1, 3, 2):
        a = full.at[:, wrap(me.y + 4 - i, 4), me.core, chunk, :, 0]
        drain(a, recv_second.at[chunk, 0, i - 1])
        send(a, a, send_pair, recv_pair, me.dp, pair)
        x = wrap(me.x + 4 - i, 4)
        b = full.at[x // 2, :, me.core, chunk, x % 2, 1]
        drain(b, recv_second.at[chunk, 1, i - 1])
        send(b, b, send_pair, recv_pair, me.dp, pair)


def start_pooled(me, part, box1, in1, send_sem, recv_sem):
    for q in range(4):
        box1[q] = part[2 * q : 2 * q + 2, :]
    in1[me.role] = box1[me.role]
    for i in range(1, 4):
        to = wrap(me.role + i, 4)
        send(box1.at[to], in1.at[me.role], send_sem, recv_sem, me.dp, me.z * 4 + to)


def pooled_along_z(me, in1, recv_first, buf2, send_sem, recv_sem):
    drain(in1.at[pl.ds(0, 3)], recv_first)
    buf2[me.z] = jnp.sum(in1[...], 0)

    for i in (8, 9, 7, 10, 6, 11, 5, 12, 4, 13, 3, 14, 2, 15, 1):
        to = wrap(me.z + i, 16) * 4 + me.role
        send(buf2.at[me.z], buf2.at[me.z], send_sem, recv_sem, me.dp, to)


def pooled_in_plane(me, buf2, recv_second, pool, send_sem, recv_sem):
    drain(buf2.at[pl.ds(0, 15)], recv_second)
    pool[me.m] = jnp.sum(buf2[...], 0) * (1.0 / 2048.0)

    mine = pool.at[me.m]

    def step(i, carry):
        dp = wrap(me.dp + i, 8)
        for role in range(4):
            send(mine, mine, send_sem, recv_sem, dp, me.z * 4 + role)
        return carry

    lax.fori_loop(1, 8, step, 0)
    for i in range(1, 4):
        send(mine, mine, send_sem, recv_sem, me.dp, me.z * 4 + wrap(me.role + i, 4))


def finish_pooled(pool, recv_sem, pooled):
    drain(pool.at[pl.ds(0, 31)], recv_sem)
    for m in range(32):
        pooled[2 * m : 2 * m + 2, :] = pool[m]


def start_weight_sum(me, box, pair_buf, send_sem, recv_sem):
    send(
        box.at[1 - me.core], pair_buf, send_sem, recv_sem, me.dp, me.seq + 1 - 2 * me.core
    )


def plane_weight_sum(me, box, pair_buf, recv_pair, own, buf, send_sem, recv_sem):
    drain(pair_buf, recv_pair)
    own[...] = (box[me.core].astype(F32) + pair_buf[...].astype(F32)).astype(BF16)
    n = me.dp * 2 + me.x_lo
    buf[n] = own[n]

    def step(i, carry):
        dp = wrap(me.dp + i, 8)
        for x_lo in range(2):
            to = me.z * 4 + x_lo * 2 + me.core
            send(own.at[dp * 2 + x_lo], buf.at[n], send_sem, recv_sem, dp, to)
        return carry

    lax.fori_loop(1, 8, step, 0)
    other = 1 - me.x_lo
    to = me.z * 4 + other * 2 + me.core
    send(own.at[me.dp * 2 + other], buf.at[n], send_sem, recv_sem, me.dp, to)


def second_weight_sum(me, buf, recv_sem, wide, box_z, buf_z, send_sem, recv_z):
    drain(buf.at[pl.ds(0, 15)], recv_sem)
    total = lax.fori_loop(
        0, 16, lambda i, t: t + buf[i].astype(F32), jnp.zeros((48, 384), F32)
    )
    wide[...] = jnp.zeros_like(wide)
    for z in range(16):
        for r in range(3):
            row = total[3 * z + r : 3 * z + r + 1, :]
            for n in range(3):
                wide[z, r * 3 + n : r * 3 + n + 1, :] = row[:, n * 128 : n * 128 + 128]
    box_z[...] = wide[...].astype(BF16)
    buf_z[me.z] = box_z[me.z]
    for i in (8, 9, 7, 10, 6, 11, 5, 12, 4, 13, 3, 14, 2, 15, 1):
        to = wrap(me.z + i, 16)
        send(box_z.at[to], buf_z.at[me.z], send_sem, recv_z, me.dp, to * 4 + me.role)


def third_weight_sum(me, buf_z, recv_z, rows, send_sem, recv_sem):
    drain(buf_z.at[pl.ds(0, 15)], recv_z)
    rows[me.core] = jnp.sum(buf_z[...].astype(F32), 0)
    send(
        rows.at[me.core], rows.at[me.core], send_sem, recv_sem,
        me.dp, me.seq + 1 - 2 * me.core,
    )


def finish_weight_sum(me, rows, recv_sem, out):
    drain(rows.at[0], recv_sem)
    halves = (rows[0], rows[1])
    first = me.core == 0

    def part(source, row, n):
        at = row * 3 + n
        return halves[source][at : at + 1]

    for n in range(3):
        at = n * 128
        out[0:1, at : at + 128] = jnp.where(first, part(0, 0, n), part(1, 1, n))
        out[0:1, 384 + at : 512 + at] = jnp.where(first, part(1, 0, n), part(0, 2, n))
        out[0:1, 768 + at : 896 + at] = jnp.where(first, part(0, 1, n), part(1, 2, n))


def start_back_pair(me, grads, buf, send_sem, recv_sem):
    theirs = 1 - me.core
    send(grads.at[theirs], buf.at[me.core], send_sem, recv_sem, me.dp, me.seq + 1 - 2 * me.core)
    buf[me.core] = grads[me.core]


def fill_back(buf, recv_pair, box):
    drain(buf.at[0], recv_pair)
    r = iota((256, 1), 0)
    at = ((r // 4) % 2) * 128 + (r % 4) * 32 + r // 8
    rows = dot(one_hot(iota((256, 256), 1) == at), buf[...].reshape(256, D))
    box[...] = rows.reshape(32, 8, D).astype(BF16)


def normalize(x):
    centered = x - jnp.mean(x, -1, keepdims=True)
    inverse = lax.rsqrt(jnp.mean(centered * centered, -1, keepdims=True) + EPS)
    return centered * inverse, inverse


def exact(a, b, contract):
    return lax.dot_general(
        a, b, (contract, ((), ())), precision=lax.Precision.HIGHEST, preferred_element_type=F32
    )


def window_units(windows, out):
    w = windows[...]
    out[...] = w * lax.rsqrt(jnp.mean(w * w, -1, keepdims=True) + EPS) * D ** (-0.5)


def contrast(pooled, units, positives, loss, grad):
    p, root = pooled[...], D ** (-0.5)
    inverse = lax.rsqrt(jnp.mean(p * p, -1, keepdims=True) + EPS)
    logits = exact(units[...], p * inverse * root, ((1,), (1,))) * SHARP
    matched = iota((64, 64), 0) == positives[...].reshape(1, 64)
    total = -jnp.sum(jnp.where(matched, logits, 0.0))
    slope = jnp.where(matched, -1.0, 0.0)
    for axis in range(2):
        top = jnp.max(logits, axis, keepdims=True)
        weight = jnp.exp(logits - top)
        size = jnp.sum(weight, axis, keepdims=True)
        total = total + 0.5 * jnp.sum(top + jnp.log(size))
        slope = slope + 0.5 * (weight / size)
    loss[...] = jnp.full((1, 1), total * (1.0 / 64.0), F32)
    grad_unit = exact(slope * (SHARP / 64.0), units[...], ((0,), (0,)))
    inner = jnp.mean(grad_unit * p, -1, keepdims=True)
    grad[...] = inverse * root * (grad_unit - p * (inverse * inverse) * inner)


def clip_pick():
    return one_hot((iota((8, 256), 1) % 32) // 4 == iota((8, 256), 0))


def unit_rows(ref, u, columns):
    return jnp.concatenate(
        [ref[u * 64 : u * 64 + 64, columns], ref[128 + u * 64 : 192 + u * 64, columns]], 0
    )


def put_rows(ref, u, columns, value):
    ref[u * 64 : u * 64 + 64, columns] = value[:64]
    ref[128 + u * 64 : 192 + u * 64, columns] = value[64:]


def heads(a):
    even = iota(a.shape, 1) < 64
    zero = jnp.zeros_like(a)
    return jnp.concatenate([jnp.where(even, a, zero), jnp.where(even, zero, a)], 0)


def same_patch():
    return (iota((256, 128), 0) // 32) % 2 == (iota((256, 128), 1) // 32) % 2


def norm_tokens(tokens, scale, bias, order, units, inverses, normed):
    unit, inverse = normalize(tokens[...].reshape(256, D).astype(F32))
    units[...] = unit
    inverses[...] = inverse
    rows = (unit * scale[...].reshape(1, D) + bias[...].reshape(1, D)).astype(BF16)
    normed[...] = dot(rows, order[...]).astype(BF16)


def project(normed, full, qkv):
    for n in range(6):
        weight = full[n // 4, n % 4].reshape(D, 384)
        qkv[:, n * 384 : n * 384 + 384] = dot(normed[...], weight).astype(BF16)


def attend(qkv, prob, context):
    keep = same_patch()
    for j in range(6):
        for u in range(2):
            columns = [slice(s * D + j * 128, s * D + j * 128 + 128) for s in range(3)]
            query, key, value = [unit_rows(qkv, u, c) for c in columns]
            score = dot_nt(heads(query), key) * 0.125
            score = jnp.where(keep, score, NEG)
            top = jnp.max(score, -1, keepdims=True)
            weight = jnp.exp(score - top)
            p = weight / jnp.sum(weight, -1, keepdims=True)
            prob[j * 2 + u] = p
            half = p.astype(BF16)
            both = jnp.concatenate([half[:128], half[128:]], 1)
            mixed = dot(both, heads(value)).astype(BF16)
            put_rows(context, u, slice(j * 128, j * 128 + 128), mixed)


def pool_clips(tokens, context, order, full, part):
    pick = clip_pick()
    ctx_sum = split3(dot(pick, context[...]))
    ctx_sum = dot(ctx_sum, order[...]).astype(BF16)
    sums = dot(pick, tokens[...].reshape(256, D))
    for n in range(2):
        weight = full[1, 2 + n].reshape(D, 384)
        s = dot(ctx_sum, weight)
        columns = slice(n * 384, n * 384 + 384)
        part[:, columns] = sums[:, columns] + s[0:8] + s[8:16] + s[16:24]


def spread(upstream, grad_clip):
    pick = one_hot((iota((256, 24), 0) % 32) // 4 == iota((256, 24), 1) % 8)
    return upstream[...].reshape(256, D).astype(F32) + dot(pick, split3(grad_clip))


def project_back(grad_half, full, order, grad_context):
    back = dot_nt(grad_half[:, :384], full[1, 2].reshape(D, 384))
    back = back + dot_nt(grad_half[:, 384:], full[1, 3].reshape(D, 384))
    grad_context[...] = dot_nt(back.astype(BF16), order[...]).astype(BF16)


def weight_term(grad_half, scatter, context, box):
    ordered = dot(context[...], scatter[...]).astype(BF16)
    term = dot_tn(ordered, grad_half).astype(BF16)
    for n in range(16):
        for c in range(2):
            box[c, n] = term[n * 48 : n * 48 + 48, c * 384 : c * 384 + 384]


def backward_attention(pairs, qkv, prob, grad_context, grad_qkv):
    for j in pairs:
        for u in range(2):
            columns = [slice(s * D + j * 128, s * D + j * 128 + 128) for s in range(3)]
            query, key, value = [unit_rows(qkv, u, c) for c in columns]
            grad = heads(unit_rows(grad_context, u, slice(j * 128, j * 128 + 128)))
            p = prob[j * 2 + u]
            half = p.astype(BF16)
            grad_prob = dot_nt(grad, value)
            grad_value = dot_tn(half, grad).astype(BF16)
            row = jnp.sum(p * grad_prob, -1, keepdims=True)
            grad_score = (p * (grad_prob - row) * 0.125).astype(BF16)
            both = jnp.concatenate([grad_score[:128], grad_score[128:]], 1)
            put_rows(grad_qkv, u, columns[0], dot(both, heads(key)).astype(BF16))
            put_rows(grad_qkv, u, columns[1], dot_tn(grad_score, heads(query)).astype(BF16))
            put_rows(grad_qkv, u, columns[2], grad_value)


def backward_tokens(units, inverses, grad_output, grad_qkv, full, order, scale, out):
    back = jnp.zeros((256, D), F32)
    for n in range(6):
        weight = full[n // 4, n % 4].reshape(D, 384)
        back = back + dot_nt(grad_qkv[:, n * 384 : n * 384 + 384], weight)
    grad_normed = dot_nt(back.astype(BF16), order[...])
    scaled = grad_normed * scale[...].reshape(1, D)
    unit, inverse = units[...], inverses[...]
    grad_norm = inverse * (
        scaled
        - jnp.mean(scaled, -1, keepdims=True)
        - unit * jnp.mean(scaled * unit, -1, keepdims=True)
    )
    out[...] = (grad_output + grad_norm).astype(BF16).reshape(2, 4, 32, D)


def kernel(
    video, upstream, w_qkv, w_out, scale_in, bias_in, windows_in, positives_in,
    video_out, weight_out, pooled_out, loss_out,
    wq, wo, scale, bias, windows, positives, order, scatter,
    vbuf, ubuf, vbox, ubox, tokens, ups, zbuf, full, normed, qkv, prob, context, part,
    box1, in1, buf2, pool, pooled, units, grad_pooled, grad_output, grad_context, grad_qkv, grads,
    box, gw_pair, gw_own, gw_buf, wide, box_z, buf_z, rows, pair_buf, out_box,
    token_unit, token_inverse,
    load, local, tok_send, tok_recv, pair_send, pair_recv,
    w_send, recv_z, recv_first, recv_second, recv_third, wp_sem,
    pool_send, pool_recv, gw_send, gw_recv, out_send, out_recv, store,
):
    me = Place()
    loads = [(w_qkv, wq), (w_out, wo), (scale_in, scale), (bias_in, bias)]
    loads += [(windows_in, windows), (positives_in, positives)]
    loads = [pltpu.make_async_copy(a, b, load.at[i]) for i, (a, b) in enumerate(loads)]
    for copy in loads:
        copy.start()
    announce(me)
    loads[0].wait()
    loads[1].wait()
    column = pl.multiple_of(lax.rem(me.dp, 6) * 384, 384)
    column_out = pl.multiple_of(lax.rem(me.dp, 2) * 384, 384)
    piece = jnp.where(me.dp < 6, wq[:, pl.ds(column, 384)], wo[:, pl.ds(column_out, 384)])
    zbuf[0] = jnp.concatenate([piece.astype(F32), jnp.zeros((4, 384), F32)], 0).astype(BF16)
    arrive()
    start_weights(me, zbuf, w_send.at[0], recv_z)
    start_tokens(me, video, vbuf, local.at[0], tok_send.at[0], tok_recv.at[0])
    order[...] = gather_order(me)
    scatter[...] = scatter_order()
    for copy in loads[2:]:
        copy.wait()
    window_units(windows, units)
    pair_sems = (wp_sem.at[0], wp_sem.at[1])
    second = (recv_second, *pair_sems)
    third = (w_send.at[3], recv_third, *pair_sems)
    spread_first(me, zbuf, full, 0, recv_z, w_send.at[1], recv_first)
    start_tokens(me, upstream, ubuf, local.at[1], tok_send.at[1], tok_recv.at[1], 16, 8)
    spread_second(me, full, 0, recv_first, w_send.at[2], *second)
    spread_first(me, zbuf, full, 1, recv_z, w_send.at[1], recv_first)
    spread_third(me, full, 0, recv_second, *third)
    spread_second(me, full, 1, recv_first, w_send.at[4], *second, to=(2, 1, 3))
    wait_tokens(me, video, vbuf, local.at[0], tok_recv.at[0])
    start_pair(me, vbuf, tokens, vbox, pair_send.at[0], pair_recv.at[0])
    spread_last(me, full, 0, recv_third, *pair_sems)
    spread_direct(me, full, 1, recv_second, *pair_sems)
    drain(tokens.at[0], pair_recv.at[0])
    norm_tokens(tokens, scale, bias, order, token_unit, token_inverse, normed)
    drain(full.at[:, :, 0], wp_sem.at[1])
    project(normed, full, qkv)
    attend(qkv, prob, context)
    pool_clips(tokens, context, order, full, part)
    start_pooled(me, part, box1, in1, pool_send.at[0], pool_recv.at[0])
    pooled_along_z(me, in1, pool_recv.at[0], buf2, pool_send.at[1], pool_recv.at[1])
    start_tokens(me, upstream, ubuf, local.at[1], tok_send.at[1], tok_recv.at[1], 7, 1)
    pooled_in_plane(me, buf2, pool_recv.at[1], pool, pool_send.at[2], pool_recv.at[2])
    wait_tokens(me, upstream, ubuf, local.at[1], tok_recv.at[1])
    start_pair(me, ubuf, ups, ubox, pair_send.at[1], pair_recv.at[1])
    finish_pooled(pool, pool_recv.at[2], pooled)
    contrast(pooled, units, positives, loss_out, grad_pooled)
    save = pltpu.make_async_copy(pooled, pooled_out, store)
    save.start()
    drain(ups.at[0], pair_recv.at[1])
    grad_clip = grad_pooled[pl.ds(pl.multiple_of(me.dp * 8, 8), 8), :] * 64.0
    grad_output[...] = spread(ups, grad_clip)
    grad_half = grad_output[...].astype(BF16)
    weight_term(grad_half, scatter, context, box)
    start_weight_sum(me, box, gw_pair, gw_send.at[0], gw_recv.at[0])
    project_back(grad_half, full, order, grad_context)
    backward_attention((0, 1), qkv, prob, grad_context, grad_qkv)
    plane_weight_sum(
        me, box, gw_pair, gw_recv.at[0], gw_own, gw_buf, gw_send.at[1], gw_recv.at[1]
    )
    backward_attention((2, 3, 4, 5), qkv, prob, grad_context, grad_qkv)
    backward_tokens(token_unit, token_inverse, grad_output[...], grad_qkv, full, order, scale, grads)
    start_back_pair(me, grads, pair_buf, out_send.at[0], out_recv.at[0])
    fill_back(pair_buf, out_recv.at[0], out_box)
    out_sems = (local.at[2], out_send.at[1], out_recv.at[1])
    start_tokens(me, out_box, video_out, *out_sems, 16, 12)
    second_weight_sum(me, gw_buf, gw_recv.at[1], wide, box_z, buf_z, gw_send.at[2], gw_recv.at[2])
    start_tokens(me, out_box, video_out, *out_sems, 11, 1)
    third_weight_sum(me, buf_z, gw_recv.at[2], rows, gw_send.at[3], gw_recv.at[3])
    finish_weight_sum(me, rows, gw_recv.at[3], weight_out)
    wait_tokens(me, out_box, video_out, local.at[2], out_recv.at[1])
    save.wait()
    drain(zbuf.at[pl.ds(0, 15)], w_send.at[0])
    drain(full.at[0, pl.ds(0, 3), 0, 0], w_send.at[1])
    drain(full.at[0, pl.ds(0, 2), 0], w_send.at[2])
    drain(full.at[0, 0, 0], w_send.at[3])
    drain(full.at[0, pl.ds(0, 3), 0], w_send.at[4])
    drain(full.at[:, :, 0], wp_sem.at[0])
    for i in range(2):
        drain(vbuf.at[pl.ds(0, 31)], tok_send.at[i])
        drain(vbox, pair_send.at[i])
    drain(in1.at[pl.ds(0, 3)], pool_send.at[0])
    drain(buf2.at[pl.ds(0, 15)], pool_send.at[1])
    drain(pool.at[pl.ds(0, 31)], pool_send.at[2])
    drain(gw_pair, gw_send.at[0])
    drain(gw_buf.at[pl.ds(0, 15)], gw_send.at[1])
    drain(buf_z.at[pl.ds(0, 15)], gw_send.at[2])
    drain(rows.at[0], gw_send.at[3])
    drain(pair_buf.at[0], out_send.at[0])
    drain(out_box.at[pl.ds(0, 31)], out_send.at[1])


def shape(*dims, dtype=BF16):
    return jax.ShapeDtypeStruct(dims, dtype)


def keep(*refs):
    n = 4
    ins, outs, held, sems = refs[:n], refs[n : 2 * n], refs[2 * n : 3 * n], refs[3 * n]
    reads = [pltpu.make_async_copy(ins[i], held[i], sems.at[0, i]) for i in range(n)]
    writes = [pltpu.make_async_copy(held[i], outs[i], sems.at[1, i]) for i in range(n)]
    for copy in reads:
        copy.start()
    for read, write in zip(reads, writes):
        read.wait()
        write.start()
    for copy in writes:
        copy.wait()


def scratch_shapes():
    dma = pltpu.SemaphoreType.DMA

    def half(*dims):
        return pltpu.VMEM(dims, BF16)

    def single(*dims):
        return pltpu.VMEM(dims, F32)

    return [
        half(12, 3 * D), half(12, D), single(D), single(D), single(64, D),
        pltpu.VMEM((64,), jnp.int32), half(D, D), half(D, D),
        half(32, 8, D), half(32, 8, D), half(4, 32, D), half(4, 32, D),
        half(2, 4, 32, D), half(2, 4, 32, D), half(16, 16, 384), half(2, 4, 2, 2, 2, 2, 48, 384),
        half(256, D), half(256, 3 * D), single(12, 256, 128), half(256, D), single(8, D),
        single(4, 2, D), single(4, 2, D), single(16, 2, D), single(32, 2, D),
        single(64, D), single(64, D), single(64, D), single(256, D),
        half(256, D), half(256, 3 * D), half(2, 4, 32, D),
        half(2, 16, 48, 384), half(16, 48, 384), half(16, 48, 384), half(16, 48, 384),
        single(16, 16, 128), half(16, 16, 128), half(16, 16, 128), single(2, 16, 128),
        half(2, 4, 32, D), half(32, 8, D), single(256, D), single(256, 1),
        dma((6,)), dma((3,)), dma((2,)), dma((2,)), dma((2,)), dma((2,)),
        dma((5,)), dma((2,)), dma((2, 2)), dma((2, 2, 3)), dma((2, 2, 2)), dma((2,)),
        dma((3,)), dma((3,)), dma((4,)), dma((4,)), dma((2,)), dma((2,)), dma,
    ]


def per_device(video, upstream, standardize_scale, ln_bias, w_qkv, w_out, windows, positives):
    anywhere, vmem = pl.BlockSpec(memory_space=pl.ANY), pl.BlockSpec(memory_space=pltpu.VMEM)
    grad_video, grad_out_weight, pooled, loss = pl.pallas_call(
        kernel,
        out_shape=[
            shape(32, 8, D), shape(1, 1152, dtype=F32), shape(64, D, dtype=F32),
            shape(1, 1, dtype=F32),
        ],
        in_specs=[anywhere] * 8,
        out_specs=[anywhere, vmem, anywhere, vmem],
        scratch_shapes=scratch_shapes(),
        compiler_params=pltpu.CompilerParams(
            vmem_limit_bytes=VMEM_LIMIT, collective_id=1, has_side_effects=True
        ),
    )(
        video.reshape(32, 8, D), upstream.reshape(32, 8, D), w_qkv, w_out,
        standardize_scale, ln_bias, windows, positives,
    )
    results = (grad_video, grad_out_weight, pooled, loss)
    grad_video, grad_out_weight, pooled, loss = pl.pallas_call(
        keep,
        out_shape=[jax.ShapeDtypeStruct(a.shape, a.dtype) for a in results],
        in_specs=[anywhere] * 4,
        out_specs=[anywhere] * 4,
        scratch_shapes=[pltpu.VMEM(a.shape, a.dtype) for a in results]
        + [pltpu.SemaphoreType.DMA((2, 4))],
    )(*results)
    return grad_video.reshape(1, 1, 256, D), grad_out_weight, pooled, loss.reshape(())


def solution(mesh):
    in_specs = (
        P("dp", "seq", None, None),
        P("dp", "seq", None, None),
        P(),
        P(),
        P("seq", None),
        P("seq", None),
        P(),
        P(),
    )
    out_specs = (P("dp", "seq", None, None), P(("dp", "seq"), None), P(), P())
    return jax.shard_map(
        per_device, mesh=mesh, in_specs=in_specs, out_specs=out_specs, check_vma=False
    )
```

```python
import jax
import jax.numpy as jnp
from jax import lax
from jax.experimental import pallas as pl
from jax.experimental.pallas import tpu as pltpu
from jax.sharding import PartitionSpec as P

MESH = pl.DeviceIdType.MESH
F32 = jnp.float32
BF16 = jnp.bfloat16
D = 768
EPS = 1e-6
NEG = -1e30
SHARP = 1.0 / 0.07
VMEM_LIMIT = 56 * 1024 * 1024


class Place:
    def __init__(self):
        self.dp = lax.axis_index("dp")
        self.seq = lax.axis_index("seq")
        self.x_hi = self.dp // 4
        self.y = self.dp % 4
        self.z = self.seq // 4
        self.role = self.seq % 4
        self.x_lo = self.role // 2
        self.core = self.seq % 2
        self.k = self.seq // 2
        self.x = self.x_hi * 2 + self.x_lo
        self.m = self.dp * 4 + self.role


def send(src, dst, send_sem, recv_sem, dp, seq):
    pltpu.make_async_remote_copy(
        src_ref=src,
        dst_ref=dst,
        send_sem=send_sem,
        recv_sem=recv_sem,
        device_id=(dp, seq),
        device_id_type=MESH,
    ).start()


def wrap(a, n):
    return jnp.where(a >= n, a - n, a)


def drain(ref, sem):
    pltpu.make_async_copy(ref, ref, sem).wait()


def announce(me):
    sem = pltpu.get_barrier_semaphore()

    def slab(i, carry):
        to = wrap(me.k + i, 32) * 2 + me.core
        pl.semaphore_signal(sem, inc=1, device_id=(me.dp, to), device_id_type=MESH)
        return carry

    def plane(i, carry):
        dp = wrap(me.dp + i, 8)
        for role in range(4):
            pl.semaphore_signal(sem, inc=1, device_id=(dp, me.z * 4 + role), device_id_type=MESH)
        return carry

    lax.fori_loop(1, 32, slab, 0)
    lax.fori_loop(1, 8, plane, 0)
    for i in range(1, 4):
        to = me.z * 4 + wrap(me.role + i, 4)
        pl.semaphore_signal(sem, inc=1, device_id=(me.dp, to), device_id_type=MESH)


def arrive():
    pl.semaphore_wait(pltpu.get_barrier_semaphore(), 62)


def dot(a, b):
    return lax.dot_general(a, b, (((1,), (0,)), ((), ())), preferred_element_type=F32)


def dot_nt(a, b):
    return lax.dot_general(a, b, (((1,), (1,)), ((), ())), preferred_element_type=F32)


def dot_tn(a, b):
    return lax.dot_general(a, b, (((0,), (0,)), ((), ())), preferred_element_type=F32)


def iota(shape, dim):
    return lax.broadcasted_iota(jnp.int32, shape, dim)


def one_hot(condition):
    return jnp.where(condition, 1.0, 0.0).astype(BF16)


def gather_order(me):
    j = iota((1, D), 1)
    block, rest = j // 96, j % 96
    core, chunk, x_lo = block // 4, (block // 2) % 2, block % 2
    z8, r = rest // 12, rest % 12
    near = jnp.where(z8 < 5, z8, z8 + 8)
    from_z = (me.z + jnp.where(chunk == 0, near, z8 + 5)) % 16
    natural = (from_z * 4 + x_lo * 2 + core) * 12 + r
    return one_hot(iota((D, D), 0) == natural)


def scatter_order():
    j = iota((1, D), 1)
    dp, rest = j // 96, j % 96
    x_lo, z, r = rest // 48, (rest % 48) // 3, rest % 3
    natural = dp * 96 + z * 6 + x_lo * 3 + r
    return one_hot(iota((D, D), 0) == natural)


def split3(a):
    high = a.astype(BF16)
    rest = a - high.astype(F32)
    mid = rest.astype(BF16)
    low = (rest - mid.astype(F32)).astype(BF16)
    return jnp.concatenate([high.astype(F32), mid.astype(F32), low.astype(F32)], 0).astype(BF16)


def start_tokens(me, src, buf, local_sem, send_sem, recv_sem, far=16, near=1):
    def one(to):
        send(src.at[to], buf.at[me.k], send_sem, recv_sem, me.dp, to * 2 + me.core)

    def step(i, carry):
        one(wrap(me.k + 16 - i, 32))
        one(wrap(me.k + 16 + i, 32))
        return carry

    if far == 16:
        pltpu.make_async_copy(src.at[me.k], buf.at[me.k], local_sem).start()
        one(wrap(me.k + 16, 32))
    lax.fori_loop(max(16 - far, 1), 17 - near, step, 0)


def wait_tokens(me, src, buf, local_sem, recv_sem):
    pltpu.make_async_copy(src.at[me.k], buf.at[me.k], local_sem).wait()
    drain(buf.at[pl.ds(0, 31)], recv_sem)


def start_pair(me, buf, out, box, send_sem, recv_sem):
    rows = buf[...].astype(F32).reshape(256, D).astype(BF16)
    r, col = iota((128, 1), 0), iota((128, 256), 1)
    at = (r % 32) * 8 + r // 32
    theirs = dot(one_hot(col == at + 4 * (1 - me.core)), rows)
    box[...] = theirs.astype(BF16).reshape(4, 32, D)
    send(box, out.at[me.core], send_sem, recv_sem, me.dp, me.seq + 1 - 2 * me.core)
    mine = dot(one_hot(col == at + 4 * me.core), rows)
    out[me.core] = mine.astype(BF16).reshape(4, 32, D)


OFFSETS = (0, 1, 2, 3, 4, 13, 14, 15, 5, 6, 7, 8, 9, 10, 11, 12)


def start_weights(me, zbuf, send_sem, recv_z):
    for d in (12, 13, 3, 14, 2, 15, 1, 8, 7, 9, 6, 10, 5, 11, 4):
        j = OFFSETS.index(16 - d)
        to = wrap(me.z + d, 16) * 4 + me.role
        send(zbuf.at[0], zbuf.at[j], send_sem, recv_z.at[j // 8], me.dp, to)


def x_device(me, x):
    return (x // 2) * 4 + me.y, me.z * 4 + (x % 2) * 2 + me.core


def spread_first(me, zbuf, wide_rows, full, chunk, recv_z, send_sem, recv):
    drain(zbuf.at[pl.ds(0, 7 + chunk)], recv_z.at[chunk])
    r = iota((96, 1), 0)
    pick = one_hot(iota((96, 128), 1) == (r // 12) * 16 + r % 12)
    wide_rows[...] = jnp.zeros_like(wide_rows)
    for j in range(8):
        wide_rows[j, 0:12, :] = zbuf[chunk * 8 + j].astype(F32)
    block = dot(pick, wide_rows[...].reshape(128, 384).astype(BF16)).astype(BF16)
    full[me.x_hi, me.y, me.core, chunk, me.x_lo] = block.reshape(2, 48, 384)
    a = full.at[me.x_hi, me.y, me.core, chunk, me.x_lo, 0]
    b = full.at[me.x_hi, me.y, me.core, chunk, me.x_lo, 1]
    for i in (2, 1, 3):
        send(a, a, send_sem, recv.at[chunk, 0], *x_device(me, wrap(me.x + i, 4)))
        send(b, b, send_sem, recv.at[chunk, 1], me.x_hi * 4 + wrap(me.y + i, 4), me.seq)


def spread_second(me, full, chunk, recv_first, send_sem, recv, send_pair, recv_pair, to=(1, 3)):
    pair = me.seq + 1 - 2 * me.core
    drain(full.at[0, pl.ds(0, 3), 0, 0, 0, 0], recv_first.at[chunk, 0])
    a = full.at[:, me.y, me.core, chunk, :, 0]
    for i in to:
        send(a, a, send_sem, recv.at[chunk, 0, i - 1], me.x_hi * 4 + wrap(me.y + i, 4), me.seq)
    drain(full.at[0, pl.ds(0, 3), 0, 0, 0, 0], recv_first.at[chunk, 1])
    b = full.at[me.x_hi, :, me.core, chunk, me.x_lo, 1]
    for i in to:
        send(b, b, send_sem, recv.at[chunk, 1, i - 1], *x_device(me, wrap(me.x + i, 4)))
    send(a, a, send_pair, recv_pair, me.dp, pair)
    send(b, b, send_pair, recv_pair, me.dp, pair)


def spread_third(me, full, chunk, recv_second, send_sem, recv, send_pair, recv_pair):
    pair = me.seq + 1 - 2 * me.core
    for n, (i, o) in enumerate(((3, 1), (1, 3))):
        y, x = wrap(me.y + i, 4), wrap(me.x + i, 4)
        a = full.at[:, y, me.core, chunk, :, 0]
        drain(a, recv_second.at[chunk, 0, 2 * n])
        half = full.at[n, y, me.core, chunk, :, 0]
        send(half, half, send_sem, recv.at[chunk, 0, n], me.x_hi * 4 + wrap(me.y + o, 4), me.seq)
        b = full.at[x // 2, :, me.core, chunk, x % 2, 1]
        drain(b, recv_second.at[chunk, 1, 2 * n])
        half = full.at[x // 2, pl.ds(2 * n, 2), me.core, chunk, x % 2, 1]
        send(half, half, send_sem, recv.at[chunk, 1, n], *x_device(me, wrap(me.x + o, 4)))
        send(a, a, send_pair, recv_pair, me.dp, pair)
        send(b, b, send_pair, recv_pair, me.dp, pair)


def spread_last(me, full, chunk, recv_third, send_pair, recv_pair):
    pair = me.seq + 1 - 2 * me.core
    y, x = wrap(me.y + 2, 4), wrap(me.x + 2, 4)
    for n in range(2):
        a = full.at[n, y, me.core, chunk, :, 0]
        drain(a, recv_third.at[chunk, 0, n])
        send(a, a, send_pair, recv_pair, me.dp, pair)
        b = full.at[x // 2, pl.ds(2 * n, 2), me.core, chunk, x % 2, 1]
        drain(b, recv_third.at[chunk, 1, n])
        send(b, b, send_pair, recv_pair, me.dp, pair)


def spread_direct(me, full, chunk, recv_second, send_pair, recv_pair):
    pair = me.seq + 1 - 2 * me.core
    for i in (1, 3, 2):
        a = full.at[:, wrap(me.y + 4 - i, 4), me.core, chunk, :, 0]
        drain(a, recv_second.at[chunk, 0, i - 1])
        send(a, a, send_pair, recv_pair, me.dp, pair)
        x = wrap(me.x + 4 - i, 4)
        b = full.at[x // 2, :, me.core, chunk, x % 2, 1]
        drain(b, recv_second.at[chunk, 1, i - 1])
        send(b, b, send_pair, recv_pair, me.dp, pair)


def start_pooled(me, part, box1, in1, send_sem, recv_sem):
    for q in range(4):
        box1[q] = part[2 * q : 2 * q + 2, :]
    in1[me.role] = box1[me.role]
    for i in range(1, 4):
        to = wrap(me.role + i, 4)
        send(box1.at[to], in1.at[me.role], send_sem, recv_sem, me.dp, me.z * 4 + to)


def pooled_along_z(me, in1, recv_first, buf2, send_sem, recv_sem):
    drain(in1.at[pl.ds(0, 3)], recv_first)
    buf2[me.z] = jnp.sum(in1[...], 0)

    for i in (8, 9, 7, 10, 6, 11, 5, 12, 4, 13, 3, 14, 2, 15, 1):
        to = wrap(me.z + i, 16) * 4 + me.role
        send(buf2.at[me.z], buf2.at[me.z], send_sem, recv_sem, me.dp, to)


def pooled_in_plane(me, buf2, recv_second, pool, send_sem, recv_sem):
    drain(buf2.at[pl.ds(0, 15)], recv_second)
    pool[me.m] = jnp.sum(buf2[...], 0) * (1.0 / 2048.0)

    mine = pool.at[me.m]

    def step(i, carry):
        dp = wrap(me.dp + i, 8)
        for role in range(4):
            send(mine, mine, send_sem, recv_sem, dp, me.z * 4 + role)
        return carry

    lax.fori_loop(1, 8, step, 0)
    for i in range(1, 4):
        send(mine, mine, send_sem, recv_sem, me.dp, me.z * 4 + wrap(me.role + i, 4))


def finish_pooled(pool, recv_sem, pooled):
    drain(pool.at[pl.ds(0, 31)], recv_sem)
    for m in range(32):
        pooled[2 * m : 2 * m + 2, :] = pool[m]


def start_weight_sum(me, box, pair_buf, send_sem, recv_sem):
    send(
        box.at[1 - me.core], pair_buf, send_sem, recv_sem, me.dp, me.seq + 1 - 2 * me.core
    )


def plane_weight_sum(me, box, pair_buf, recv_pair, own, buf, send_sem, recv_sem):
    drain(pair_buf, recv_pair)
    own[...] = (box[me.core].astype(F32) + pair_buf[...].astype(F32)).astype(BF16)
    n = me.dp * 2 + me.x_lo
    buf[n] = own[n]

    def step(i, carry):
        dp = wrap(me.dp + i, 8)
        for x_lo in range(2):
            to = me.z * 4 + x_lo * 2 + me.core
            send(own.at[dp * 2 + x_lo], buf.at[n], send_sem, recv_sem, dp, to)
        return carry

    lax.fori_loop(1, 8, step, 0)
    other = 1 - me.x_lo
    to = me.z * 4 + other * 2 + me.core
    send(own.at[me.dp * 2 + other], buf.at[n], send_sem, recv_sem, me.dp, to)


def second_weight_sum(me, buf, recv_sem, wide, box_z, buf_z, send_sem, recv_z):
    drain(buf.at[pl.ds(0, 15)], recv_sem)
    total = lax.fori_loop(
        0, 16, lambda i, t: t + buf[i].astype(F32), jnp.zeros((48, 384), F32)
    )
    wide[...] = jnp.zeros_like(wide)
    for z in range(16):
        for r in range(3):
            row = total[3 * z + r : 3 * z + r + 1, :]
            for n in range(3):
                wide[z, r * 3 + n : r * 3 + n + 1, :] = row[:, n * 128 : n * 128 + 128]
    box_z[...] = wide[...].astype(BF16)
    buf_z[me.z] = box_z[me.z]
    for i in (8, 9, 7, 10, 6, 11, 5, 12, 4, 13, 3, 14, 2, 15, 1):
        to = wrap(me.z + i, 16)
        send(box_z.at[to], buf_z.at[me.z], send_sem, recv_z, me.dp, to * 4 + me.role)


def third_weight_sum(me, buf_z, recv_z, rows, send_sem, recv_sem):
    drain(buf_z.at[pl.ds(0, 15)], recv_z)
    rows[me.core] = jnp.sum(buf_z[...].astype(F32), 0)
    send(
        rows.at[me.core], rows.at[me.core], send_sem, recv_sem,
        me.dp, me.seq + 1 - 2 * me.core,
    )


def finish_weight_sum(me, rows, recv_sem, out):
    drain(rows.at[0], recv_sem)
    halves = (rows[0], rows[1])
    first = me.core == 0

    def part(source, row, n):
        at = row * 3 + n
        return halves[source][at : at + 1]

    for n in range(3):
        at = n * 128
        out[0:1, at : at + 128] = jnp.where(first, part(0, 0, n), part(1, 1, n))
        out[0:1, 384 + at : 512 + at] = jnp.where(first, part(1, 0, n), part(0, 2, n))
        out[0:1, 768 + at : 896 + at] = jnp.where(first, part(0, 1, n), part(1, 2, n))


def start_back_pair(me, grads, buf, send_sem, recv_sem):
    theirs = 1 - me.core
    send(grads.at[theirs], buf.at[me.core], send_sem, recv_sem, me.dp, me.seq + 1 - 2 * me.core)
    buf[me.core] = grads[me.core]


def fill_back(buf, recv_pair, box):
    drain(buf.at[0], recv_pair)
    r = iota((256, 1), 0)
    at = ((r // 4) % 2) * 128 + (r % 4) * 32 + r // 8
    rows = dot(one_hot(iota((256, 256), 1) == at), buf[...].reshape(256, D))
    box[...] = rows.reshape(32, 8, D).astype(BF16)


def normalize(x):
    centered = x - jnp.mean(x, -1, keepdims=True)
    inverse = lax.rsqrt(jnp.mean(centered * centered, -1, keepdims=True) + EPS)
    return centered * inverse, inverse


def exact(a, b, contract):
    return lax.dot_general(
        a, b, (contract, ((), ())), precision=lax.Precision.HIGHEST, preferred_element_type=F32
    )


def window_units(windows, out):
    w = windows[...]
    out[...] = w * lax.rsqrt(jnp.mean(w * w, -1, keepdims=True) + EPS) * D ** (-0.5)


def contrast(pooled, units, positives, loss, grad):
    p, root = pooled[...], D ** (-0.5)
    inverse = lax.rsqrt(jnp.mean(p * p, -1, keepdims=True) + EPS)
    logits = exact(units[...], p * inverse * root, ((1,), (1,))) * SHARP
    matched = iota((64, 64), 0) == positives[...].reshape(1, 64)
    total = -jnp.sum(jnp.where(matched, logits, 0.0))
    slope = jnp.where(matched, -1.0, 0.0)
    for axis in range(2):
        top = jnp.max(logits, axis, keepdims=True)
        weight = jnp.exp(logits - top)
        size = jnp.sum(weight, axis, keepdims=True)
        total = total + 0.5 * jnp.sum(top + jnp.log(size))
        slope = slope + 0.5 * (weight / size)
    loss[...] = jnp.full((1, 1), total * (1.0 / 64.0), F32)
    grad_unit = exact(slope * (SHARP / 64.0), units[...], ((0,), (0,)))
    inner = jnp.mean(grad_unit * p, -1, keepdims=True)
    grad[...] = inverse * root * (grad_unit - p * (inverse * inverse) * inner)


def clip_pick():
    return one_hot((iota((8, 256), 1) % 32) // 4 == iota((8, 256), 0))


def unit_rows(ref, u, columns):
    return jnp.concatenate(
        [ref[u * 64 : u * 64 + 64, columns], ref[128 + u * 64 : 192 + u * 64, columns]], 0
    )


def put_rows(ref, u, columns, value):
    ref[u * 64 : u * 64 + 64, columns] = value[:64]
    ref[128 + u * 64 : 192 + u * 64, columns] = value[64:]


def heads(a):
    even = iota(a.shape, 1) < 64
    zero = jnp.zeros_like(a)
    return jnp.concatenate([jnp.where(even, a, zero), jnp.where(even, zero, a)], 0)


def same_patch():
    return (iota((256, 128), 0) // 32) % 2 == (iota((256, 128), 1) // 32) % 2


def norm_tokens(tokens, scale, bias, order, units, inverses, normed):
    unit, inverse = normalize(tokens[...].reshape(256, D).astype(F32))
    units[...] = unit
    inverses[...] = inverse
    rows = (unit * scale[...].reshape(1, D) + bias[...].reshape(1, D)).astype(BF16)
    normed[...] = dot(rows, order[...]).astype(BF16)


def project(normed, full, qkv):
    for n in range(6):
        weight = full[n // 4, n % 4].reshape(D, 384)
        qkv[:, n * 384 : n * 384 + 384] = dot(normed[...], weight).astype(BF16)


def attend(qkv, prob, context):
    keep = same_patch()
    for j in range(6):
        for u in range(2):
            columns = [slice(s * D + j * 128, s * D + j * 128 + 128) for s in range(3)]
            query, key, value = [unit_rows(qkv, u, c) for c in columns]
            score = dot_nt(heads(query), key) * 0.125
            score = jnp.where(keep, score, NEG)
            top = jnp.max(score, -1, keepdims=True)
            weight = jnp.exp(score - top)
            p = weight / jnp.sum(weight, -1, keepdims=True)
            prob[j * 2 + u] = p
            half = p.astype(BF16)
            both = jnp.concatenate([half[:128], half[128:]], 1)
            mixed = dot(both, heads(value)).astype(BF16)
            put_rows(context, u, slice(j * 128, j * 128 + 128), mixed)


def pool_clips(tokens, context, order, full, part):
    pick = clip_pick()
    ctx_sum = split3(dot(pick, context[...]))
    ctx_sum = dot(ctx_sum, order[...]).astype(BF16)
    sums = dot(pick, tokens[...].reshape(256, D))
    for n in range(2):
        weight = full[1, 2 + n].reshape(D, 384)
        s = dot(ctx_sum, weight)
        columns = slice(n * 384, n * 384 + 384)
        part[:, columns] = sums[:, columns] + s[0:8] + s[8:16] + s[16:24]


def spread(upstream, grad_clip):
    pick = one_hot((iota((256, 24), 0) % 32) // 4 == iota((256, 24), 1) % 8)
    return upstream[...].reshape(256, D).astype(F32) + dot(pick, split3(grad_clip))


def project_back(grad_half, full, order, grad_context):
    back = dot_nt(grad_half[:, :384], full[1, 2].reshape(D, 384))
    back = back + dot_nt(grad_half[:, 384:], full[1, 3].reshape(D, 384))
    grad_context[...] = dot_nt(back.astype(BF16), order[...]).astype(BF16)


def weight_term(grad_half, scatter, context, box):
    ordered = dot(context[...], scatter[...]).astype(BF16)
    term = dot_tn(ordered, grad_half).astype(BF16)
    for n in range(16):
        for c in range(2):
            box[c, n] = term[n * 48 : n * 48 + 48, c * 384 : c * 384 + 384]


def backward_attention(pairs, qkv, prob, grad_context, grad_qkv):
    for j in pairs:
        for u in range(2):
            columns = [slice(s * D + j * 128, s * D + j * 128 + 128) for s in range(3)]
            query, key, value = [unit_rows(qkv, u, c) for c in columns]
            grad = heads(unit_rows(grad_context, u, slice(j * 128, j * 128 + 128)))
            p = prob[j * 2 + u]
            half = p.astype(BF16)
            grad_prob = dot_nt(grad, value)
            grad_value = dot_tn(half, grad).astype(BF16)
            row = jnp.sum(p * grad_prob, -1, keepdims=True)
            grad_score = (p * (grad_prob - row) * 0.125).astype(BF16)
            both = jnp.concatenate([grad_score[:128], grad_score[128:]], 1)
            put_rows(grad_qkv, u, columns[0], dot(both, heads(key)).astype(BF16))
            put_rows(grad_qkv, u, columns[1], dot_tn(grad_score, heads(query)).astype(BF16))
            put_rows(grad_qkv, u, columns[2], grad_value)


def backward_tokens(units, inverses, grad_output, grad_qkv, full, order, scale, out):
    back = jnp.zeros((256, D), F32)
    for n in range(6):
        weight = full[n // 4, n % 4].reshape(D, 384)
        back = back + dot_nt(grad_qkv[:, n * 384 : n * 384 + 384], weight)
    grad_normed = dot_nt(back.astype(BF16), order[...])
    scaled = grad_normed * scale[...].reshape(1, D)
    unit, inverse = units[...], inverses[...]
    grad_norm = inverse * (
        scaled
        - jnp.mean(scaled, -1, keepdims=True)
        - unit * jnp.mean(scaled * unit, -1, keepdims=True)
    )
    out[...] = (grad_output + grad_norm).astype(BF16).reshape(2, 4, 32, D)


def kernel(
    video, upstream, w_qkv, w_out, scale_in, bias_in, windows_in, positives_in,
    video_out, weight_out, pooled_out, loss_out,
    wq, wo, scale, bias, windows, positives, order, scatter,
    vbuf, ubuf, vbox, ubox, tokens, ups, zbuf, full, normed, qkv, prob, context, part,
    box1, in1, buf2, pool, pooled, units, grad_pooled, grad_output, grad_context, grad_qkv, grads,
    box, gw_pair, gw_own, gw_buf, wide, box_z, buf_z, rows, pair_buf, out_box,
    token_unit, token_inverse, wide_rows,
    load, local, tok_send, tok_recv, pair_send, pair_recv,
    w_send, recv_z, recv_first, recv_second, recv_third, wp_sem,
    pool_send, pool_recv, gw_send, gw_recv, out_send, out_recv, store,
):
    me = Place()
    loads = [(w_qkv, wq), (w_out, wo), (scale_in, scale), (bias_in, bias)]
    loads += [(windows_in, windows), (positives_in, positives)]
    loads = [pltpu.make_async_copy(a, b, load.at[i]) for i, (a, b) in enumerate(loads)]
    for copy in loads:
        copy.start()
    announce(me)
    loads[0].wait()
    loads[1].wait()
    column = pl.multiple_of(lax.rem(me.dp, 6) * 384, 384)
    column_out = pl.multiple_of(lax.rem(me.dp, 2) * 384, 384)
    piece = jnp.where(me.dp < 6, wq[:, pl.ds(column, 384)], wo[:, pl.ds(column_out, 384)])
    zbuf[0] = piece
    arrive()
    start_weights(me, zbuf, w_send.at[0], recv_z)
    start_tokens(me, video, vbuf, local.at[0], tok_send.at[0], tok_recv.at[0])
    order[...] = gather_order(me)
    scatter[...] = scatter_order()
    for copy in loads[2:]:
        copy.wait()
    window_units(windows, units)
    pair_sems = (wp_sem.at[0], wp_sem.at[1])
    second = (recv_second, *pair_sems)
    third = (w_send.at[3], recv_third, *pair_sems)
    spread_first(me, zbuf, wide_rows, full, 0, recv_z, w_send.at[1], recv_first)
    start_tokens(me, upstream, ubuf, local.at[1], tok_send.at[1], tok_recv.at[1], 16, 8)
    spread_second(me, full, 0, recv_first, w_send.at[2], *second)
    spread_first(me, zbuf, wide_rows, full, 1, recv_z, w_send.at[1], recv_first)
    spread_third(me, full, 0, recv_second, *third)
    spread_second(me, full, 1, recv_first, w_send.at[4], *second, to=(2, 1, 3))
    wait_tokens(me, video, vbuf, local.at[0], tok_recv.at[0])
    start_pair(me, vbuf, tokens, vbox, pair_send.at[0], pair_recv.at[0])
    spread_last(me, full, 0, recv_third, *pair_sems)
    spread_direct(me, full, 1, recv_second, *pair_sems)
    drain(tokens.at[0], pair_recv.at[0])
    norm_tokens(tokens, scale, bias, order, token_unit, token_inverse, normed)
    drain(full.at[:, :, 0], wp_sem.at[1])
    project(normed, full, qkv)
    attend(qkv, prob, context)
    pool_clips(tokens, context, order, full, part)
    start_pooled(me, part, box1, in1, pool_send.at[0], pool_recv.at[0])
    pooled_along_z(me, in1, pool_recv.at[0], buf2, pool_send.at[1], pool_recv.at[1])
    start_tokens(me, upstream, ubuf, local.at[1], tok_send.at[1], tok_recv.at[1], 7, 1)
    pooled_in_plane(me, buf2, pool_recv.at[1], pool, pool_send.at[2], pool_recv.at[2])
    wait_tokens(me, upstream, ubuf, local.at[1], tok_recv.at[1])
    start_pair(me, ubuf, ups, ubox, pair_send.at[1], pair_recv.at[1])
    finish_pooled(pool, pool_recv.at[2], pooled)
    contrast(pooled, units, positives, loss_out, grad_pooled)
    save = pltpu.make_async_copy(pooled, pooled_out, store)
    save.start()
    drain(ups.at[0], pair_recv.at[1])
    grad_clip = grad_pooled[pl.ds(pl.multiple_of(me.dp * 8, 8), 8), :] * 64.0
    grad_output[...] = spread(ups, grad_clip)
    grad_half = grad_output[...].astype(BF16)
    weight_term(grad_half, scatter, context, box)
    start_weight_sum(me, box, gw_pair, gw_send.at[0], gw_recv.at[0])
    project_back(grad_half, full, order, grad_context)
    backward_attention((0, 1), qkv, prob, grad_context, grad_qkv)
    plane_weight_sum(
        me, box, gw_pair, gw_recv.at[0], gw_own, gw_buf, gw_send.at[1], gw_recv.at[1]
    )
    backward_attention((2, 3, 4, 5), qkv, prob, grad_context, grad_qkv)
    backward_tokens(token_unit, token_inverse, grad_output[...], grad_qkv, full, order, scale, grads)
    start_back_pair(me, grads, pair_buf, out_send.at[0], out_recv.at[0])
    fill_back(pair_buf, out_recv.at[0], out_box)
    out_sems = (local.at[2], out_send.at[1], out_recv.at[1])
    start_tokens(me, out_box, video_out, *out_sems, 16, 12)
    second_weight_sum(me, gw_buf, gw_recv.at[1], wide, box_z, buf_z, gw_send.at[2], gw_recv.at[2])
    start_tokens(me, out_box, video_out, *out_sems, 11, 1)
    third_weight_sum(me, buf_z, gw_recv.at[2], rows, gw_send.at[3], gw_recv.at[3])
    finish_weight_sum(me, rows, gw_recv.at[3], weight_out)
    wait_tokens(me, out_box, video_out, local.at[2], out_recv.at[1])
    save.wait()
    drain(zbuf.at[pl.ds(0, 15)], w_send.at[0])
    drain(full.at[0, pl.ds(0, 3), 0, 0], w_send.at[1])
    drain(full.at[0, pl.ds(0, 2), 0], w_send.at[2])
    drain(full.at[0, 0, 0], w_send.at[3])
    drain(full.at[0, pl.ds(0, 3), 0], w_send.at[4])
    drain(full.at[:, :, 0], wp_sem.at[0])
    for i in range(2):
        drain(vbuf.at[pl.ds(0, 31)], tok_send.at[i])
        drain(vbox, pair_send.at[i])
    drain(in1.at[pl.ds(0, 3)], pool_send.at[0])
    drain(buf2.at[pl.ds(0, 15)], pool_send.at[1])
    drain(pool.at[pl.ds(0, 31)], pool_send.at[2])
    drain(gw_pair, gw_send.at[0])
    drain(gw_buf.at[pl.ds(0, 15)], gw_send.at[1])
    drain(buf_z.at[pl.ds(0, 15)], gw_send.at[2])
    drain(rows.at[0], gw_send.at[3])
    drain(pair_buf.at[0], out_send.at[0])
    drain(out_box.at[pl.ds(0, 31)], out_send.at[1])


def shape(*dims, dtype=BF16):
    return jax.ShapeDtypeStruct(dims, dtype)


def keep(*refs):
    n = 4
    ins, outs, held, sems = refs[:n], refs[n : 2 * n], refs[2 * n : 3 * n], refs[3 * n]
    reads = [pltpu.make_async_copy(ins[i], held[i], sems.at[0, i]) for i in range(n)]
    writes = [pltpu.make_async_copy(held[i], outs[i], sems.at[1, i]) for i in range(n)]
    for copy in reads:
        copy.start()
    for read, write in zip(reads, writes):
        read.wait()
        write.start()
    for copy in writes:
        copy.wait()


def scratch_shapes():
    dma = pltpu.SemaphoreType.DMA

    def half(*dims):
        return pltpu.VMEM(dims, BF16)

    def single(*dims):
        return pltpu.VMEM(dims, F32)

    return [
        half(12, 3 * D), half(12, D), single(D), single(D), single(64, D),
        pltpu.VMEM((64,), jnp.int32), half(D, D), half(D, D),
        half(32, 8, D), half(32, 8, D), half(4, 32, D), half(4, 32, D),
        half(2, 4, 32, D), half(2, 4, 32, D), half(16, 12, 384), half(2, 4, 2, 2, 2, 2, 48, 384),
        half(256, D), half(256, 3 * D), single(12, 256, 128), half(256, D), single(8, D),
        single(4, 2, D), single(4, 2, D), single(16, 2, D), single(32, 2, D),
        single(64, D), single(64, D), single(64, D), single(256, D),
        half(256, D), half(256, 3 * D), half(2, 4, 32, D),
        half(2, 16, 48, 384), half(16, 48, 384), half(16, 48, 384), half(16, 48, 384),
        single(16, 16, 128), half(16, 16, 128), half(16, 16, 128), single(2, 16, 128),
        half(2, 4, 32, D), half(32, 8, D), single(256, D), single(256, 1), single(8, 16, 384),
        dma((6,)), dma((3,)), dma((2,)), dma((2,)), dma((2,)), dma((2,)),
        dma((5,)), dma((2,)), dma((2, 2)), dma((2, 2, 3)), dma((2, 2, 2)), dma((2,)),
        dma((3,)), dma((3,)), dma((4,)), dma((4,)), dma((2,)), dma((2,)), dma,
    ]


def per_device(video, upstream, standardize_scale, ln_bias, w_qkv, w_out, windows, positives):
    anywhere, vmem = pl.BlockSpec(memory_space=pl.ANY), pl.BlockSpec(memory_space=pltpu.VMEM)
    grad_video, grad_out_weight, pooled, loss = pl.pallas_call(
        kernel,
        out_shape=[
            shape(32, 8, D), shape(1, 1152, dtype=F32), shape(64, D, dtype=F32),
            shape(1, 1, dtype=F32),
        ],
        in_specs=[anywhere] * 8,
        out_specs=[anywhere, vmem, anywhere, vmem],
        scratch_shapes=scratch_shapes(),
        compiler_params=pltpu.CompilerParams(
            vmem_limit_bytes=VMEM_LIMIT, collective_id=1, has_side_effects=True
        ),
    )(
        video.reshape(32, 8, D), upstream.reshape(32, 8, D), w_qkv, w_out,
        standardize_scale, ln_bias, windows, positives,
    )
    results = (grad_video, grad_out_weight, pooled, loss)
    grad_video, grad_out_weight, pooled, loss = pl.pallas_call(
        keep,
        out_shape=[jax.ShapeDtypeStruct(a.shape, a.dtype) for a in results],
        in_specs=[anywhere] * 4,
        out_specs=[anywhere] * 4,
        scratch_shapes=[pltpu.VMEM(a.shape, a.dtype) for a in results]
        + [pltpu.SemaphoreType.DMA((2, 4))],
    )(*results)
    return grad_video.reshape(1, 1, 256, D), grad_out_weight, pooled, loss.reshape(())


def solution(mesh):
    in_specs = (
        P("dp", "seq", None, None),
        P("dp", "seq", None, None),
        P(),
        P(),
        P("seq", None),
        P("seq", None),
        P(),
        P(),
    )
    out_specs = (P("dp", "seq", None, None), P(("dp", "seq"), None), P(), P())
    return jax.shard_map(
        per_device, mesh=mesh, in_specs=in_specs, out_specs=out_specs, check_vma=False
    )
```
